128 devices in a mesh: space: 8 (over y, core), mode: 16 (over x, z).
Axes of the slice: x: 4, y: 4, z: 4, core: 2. Of those that a mesh axis runs over, the one named last changes fastest.
Arguments:
- intensity: float32 [1024, 8, 128, 256], P('mode', None, 'space'), may hold values from 0.1 to 2
- dir_cos: float32 [3, 32], replicated, may hold values from -1 to 1, as said below
- velocity: float32 [32], replicated, may hold values from 0.2 to 1
- rate: float32 [32], replicated, may hold values from 0.05 to 2
- spectrum: float32 [32], replicated, may hold values from 0.2 to 2
- weight: float32 [32], replicated, may hold values from 0.25 to 1.75
- heat: float32 [128, 256], P('space'), may hold values from 0.5 to 4
- rough_cells: int32 [8192], P('space'), may hold values from 0 to 4095, as said below
- rough_count: int32 [8], P('space'), may hold values from 256 to 1024, as said below
- rough_map: int32 [8192, 16], P('space'), may hold values from 0 to 15
Outputs:
- intensity_new: float32 [1024, 8, 128, 256], P('mode', None, 'space')
- energy_new: float32 [8, 128, 256], P(None, 'space')
The draws below stay inside these ranges and needn't reach their ends.
Inputs may be any that keep to these rules, and one draw needn't show every extreme that they name: `dir_cos`: even directions have a positive third cosine, and direction 2k+1 equals direction 2k with the third cosine negated; every direction has a third cosine of magnitude 0.3 or more. `rough_cells`: the entries of one index of space are distinct. `rough_count`: some index of space has all 1024 slots live.
All inputs are finite; a program needn't handle non-finite values.
Results may differ from the reference program's by a relative error of at most 0.0015.
Values sent between devices are 32-bit elements; how exact they have to be, the bound alone decides.
No kernel may reach another device: no remote copies, remote signals or barrier semaphores. Data moves between devices by JAX's collectives and lax.ppermute only.
A program may use at most 128 MiB of HBM per device.

```python
import math
import jax
import jax.numpy as jnp

DIRS = 32
MODES = 32
Z = 8
XR = 16
NY = 256
PAIRS = 1024
NX = 128
ROUGH = 1024
N_SPACE = 8


def draw_dir_cos(key, part):
    keys = jax.random.split(jax.random.fold_in(key, 11), 3)
    half = DIRS // 2
    ux = jax.random.normal(keys[0], (half,), jnp.float32)
    uy = jax.random.normal(keys[1], (half,), jnp.float32)
    uz = jax.random.uniform(keys[2], (half,), jnp.float32, 0.6, 1.6)
    length = jnp.sqrt(ux * ux + uy * uy + uz * uz)
    ux = ux / length
    uy = uy / length
    uz = jnp.maximum(uz / length, 0.3)
    cx = jnp.stack([ux, ux], axis=1).reshape(DIRS)
    cy = jnp.stack([uy, uy], axis=1).reshape(DIRS)
    cz = jnp.stack([uz, -uz], axis=1).reshape(DIRS)
    return jnp.stack([cx, cy, cz], axis=0).astype(jnp.float32)


def draw_rough_cells(key, part):
    keys = jax.random.split(jax.random.fold_in(key, 23), N_SPACE)
    lists = jax.vmap(lambda k: jax.random.permutation(k, XR * NY)[:ROUGH])(keys)
    return lists.reshape(-1).astype(jnp.int32)


def draw_rough_count(key, part):
    keys = jax.random.split(jax.random.fold_in(key, 37), 2)
    counts = jax.random.randint(keys[0], (N_SPACE,), ROUGH // 4, ROUGH + 1)
    fullest = jax.random.randint(keys[1], (), 0, N_SPACE)
    return counts.at[fullest].set(ROUGH).astype(jnp.int32)


def touch_ends(array, rng, smallest, top_value):
    spot = [jax.random.randint(jax.random.fold_in(rng, axis), (), 0, length) for axis, length in enumerate(array.shape)]
    main_axis = array.shape.index(max(array.shape))
    neighbour = spot[:main_axis] + [(spot[main_axis] + 1) % array.shape[main_axis]] + spot[main_axis + 1:]
    return array.at[tuple(spot)].set(smallest).at[tuple(neighbour)].set(top_value)


def block_levels(key, shape, cuts, least, largest):
    def one(position, parts):
        draws = jax.random.uniform(jax.random.fold_in(jax.random.fold_in(key, 6), position), (parts,), jnp.float32, least / len(cuts), largest / len(cuts))
        return jnp.repeat(jnp.exp(draws), shape[position] // parts).reshape((-1,) + (1,) * (len(shape) - position - 1))

    loudness = one(*cuts[0])
    for cut in cuts[1:]:
        loudness = loudness * one(*cut)
    return loudness


def setup_inputs(seed: int = 0) -> dict:
    seeds = jax.random.split(jax.random.key(seed), 11)
    return {
        "intensity": jnp.clip(jnp.exp(math.log(2.0) - 2.9957323 * jax.random.uniform(seeds[0], (PAIRS, Z, NX, NY), jnp.float32) ** block_levels(seeds[0], (PAIRS, Z, NX, NY), ((0, 16), (2, 8)), -0.2, 0.2)), 0.1, 2.0),
        "dir_cos": draw_dir_cos(jax.random.fold_in(seeds[10], 71), 0),
        "velocity": jnp.clip(jnp.exp(jax.random.uniform(seeds[2], (MODES,), jnp.float32, math.log(0.2), math.log(1.0))), 0.2, 1.0),
        "rate": jnp.clip(jnp.exp(jax.random.uniform(seeds[3], (MODES,), jnp.float32, math.log(0.05), math.log(2.0))), 0.05, 2.0),
        "spectrum": jnp.clip(jnp.exp(jax.random.uniform(seeds[4], (MODES,), jnp.float32, math.log(0.2), math.log(2.0))), 0.2, 2.0),
        "weight": jnp.clip(1.0 + 0.15 * jax.random.normal(seeds[5], (DIRS,), jnp.float32), 0.25, 1.75),
        "heat": jnp.clip(jnp.exp(math.log(4.0) - 2.0794415 * jax.random.uniform(seeds[6], (NX, NY), jnp.float32) ** block_levels(seeds[6], (NX, NY), ((0, 8),), -0.2, 0.2)), 0.5, 4.0),
        "rough_cells": draw_rough_cells(jax.random.fold_in(seeds[10], 71), 0),
        "rough_count": draw_rough_count(jax.random.fold_in(seeds[10], 71), 0),
        "rough_map": touch_ends(jax.random.randint(seeds[9], (N_SPACE * ROUGH, DIRS // 2), 0, DIRS // 2), jax.random.fold_in(seeds[9], 1), 0, (DIRS // 2) - 1).astype(jnp.int32),
    }


def drift_of(field, dir_cos, velocity):
    ox = dir_cos[0][:, None, None, None, None]
    oy = dir_cos[1][:, None, None, None, None]
    speed = velocity[None, :, None, None, None]
    padx = jnp.pad(field, ((0, 0), (0, 0), (0, 0), (1, 1), (0, 0)))
    pady = jnp.pad(field, ((0, 0), (0, 0), (0, 0), (0, 0), (1, 1)))
    along = jnp.maximum(ox, 0.0) * (field - padx[:, :, :, :-2]) + jnp.minimum(ox, 0.0) * (padx[:, :, :, 2:] - field)
    across = jnp.maximum(oy, 0.0) * (field - pady[..., :-2]) + jnp.minimum(oy, 0.0) * (pady[..., 2:] - field)
    return speed * (along + across)


def reference(intensity, dir_cos, velocity, rate, spectrum, weight, heat, rough_cells, rough_count, rough_map):
    field = intensity.reshape(DIRS, MODES, Z, NX, NY)
    energy = jnp.einsum('s,smzxy->zxy', weight, field) / PAIRS
    equil = energy / (1.0 + 0.3 * jnp.abs(energy))
    source = (rate * spectrum)[:, None, None, None] * equil[None]
    rhs = field + source[None] - drift_of(field, dir_cos, velocity)
    diag = 1.0 + rate
    couple = velocity[None, :] * jnp.abs(dir_cos[2])[:, None]
    up_rhs = rhs[0::2]
    down_rhs = rhs[1::2]
    cdown = couple[1::2][:, :, None, None]
    adown = diag[None, :, None, None] + cdown
    carry = spectrum[None, :, None, None] * heat[None, None]
    planes = [None] * Z
    for level in reversed(range(Z)):
        carry = (down_rhs[:, :, level] + cdown * carry) / adown
        planes[level] = carry
    down_new = jnp.stack(planes, axis=2)
    bottom = down_new[:, :, 0].reshape(DIRS // 2, MODES, NX * NY)
    offsets = jnp.arange(N_SPACE, dtype=jnp.int32) * (XR * NY)
    cells = (rough_cells.reshape(N_SPACE, ROUGH) + offsets[:, None]).reshape(-1).astype(jnp.int32)
    live = (jnp.arange(ROUGH, dtype=jnp.int32)[None, :] < rough_count[:, None]).reshape(-1)
    values = bottom[:, :, cells].transpose(2, 0, 1)
    picked = jnp.take_along_axis(values, rough_map[:, :, None], axis=1).transpose(1, 2, 0)
    current = bottom[:, :, cells]
    inflow = 0.9 * bottom.at[:, :, cells].set(jnp.where(live[None, None, :], picked, current))
    inflow = inflow.reshape(DIRS // 2, MODES, NX, NY)
    cup = couple[0::2][:, :, None, None]
    aup = diag[None, :, None, None] + cup
    carry = inflow
    planes = []
    for level in range(Z):
        carry = (up_rhs[:, :, level] + cup * carry) / aup
        planes.append(carry)
    up_new = jnp.stack(planes, axis=2)
    fresh = jnp.stack([up_new, down_new], axis=1).reshape(DIRS, MODES, Z, NX, NY)
    energy_new = jnp.einsum('s,smzxy->zxy', weight, fresh) / PAIRS
    return fresh.reshape(PAIRS, Z, NX, NY), energy_new
```

```python
import jax
import jax.numpy as jnp
from jax import lax
from jax.experimental import pallas as pl
from jax.experimental.pallas import tpu as pltpu
from jax.sharding import PartitionSpec as P

PAIRS = 1024
DIRS = 32
MODES = 32
Z = 8
ROWS = 16
COLS = 256
GROUP = 16
PLANE = Z * ROWS
PACK = 48
F32 = jnp.float32


def column(row):
    r = lax.broadcasted_iota(jnp.int32, (MODES, MODES), 0)
    c = lax.broadcasted_iota(jnp.int32, (MODES, MODES), 1)
    return jnp.sum(jnp.where(r == c, jnp.broadcast_to(row, (MODES, MODES)), 0.0), axis=1, keepdims=True)


def edge_kernel(
    pos, dcs, wts, cnt, left, right, dcv, vel, rate, spec, wv, cells, rmap,
    e_ref, edge_ref, small_ref, jm_ref, k0_ref, kap, bet, acc,
):
    g = pl.program_id(0)
    k = pos[0]
    cx = dcs[0, 2 * k]
    cz = jnp.abs(dcs[2, 2 * k])
    row = jnp.where(cx > 0.0, ROWS - 1, 0)

    @pl.when(g == 0)
    def _():
        v, a = column(vel[...]), 1.0 + column(rate[...])
        inv = 1.0 / (a + v * cz)
        kap[...] = jnp.broadcast_to(v * cz * inv, (MODES, COLS))
        bet[...] = jnp.broadcast_to(v * jnp.abs(cx) * inv, (MODES, COLS))
        acc[...] = jnp.zeros_like(acc)
        e_ref[...] = jnp.zeros_like(e_ref)
        slot = lax.broadcasted_iota(jnp.int32, (1, cells.shape[1]), 1)
        local = jnp.where(slot < cnt[0], cells[...] - k * COLS, -1)
        q = lax.broadcasted_iota(jnp.int32, (COLS, cells.shape[1]), 0)
        hot = jnp.where(q == local, 1.0, 0.0).astype(jnp.bfloat16)
        idx = (rmap[...] + 1).astype(F32).astype(jnp.bfloat16)
        jm_ref[...] = lax.dot_general(idx, hot, (((1,), (1,)), ((), ())), preferred_element_type=F32)
        czr = jnp.abs(dcv[2:3, :])
        c_all = v * czr
        inv_all = 1.0 / (a + c_all)
        k_all = c_all * inv_all
        term = column(rate[...]) * column(spec[...]) * inv_all * wv[...]
        odd = lax.broadcasted_iota(jnp.int32, (MODES, DIRS), 1) % 2 == 1
        zr = lax.broadcasted_iota(jnp.int32, (Z, 128), 0)
        zc = lax.broadcasted_iota(jnp.int32, (Z, 128), 1)
        total = jnp.zeros((Z, 128), F32)
        for n in range(Z):
            down = jnp.sum(jnp.sum(jnp.where(odd, term, 0.0), axis=1, keepdims=True), axis=0, keepdims=True)
            up = jnp.sum(jnp.sum(jnp.where(odd, 0.0, term), axis=1, keepdims=True), axis=0, keepdims=True)
            total += jnp.where(zc - zr == n, down, 0.0) + jnp.where(zr - zc == n, up, 0.0)
            term = term * k_all
        k0_ref[...] = total

    w = wts[2 * k + g // 4]
    for h, x_ref in enumerate((left, right)):
        for t in range(PLANE // 8):
            part = x_ref[pl.ds(t * 8, 8), :]
            for p in range(1, 8):
                part += x_ref[pl.ds(p * PLANE + t * 8, 8), :]
            e_ref[h, pl.ds(t * 8, 8), :] += w * part
    m0 = pl.multiple_of(8 * (g % 4), 8)
    kp = kap[pl.ds(m0, 8), :]
    bt = bet[pl.ds(m0, 8), :]
    rows = []
    for z in range(Z):
        halves = [x_ref[pl.ds(z * ROWS + row, 8, stride=PLANE), :] for x_ref in (left, right)]
        for h in range(2):
            edge_ref[h, pl.ds(pl.multiple_of(z * 64 + 8 * g, 8), 8), :] = halves[h]
        rows.append(bt * jnp.concatenate(halves, axis=1))

    @pl.when(g < 4)
    def _():
        t = rows[0]
        acc[pl.ds(0, 8), :] += w * t
        for z in range(1, Z):
            t = kp * t + rows[z]
            acc[pl.ds(8 * z, 8), :] += w * t

    @pl.when(g >= 4)
    def _():
        t = rows[Z - 1]
        acc[pl.ds(8 * (Z - 1), 8), :] += w * t
        for z in reversed(range(Z - 1)):
            t = kp * t + rows[z]
            acc[pl.ds(8 * z, 8), :] += w * t
        small_ref[pl.ds(8 + m0, 8), :] = t

    @pl.when(g == 7)
    def _():
        for z in range(Z):
            small_ref[pl.ds(z, 1), :] = jnp.sum(acc[pl.ds(8 * z, 8), :], axis=0, keepdims=True)


def places(dcs, k):
    up_x, up_y = dcs[0, 2 * k] > 0.0, dcs[1, 2 * k] > 0.0
    first_row = jnp.where(up_x, 0, 8)
    first_col = jnp.where(up_y, 0, 128)
    rows = [pl.multiple_of(first_row, 8), pl.multiple_of(8 - first_row, 8)]
    cols = [pl.multiple_of(first_col, 128), pl.multiple_of(128 - first_col, 128)]
    sub = lax.broadcasted_iota(jnp.int32, (8, 128), 0) == jnp.where(up_x, 0, 7)
    lane = lax.broadcasted_iota(jnp.int32, (8, 128), 1) == jnp.where(up_y, 0, 127)
    return rows, cols, jnp.where(up_x, 1, 7), jnp.where(up_y, 1, 127), sub, lane


def sweep_kernel(
    pos, dcs, wts, x_ref, vel, rate, spec, heat, e_ref, l0_ref, pack_ref, tab, accd, accu, d0,
):
    m = pl.program_id(0)
    k = pos[0]
    cx, cy = jnp.abs(dcs[0, 2 * k]), jnp.abs(dcs[1, 2 * k])
    cz = jnp.abs(dcs[2, 2 * k])

    @pl.when(m == 0)
    def _():
        v, a = column(vel[...]), 1.0 + column(rate[...])
        inv = 1.0 / (a + v * cz)
        for i, c in enumerate(((1.0 - v * cx - v * cy) * inv, v * cx * inv, v * cy * inv, v * cz * inv, column(spec[...]))):
            tab[i] = jnp.broadcast_to(c, (MODES, 128))
        accd[...] = jnp.zeros_like(accd)
        accu[...] = jnp.zeros_like(accu)

    rows, cols, shift_x, shift_y, sub, lane = places(dcs, k)
    alpha, beta, gamma, kappa, share = [jnp.broadcast_to(tab[i, pl.ds(m, 1), :], (8, 128)) for i in range(5)]

    def rhs(d, z):
        i = [[x_ref[d, 0, pl.ds(z * ROWS + r, 8), pl.ds(c, 128)] for c in cols] for r in rows]
        rx = [[pltpu.roll(t, shift_x, 0) for t in ts] for ts in i]
        ry = [[pltpu.roll(t, shift_y, 1) for t in ts] for ts in i]
        out = []
        for r in range(2):
            for c in range(2):
                x = jnp.where(sub, 0.0 if r == 0 else rx[0][c], rx[r][c])
                y = jnp.where(lane, 0.0 if c == 0 else ry[r][0], ry[r][c])
                out.append(alpha * i[r][c] + beta * x + gamma * y)
        return out

    tiles = [(r, c) for r in rows for c in cols]
    down = [share * heat[pl.ds(r, 8), pl.ds(c, 128)] for r, c in tiles]
    for z in reversed(range(Z)):
        down = [f + kappa * t for f, t in zip(rhs(1, z), down)]
        for t, (r, c) in zip(down, tiles):
            at = pl.ds(z * ROWS + r, 8)
            l0_ref[1, 0, at, pl.ds(c, 128)] = t
            accd[c // 128, at, :] += t
    for t, (r, c) in zip(down, tiles):
        d0[c // 128, pl.ds(pl.multiple_of(m * ROWS, ROWS) + r, 8), :] = t
    up = None
    for z in range(Z):
        up = rhs(0, z) if up is None else [f + kappa * t for f, t in zip(rhs(0, z), up)]
        for t, (r, c) in zip(up, tiles):
            at = pl.ds(z * ROWS + r, 8)
            l0_ref[0, 0, at, pl.ds(c, 128)] = t
            accu[c // 128, at, :] += t

    @pl.when(m == MODES - 1)
    def _():
        accd[...] = wts[2 * k + 1] * accd[...] + wts[2 * k] * accu[...]
        for r in range(ROWS):
            for h in range(2):
                at = pl.ds(h * 128, 128)
                pack_ref[pl.ds(r * PACK, 8), at] = e_ref[h, pl.ds(r, 8, stride=ROWS), :]
                pack_ref[pl.ds(r * PACK + 8, 8), at] = accd[h, pl.ds(r, 8, stride=ROWS), :]
                for t in range(MODES // 8):
                    pack_ref[pl.ds(r * PACK + 16 + 8 * t, 8), at] = d0[h, pl.ds(t * PLANE + r, 8, stride=ROWS), :]


def middle_kernel(wts, got, dcv, vel, rate, spec, jm_ref, k0_ref, out, q_ref):
    energy = got[0, 0:8, :]
    rest = got[0, 8:16, :]
    for s in range(1, GROUP):
        energy += got[s, 0:8, :]
        rest += got[s, 8:16, :]
    energy = energy * (1.0 / PAIRS)
    equil = energy / (1.0 + 0.3 * jnp.abs(energy))
    eq = [jnp.broadcast_to(equil[z : z + 1, :], (8, COLS)) for z in range(Z)]
    v, a = column(vel[...]), 1.0 + column(rate[...])
    c_all = v * jnp.abs(dcv[2:3, :])
    inv_all = 1.0 / (a + c_all)
    k_all = c_all * inv_all
    n_all = column(rate[...]) * column(spec[...]) * inv_all
    for j in range(GROUP):
        for t in range(MODES // 8):
            at = slice(8 * t, 8 * t + 8)
            kp = jnp.broadcast_to(k_all[at, 2 * j + 1 : 2 * j + 2], (8, COLS))
            eta = jnp.broadcast_to(n_all[at, 2 * j + 1 : 2 * j + 2], (8, COLS))
            s = eq[Z - 1]
            for z in reversed(range(Z - 1)):
                s = kp * s + eq[z]
            q_ref[j, at, :] = 0.9 * (got[j, 16 + 8 * t : 24 + 8 * t, :] + eta * s)
    acc = [jnp.zeros((8, COLS), F32) for _ in range(Z)]
    for k in range(GROUP):
        jm = jnp.broadcast_to(jm_ref[k : k + 1, :], (8, COLS))
        jm = jnp.where(jm < 0.5, float(k + 1), jm)
        near = [jnp.abs(jm - float(j + 1)) < 0.5 for j in range(GROUP)]
        w = wts[2 * k]
        for t in range(MODES // 8):
            at = slice(8 * t, 8 * t + 8)
            pick = q_ref[0, at, :]
            for j in range(1, GROUP):
                pick = jnp.where(near[j], q_ref[j, at, :], pick)
            out[k, at, :] = pick
            kp = jnp.broadcast_to(k_all[at, 2 * k : 2 * k + 1], (8, COLS))
            pick = w * pick
            for z in range(Z):
                pick = kp * pick
                acc[z] += pick
    bounce = jnp.concatenate([jnp.sum(t, axis=0, keepdims=True) for t in acc], axis=0)
    fresh = rest + bounce
    for z in range(Z):
        fresh += jnp.broadcast_to(k0_ref[:, z : z + 1], (8, COLS)) * eq[z]
    fresh = fresh * (1.0 / PAIRS)
    for k in range(GROUP):
        out[k, 32:40, :] = equil
        out[k, 40:48, :] = fresh


def finish_kernel(
    pos, dcs, l0_ref, left, right, low, high, vel, rate, spec, out_ref, en_ref, tab, eq,
):
    m = pl.program_id(0)
    k = pos[0]
    cx, cz = dcs[0, 2 * k], jnp.abs(dcs[2, 2 * k])

    @pl.when(m == 0)
    def _():
        v, a = column(vel[...]), 1.0 + column(rate[...])
        inv = 1.0 / (a + v * cz)
        for i, c in enumerate((column(rate[...]) * column(spec[...]) * inv, v * jnp.abs(cx) * inv, v * cz * inv)):
            tab[i] = jnp.broadcast_to(c, (MODES, 128))
        for z in range(Z):
            for h, back in enumerate((left, right)):
                for b in range(2):
                    to = (pl.ds(z * ROWS + 8 * b, 8), pl.ds(h * 128, 128))
                    eq[to] = back[pl.ds(8 * b * PACK + 32 + z, 8, stride=PACK), :]
                    en_ref[to] = back[pl.ds(8 * b * PACK + 40 + z, 8, stride=PACK), :]

    rows, _, _, _, sub, _ = places(dcs, k)
    eta, beta, kappa = [jnp.broadcast_to(tab[i, pl.ds(m, 1), :], (8, 128)) for i in range(3)]
    tiles = [(i, r, 128 * h, back) for i, r in enumerate(rows) for h, back in enumerate((left, right))]

    def source(d, z, i, r, c):
        s = eta * eq[pl.ds(z * ROWS + r, 8), pl.ds(c, 128)]
        if i == 0:
            at = (c // 128, pl.ds(z * 64 + d * 32 + m, 1))
            e = jnp.where(cx > 0.0, low[at], high[at])
            s += jnp.where(sub, beta * e, 0.0)
        return s

    for i, r, c, back in tiles:
        at = [(pl.ds(z * ROWS + r, 8), pl.ds(c, 128)) for z in range(Z)]
        t = None
        for z in reversed(range(Z)):
            s = source(1, z, i, r, c)
            t = s if t is None else kappa * t + s
            out_ref[(1, 0) + at[z]] = l0_ref[(1, 0) + at[z]] + t
        t = back[pl.ds(r * PACK + m, 8, stride=PACK), :]
        for z in range(Z):
            t = kappa * t + source(0, z, i, r, c)
            out_ref[(0, 0) + at[z]] = l0_ref[(0, 0) + at[z]] + t


def per_device(
    intensity, dir_cos, velocity, rate, spectrum, weight, heat, rough_cells, rough_count, rough_map
):
    position = lax.axis_index("mode").astype(jnp.int32)
    pos = position.reshape(1)
    vel, rat, spe, wei = [t.reshape(1, -1) for t in (velocity, rate, spectrum, weight)]
    slots = rough_cells.shape[0]
    smem = pl.BlockSpec(memory_space=pltpu.SMEM)

    def whole(*shape):
        return pl.BlockSpec(shape, lambda i: (0,) * len(shape))

    rows_flat = intensity.reshape(64 * PLANE, COLS)
    params = pltpu.CompilerParams(vmem_limit_bytes=40 << 20)
    energy, edge, small, jm, k0 = pl.pallas_call(
        edge_kernel,
        grid=(8,),
        in_specs=[smem] * 4
        + [pl.BlockSpec((8 * PLANE, 128), lambda i: (i, 0)), pl.BlockSpec((8 * PLANE, 128), lambda i: (i, 1)), whole(3, DIRS)]
        + [whole(1, 32)] * 4
        + [whole(1, slots), whole(GROUP, slots)],
        out_specs=[whole(2, PLANE, 128), whole(2, 512, 128), whole(40, COLS), whole(GROUP, COLS), whole(Z, 128)],
        out_shape=[
            jax.ShapeDtypeStruct(s, F32)
            for s in ((2, PLANE, 128), (2, 512, 128), (40, COLS), (GROUP, COLS), (Z, 128))
        ],
        scratch_shapes=[pltpu.VMEM((MODES, COLS), F32)] * 2 + [pltpu.VMEM((64, COLS), F32)],
        compiler_params=params,
        cost_estimate=pl.CostEstimate(flops=4 << 20, bytes_accessed=8 << 20, transcendentals=0),
        name="edges",
    )(
        pos, dir_cos, weight, rough_count, rows_flat, rows_flat, dir_cos, vel, rat, spe, wei,
        rough_cells.reshape(1, slots), rough_map.T,
    )
    count = lax.axis_size("space")
    forward = [(i, i + 1) for i in range(count - 1)]
    backward = [(t, s) for s, t in forward]
    small_low = lax.ppermute(small, "space", forward)
    small_high = lax.ppermute(small, "space", backward)
    edge_low = lax.ppermute(edge, "space", forward)
    edge_high = lax.ppermute(edge, "space", backward)

    field = intensity.reshape(2, MODES, PLANE, COLS)
    block = pl.BlockSpec((2, 1, PLANE, COLS), lambda i: (0, i, 0, 0))
    base, pack = pl.pallas_call(
        sweep_kernel,
        grid=(MODES,),
        in_specs=[smem] * 3 + [block] + [whole(1, 32)] * 3 + [whole(ROWS, COLS), whole(2, PLANE, 128)],
        out_specs=[block, whole(ROWS * PACK, COLS)],
        out_shape=[
            jax.ShapeDtypeStruct(field.shape, F32),
            jax.ShapeDtypeStruct((ROWS * PACK, COLS), F32),
        ],
        scratch_shapes=[
            pltpu.VMEM((5, MODES, 128), F32),
            pltpu.VMEM((2, PLANE, 128), F32),
            pltpu.VMEM((2, PLANE, 128), F32),
            pltpu.VMEM((2, MODES * ROWS, 128), F32),
        ],
        compiler_params=params,
        cost_estimate=pl.CostEstimate(flops=30 << 20, bytes_accessed=16 << 20, transcendentals=0),
        name="sweep",
    )(pos, dir_cos, weight, field, vel, rat, spe, heat, energy)

    up_x = lax.dynamic_slice(dir_cos, (0, 2 * position), (1, 1))[0, 0] > 0.0
    delta = jnp.where(up_x, small_low, small_high)
    start = jnp.where(up_x, 0, (ROWS - 1) * PACK) + 8
    pack = lax.dynamic_update_slice(pack, lax.dynamic_slice(pack, (start, 0), (40, COLS)) + delta, (start, 0))
    got = lax.all_to_all(pack.reshape(GROUP, PACK, COLS), "mode", 0, 0, tiled=True)

    reply = pl.pallas_call(
        middle_kernel,
        in_specs=[smem] + [pl.BlockSpec(memory_space=pltpu.VMEM)] * 7,
        out_specs=pl.BlockSpec(memory_space=pltpu.VMEM),
        out_shape=jax.ShapeDtypeStruct((GROUP, PACK, COLS), F32),
        scratch_shapes=[pltpu.VMEM((GROUP, MODES, COLS), F32)],
        compiler_params=params,
        name="middle",
    )(weight, got, dir_cos, vel, rat, spe, jm, k0)
    back = lax.all_to_all(reply, "mode", 0, 0, tiled=True).reshape(GROUP * PACK, COLS)

    fresh, energy_new = pl.pallas_call(
        finish_kernel,
        grid=(MODES,),
        in_specs=[smem] * 2
        + [block] + [pl.BlockSpec((GROUP * PACK, 128), lambda i, h=h: (0, h)) for h in range(2)]
        + [whole(2, 512, 128), whole(2, 512, 128)]
        + [whole(1, 32)] * 3,
        out_specs=[block, whole(PLANE, COLS)],
        out_shape=[
            jax.ShapeDtypeStruct(field.shape, F32),
            jax.ShapeDtypeStruct((PLANE, COLS), F32),
        ],
        scratch_shapes=[pltpu.VMEM((3, MODES, 128), F32), pltpu.VMEM((PLANE, COLS), F32)],
        compiler_params=params,
        name="finish",
    )(pos, dir_cos, base, back, back, edge_low, edge_high, vel, rat, spe)
    return fresh.reshape(intensity.shape), energy_new.reshape(Z, ROWS, COLS)


def solution(mesh):
    in_specs = (
        P("mode", None, "space", None),
        P(),
        P(),
        P(),
        P(),
        P(),
        P("space", None),
        P("space"),
        P("space"),
        P("space", None),
    )
    out_specs = (P("mode", None, "space", None), P(None, "space", None))
    return jax.shard_map(
        per_device, mesh=mesh, in_specs=in_specs, out_specs=out_specs, check_vma=False
    )
```

```python
import jax
import jax.numpy as jnp
from jax import lax
from jax.experimental import pallas as pl
from jax.experimental.pallas import tpu as pltpu
from jax.sharding import PartitionSpec as P

PAIRS = 1024
DIRS = 32
MODES = 32
Z = 8
ROWS = 16
COLS = 256
GROUP = 16
PLANE = Z * ROWS
PACK = 48
STEP = 4
F32 = jnp.float32


def column(row):
    r = lax.broadcasted_iota(jnp.int32, (MODES, MODES), 0)
    c = lax.broadcasted_iota(jnp.int32, (MODES, MODES), 1)
    return jnp.sum(jnp.where(r == c, jnp.broadcast_to(row, (MODES, MODES)), 0.0), axis=1, keepdims=True)


ALPHA, BETA, GAMMA, KAPPA, SHARE, ETA = range(6)
CHUNK = 8 * PLANE
SMALL = 512


def edge_kernel(
    pos, cnt, x_hbm, dc_h, v_h, r_h, s_h, w_h, c_h, m_h,
    x_ref, e_ref, edge_ref, tab, par, jm_ref, k0_ref, flags,
    dcv, vel, rate, spec, wv, cells, rmap, acc, sems, xsems,
):
    k = pos[0]

    def chunk(c, h):
        rows = pl.ds(pl.multiple_of(c * CHUNK, CHUNK), CHUNK)
        return pltpu.make_async_copy(x_hbm.at[rows, pl.ds(h * 128, 128)], x_ref.at[h, rows, :], xsems.at[h, c])

    few = list(zip((dc_h, v_h, r_h, s_h, w_h, c_h, m_h), (dcv, vel, rate, spec, wv, cells, rmap)))
    few = [pltpu.make_async_copy(a, b, sems.at[n]) for n, (a, b) in enumerate(few)]
    for copy in few:
        copy.start()
    for c in range(8):
        for h in range(2):
            chunk(c, h).start()
    for copy in few:
        copy.wait()

    lane = lax.broadcasted_iota(jnp.int32, (1, DIRS), 1)

    def pick(row, at):
        return jnp.sum(jnp.where(lane == at, row, 0.0))

    cx, cy, cz = [pick(dcv[n : n + 1, :], 2 * k) for n in range(3)]
    cz = jnp.abs(cz)
    flags[0] = cx
    flags[1] = cy
    flags[2] = pick(wv[...], 2 * k)
    flags[3] = pick(wv[...], 2 * k + 1)
    v, a = column(vel[...]), 1.0 + column(rate[...])
    share, eta = column(spec[...]), column(rate[...]) * column(spec[...])
    inv = 1.0 / (a + v * cz)
    table = {
        ALPHA: (1.0 - v * jnp.abs(cx) - v * jnp.abs(cy)) * inv,
        BETA: v * jnp.abs(cx) * inv,
        GAMMA: v * jnp.abs(cy) * inv,
        KAPPA: v * cz * inv,
        SHARE: share,
        ETA: eta * inv,
    }
    for n, col in table.items():
        tab[n] = jnp.broadcast_to(col, (MODES, 128))
    acc[...] = jnp.zeros_like(acc)
    e_ref[...] = jnp.zeros_like(e_ref)

    slot = lax.broadcasted_iota(jnp.int32, (1, cells.shape[1]), 1)
    local = jnp.where(slot < cnt[0], cells[...] - k * COLS, -1)
    q = lax.broadcasted_iota(jnp.int32, (COLS, cells.shape[1]), 0)
    hot = jnp.where(q == local, 1.0, 0.0).astype(jnp.bfloat16)
    idx = (rmap[...] + 1).astype(F32).astype(jnp.bfloat16)
    jm_ref[...] = lax.dot_general(idx, hot, (((1,), (1,)), ((), ())), preferred_element_type=F32)

    c_all = v * jnp.abs(dcv[2:3, :])
    inv_all = 1.0 / (a + c_all)
    k_all = c_all * inv_all
    for n, block in enumerate((k_all, eta * inv_all, jnp.broadcast_to(wv[...], (MODES, DIRS)))):
        par[n, :, pl.ds(0, DIRS)] = block
    term = eta * inv_all * wv[...]
    odd = lax.broadcasted_iota(jnp.int32, (MODES, DIRS), 1) % 2 == 1
    zr = lax.broadcasted_iota(jnp.int32, (Z, 128), 0)
    zc = lax.broadcasted_iota(jnp.int32, (Z, 128), 1)
    total = jnp.zeros((Z, 128), F32)
    for n in range(Z):
        down = jnp.sum(jnp.sum(jnp.where(odd, term, 0.0), axis=1, keepdims=True), axis=0, keepdims=True)
        up = jnp.sum(jnp.sum(jnp.where(odd, 0.0, term), axis=1, keepdims=True), axis=0, keepdims=True)
        total += jnp.where(zc - zr == n, down, 0.0) + jnp.where(zr - zc == n, up, 0.0)
        term = term * k_all
    k0_ref[...] = total

    row = jnp.where(cx > 0.0, ROWS - 1, 0)

    def one(c, carry):
        w = flags[2 + c // 4]
        base = pl.multiple_of(c * CHUNK, CHUNK)
        m0 = pl.multiple_of(8 * (c % 4), 8)
        for h in range(2):
            chunk(c, h).wait()
            for t in range(PLANE // 8):
                part = x_ref[h, pl.ds(base + t * 8, 8), :]
                for p in range(1, 8):
                    part += x_ref[h, pl.ds(base + p * PLANE + t * 8, 8), :]
                e_ref[h, pl.ds(t * 8, 8), :] += w * part
            kp, bt = [tab[n, pl.ds(m0, 8), :] for n in (KAPPA, BETA)]
            rows = []
            for z in range(Z):
                e = x_ref[h, pl.ds(base + z * ROWS + row, 8, stride=PLANE), :]
                edge_ref[h, pl.ds(pl.multiple_of(z * 64 + 8 * c, 8), 8), :] = e
                rows.append(bt * e)

            @pl.when(c < 4)
            def _():
                t = rows[0]
                acc[h, pl.ds(0, 8), :] += w * t
                for z in range(1, Z):
                    t = kp * t + rows[z]
                    acc[h, pl.ds(8 * z, 8), :] += w * t

            @pl.when(c >= 4)
            def _():
                t = rows[Z - 1]
                acc[h, pl.ds(8 * (Z - 1), 8), :] += w * t
                for z in reversed(range(Z - 1)):
                    t = kp * t + rows[z]
                    acc[h, pl.ds(8 * z, 8), :] += w * t
                edge_ref[h, pl.ds(SMALL + 8 + m0, 8), :] = t

        return carry

    lax.fori_loop(0, 8, one, 0)
    for h in range(2):
        for z in range(Z):
            edge_ref[h, pl.ds(SMALL + z, 1), :] = jnp.sum(acc[h, pl.ds(8 * z, 8), :], axis=0, keepdims=True)


def sweep_kernel(
    flags, tab, x_ref, heat, l0_ref, e0_ref, d0, accd, accu,
):
    up_x, up_y = flags[0] > 0.0, flags[1] > 0.0
    accd[...] = jnp.zeros_like(accd)
    accu[...] = jnp.zeros_like(accu)

    def run(pos_x, pos_y):
        rows = (0, 8) if pos_x else (8, 0)
        cols = (0, 1) if pos_y else (1, 0)
        tiles = [(r, c) for r in rows for c in cols]
        sub = lax.broadcasted_iota(jnp.int32, (8, 128), 0) == (0 if pos_x else 7)
        lane = lax.broadcasted_iota(jnp.int32, (8, 128), 1) == (0 if pos_y else 127)

        def pair(i, carry):
            modes = [2 * i, 2 * i + 1]
            coef = [[jnp.broadcast_to(tab[n, pl.ds(m, 1), :], (8, 128)) for n in range(4)] for m in modes]

            def rhs(d, t, z):
                alpha, beta, gamma, _ = coef[t]
                at = pl.multiple_of((d * MODES + modes[t]) * PLANE, PLANE) + z * ROWS
                f = [[x_ref[c, pl.ds(at + r, 8), :] for c in cols] for r in rows]
                rx = [[pltpu.roll(v, 1 if pos_x else 7, 0) for v in vs] for vs in f]
                ry = [[pltpu.roll(v, 1 if pos_y else 127, 1) for v in vs] for vs in f]
                out = []
                for r in range(2):
                    for c in range(2):
                        x = jnp.where(sub, 0.0 if r == 0 else rx[0][c], rx[r][c])
                        y = jnp.where(lane, 0.0 if c == 0 else ry[r][0], ry[r][c])
                        out.append(alpha * f[r][c] + beta * x + gamma * y)
                return out

            for d, acc, order in ((1, accd, range(Z - 1, -1, -1)), (0, accu, range(Z))):
                if d == 1:
                    state = [
                        [jnp.broadcast_to(tab[4, pl.ds(m, 1), :], (8, 128)) * heat[pl.ds(r, 8), pl.ds(c * 128, 128)] for r, c in tiles]
                        for m in modes
                    ]
                else:
                    state = [None, None]
                for z in order:
                    for t in range(2):
                        f = rhs(d, t, z)
                        state[t] = f if state[t] is None else [a + coef[t][3] * b for a, b in zip(f, state[t])]
                        for v, (r, c) in zip(state[t], tiles):
                            l0_ref[d, modes[t], pl.ds(z * ROWS + r, 8), pl.ds(c * 128, 128)] = v
                    for n, (r, c) in enumerate(tiles):
                        acc[c, pl.ds(z * ROWS + r, 8), :] += state[0][n] + state[1][n]
                if d == 1:
                    for t in range(2):
                        for v, (r, c) in zip(state[t], tiles):
                            d0[c, pl.ds(pl.multiple_of(modes[t] * ROWS, ROWS) + r, 8), :] = v
            return carry

        lax.fori_loop(0, MODES // 2, pair, 0)

    for pos_x in (True, False):
        for pos_y in (True, False):
            pl.when((up_x == pos_x) & (up_y == pos_y))(lambda px=pos_x, py=pos_y: run(px, py))

    e0_ref[...] = flags[3] * accd[...] + flags[2] * accu[...]


def pack_kernel(flags, e_ref, e0_ref, d0, low, high, out):
    up_x = flags[0] > 0.0
    for h in range(2):
        at = pl.ds(h * 128, 128)
        for r in range(ROWS):
            more = None
            if r == 0:
                more = jnp.where(up_x, low[h, pl.ds(SMALL, 40), :], 0.0)
            if r == ROWS - 1:
                more = jnp.where(up_x, 0.0, high[h, pl.ds(SMALL, 40), :])
            out[pl.ds(r * PACK, 8), at] = e_ref[h, pl.ds(r, 8, stride=ROWS), :]
            for t in range(5):
                if t == 0:
                    part = e0_ref[h, pl.ds(r, 8, stride=ROWS), :]
                else:
                    part = d0[h, pl.ds((t - 1) * PLANE + r, 8, stride=ROWS), :]
                if more is not None:
                    part += more[8 * t : 8 * t + 8, :]
                out[pl.ds(r * PACK + 8 + 8 * t, 8), at] = part


def middle_kernel(got, par, jm_ref, k0_ref, out, q_ref):
    energy = got[0, 0:8, :]
    rest = got[0, 8:16, :]
    for s in range(1, GROUP):
        energy += got[s, 0:8, :]
        rest += got[s, 8:16, :]
    energy = energy * (1.0 / PAIRS)
    equil = energy / (1.0 + 0.3 * jnp.abs(energy))
    eq = [jnp.broadcast_to(equil[z : z + 1, :], (8, COLS)) for z in range(Z)]
    k_all, n_all, w_all = par[0], par[1], par[2]
    for j in range(GROUP):
        for t in range(MODES // 8):
            at = slice(8 * t, 8 * t + 8)
            kp = jnp.broadcast_to(k_all[at, 2 * j + 1 : 2 * j + 2], (8, COLS))
            eta = jnp.broadcast_to(n_all[at, 2 * j + 1 : 2 * j + 2], (8, COLS))
            s = eq[Z - 1]
            for z in reversed(range(Z - 1)):
                s = kp * s + eq[z]
            q_ref[j, at, :] = 0.9 * (got[j, 16 + 8 * t : 24 + 8 * t, :] + eta * s)
    acc = [jnp.zeros((8, COLS), F32) for _ in range(Z)]
    for k in range(GROUP):
        jm = jnp.broadcast_to(jm_ref[k : k + 1, :], (8, COLS))
        jm = jnp.where(jm < 0.5, float(k + 1), jm)
        near = [jnp.abs(jm - float(j + 1)) < 0.5 for j in range(GROUP)]
        w = jnp.broadcast_to(w_all[0:8, 2 * k : 2 * k + 1], (8, COLS))
        for t in range(MODES // 8):
            at = slice(8 * t, 8 * t + 8)
            pick = q_ref[0, at, :]
            for j in range(1, GROUP):
                pick = jnp.where(near[j], q_ref[j, at, :], pick)
            out[k, at, :] = pick
            kp = jnp.broadcast_to(k_all[at, 2 * k : 2 * k + 1], (8, COLS))
            pick = w * pick
            for z in range(Z):
                pick = kp * pick
                acc[z] += pick
    bounce = jnp.concatenate([jnp.sum(t, axis=0, keepdims=True) for t in acc], axis=0)
    fresh = rest + bounce
    for z in range(Z):
        fresh += jnp.broadcast_to(k0_ref[:, z : z + 1], (8, COLS)) * eq[z]
    fresh = fresh * (1.0 / PAIRS)
    for k in range(GROUP):
        out[k, 32:40, :] = equil
        out[k, 40:48, :] = fresh


def finish_kernel(
    flags, tab, l0_ref, left, right, low, high, out_hbm, en_ref, eq, res, sems,
):
    up_x = flags[0] > 0.0
    for z in range(Z):
        for h, back in enumerate((left, right)):
            for b in range(2):
                to = (pl.ds(z * ROWS + 8 * b, 8), pl.ds(h * 128, 128))
                eq[to] = back[pl.ds(8 * b * PACK + 32 + z, 8, stride=PACK), :]
                en_ref[to] = back[pl.ds(8 * b * PACK + 40 + z, 8, stride=PACK), :]

    def leave(g, d):
        part = pl.ds(g * STEP, STEP)
        return pltpu.make_async_copy(res.at[d, part], out_hbm.at[d, part], sems.at[d, g])

    def run(pos_x):
        edge = low if pos_x else high
        first = 0 if pos_x else 8
        sub = lax.broadcasted_iota(jnp.int32, (8, 128), 0) == (0 if pos_x else 7)

        def one(m, carry):
            eta, beta, kappa = [jnp.broadcast_to(tab[n, pl.ds(m, 1), :], (8, 128)) for n in (ETA, BETA, KAPPA)]
            for r in (0, 8):
                for h, back in enumerate((left, right)):
                    at = [(pl.ds(z * ROWS + r, 8), pl.ds(h * 128, 128)) for z in range(Z)]
                    src = [eta * eq[at[z]] for z in range(Z)]

                    def source(d, z):
                        if r != first:
                            return src[z]
                        e = jnp.broadcast_to(edge[h, pl.ds(z * 64 + d * 32 + m, 1), :], (8, 128))
                        return src[z] + jnp.where(sub, beta * e, 0.0)

                    t = None
                    for z in reversed(range(Z)):
                        t = source(1, z) if t is None else kappa * t + source(1, z)
                        res[(1, m) + at[z]] = l0_ref[(1, m) + at[z]] + t
                    t = back[pl.ds(r * PACK + m, 8, stride=PACK), :]
                    for z in range(Z):
                        t = kappa * t + source(0, z)
                        res[(0, m) + at[z]] = l0_ref[(0, m) + at[z]] + t
            return carry

        def some(g, carry):
            lax.fori_loop(g * STEP, g * STEP + STEP, one, 0)
            for d in range(2):
                leave(g, d).start()
            return carry

        lax.fori_loop(0, MODES // STEP, some, 0)

    pl.when(up_x)(lambda: run(True))
    pl.when(jnp.logical_not(up_x))(lambda: run(False))
    for g in range(MODES // STEP):
        for d in range(2):
            leave(g, d).wait()


def per_device(
    intensity, dir_cos, velocity, rate, spectrum, weight, heat, rough_cells, rough_count, rough_map
):
    pos = lax.axis_index("mode").astype(jnp.int32).reshape(1)
    slots = rough_cells.shape[0]
    smem = pl.BlockSpec(memory_space=pltpu.SMEM)
    vmem = pl.BlockSpec(memory_space=pltpu.VMEM)

    def hbm(x):
        return pltpu.with_memory_space_constraint(x, pltpu.HBM)

    anywhere = pl.BlockSpec(memory_space=pltpu.HBM)
    field = (2, MODES, PLANE, COLS)
    ones = [t.reshape(1, -1) for t in (velocity, rate, spectrum, weight, rough_cells)]
    x, energy, edge, tab, par, jm, k0, flags = pl.pallas_call(
        edge_kernel,
        in_specs=[smem] * 2 + [anywhere] * 8,
        out_specs=[vmem] * 7 + [smem],
        out_shape=[
            pltpu.VMEM(s, F32)
            for s in (
                (2, 64 * PLANE, 128), (2, PLANE, 128), (2, SMALL + 40, 128), (6, MODES, 128), (3, MODES, 128),
                (GROUP, COLS), (Z, 128),
            )
        ]
        + [pltpu.SMEM((4,), F32)],
        scratch_shapes=[
            pltpu.VMEM((3, DIRS), F32),
            pltpu.VMEM((1, MODES), F32),
            pltpu.VMEM((1, MODES), F32),
            pltpu.VMEM((1, MODES), F32),
            pltpu.VMEM((1, DIRS), F32),
            pltpu.VMEM((1, slots), jnp.int32),
            pltpu.VMEM((GROUP, slots), jnp.int32),
            pltpu.VMEM((2, 64, 128), F32),
            pltpu.SemaphoreType.DMA((7,)),
            pltpu.SemaphoreType.DMA((2, 8)),
        ],
        compiler_params=pltpu.CompilerParams(vmem_limit_bytes=8 << 20),
        cost_estimate=pl.CostEstimate(flops=4 << 20, bytes_accessed=8 << 20, transcendentals=0),
        name="edges",
    )(
        pos, rough_count, hbm(intensity.reshape(64 * PLANE, COLS)), hbm(dir_cos), *[hbm(t) for t in ones], hbm(rough_map.T),
    )
    count = lax.axis_size("space")
    forward = [(i, i + 1) for i in range(count - 1)]
    backward = [(t, s) for s, t in forward]
    low = lax.ppermute(edge, "space", forward)
    high = lax.ppermute(edge, "space", backward)

    base, e0, d0 = pl.pallas_call(
        sweep_kernel,
        in_specs=[smem] + [vmem] * 3,
        out_specs=[vmem] * 3,
        out_shape=[pltpu.VMEM(s, F32) for s in (field, (2, PLANE, 128), (2, MODES * ROWS, 128))],
        scratch_shapes=[pltpu.VMEM((2, PLANE, 128), F32), pltpu.VMEM((2, PLANE, 128), F32)],
        compiler_params=pltpu.CompilerParams(vmem_limit_bytes=8 << 20),
        cost_estimate=pl.CostEstimate(flops=30 << 20, bytes_accessed=16 << 20, transcendentals=0),
        name="sweep",
    )(flags, tab, x, heat)

    pack = pl.pallas_call(
        pack_kernel,
        in_specs=[smem] + [vmem] * 5,
        out_specs=vmem,
        out_shape=pltpu.VMEM((ROWS * PACK, COLS), F32),
        compiler_params=pltpu.CompilerParams(vmem_limit_bytes=8 << 20),
        name="pack",
    )(flags, energy, e0, d0, low, high)
    got = lax.all_to_all(pack.reshape(GROUP, PACK, COLS), "mode", 0, 0, tiled=True)

    reply = pl.pallas_call(
        middle_kernel,
        in_specs=[vmem] * 4,
        out_specs=vmem,
        out_shape=pltpu.VMEM((GROUP, PACK, COLS), F32),
        scratch_shapes=[pltpu.VMEM((GROUP, MODES, COLS), F32)],
        compiler_params=pltpu.CompilerParams(vmem_limit_bytes=8 << 20),
        name="middle",
    )(got, par, jm, k0)
    back = lax.all_to_all(reply, "mode", 0, 0, tiled=True).reshape(GROUP * PACK, COLS)

    fresh, energy_new = pl.pallas_call(
        finish_kernel,
        grid=(1,),
        in_specs=[smem, vmem, vmem]
        + [pl.BlockSpec((GROUP * PACK, 128), lambda i, h=h: (0, h)) for h in range(2)]
        + [vmem] * 2,
        out_specs=[anywhere, vmem],
        out_shape=[pltpu.HBM(field, F32), jax.ShapeDtypeStruct((PLANE, COLS), F32)],
        scratch_shapes=[
            pltpu.VMEM((PLANE, COLS), F32),
            pltpu.VMEM(field, F32),
            pltpu.SemaphoreType.DMA((2, MODES // STEP)),
        ],
        compiler_params=pltpu.CompilerParams(vmem_limit_bytes=20 << 20),
        name="finish",
    )(flags, tab, base, back, back, low, high)
    return fresh.reshape(intensity.shape), energy_new.reshape(Z, ROWS, COLS)


def solution(mesh):
    in_specs = (
        P("mode", None, "space", None),
        P(),
        P(),
        P(),
        P(),
        P(),
        P("space", None),
        P("space"),
        P("space"),
        P("space", None),
    )
    out_specs = (P("mode", None, "space", None), P(None, "space", None))
    return jax.shard_map(
        per_device, mesh=mesh, in_specs=in_specs, out_specs=out_specs, check_vma=False
    )
```

```python
import jax
import jax.numpy as jnp
from jax import lax
from jax.experimental import pallas as pl
from jax.experimental.pallas import tpu as pltpu
from jax.sharding import PartitionSpec as P

PAIRS = 1024
DIRS = 32
MODES = 32
Z = 8
ROWS = 16
COLS = 256
GROUP = 16
PLANE = Z * ROWS
SEND = 24
BACK = 32
SLOTS = 1024
STEP = 4
F32 = jnp.float32


def column(row):
    r = lax.broadcasted_iota(jnp.int32, (MODES, MODES), 0)
    c = lax.broadcasted_iota(jnp.int32, (MODES, MODES), 1)
    return jnp.sum(jnp.where(r == c, jnp.broadcast_to(row, (MODES, MODES)), 0.0), axis=1, keepdims=True)


ALPHA, BETA, GAMMA, KAPPA, SHARE, ETA = range(6)
CHUNK = 8 * PLANE
EDGE = 512


def edge_kernel(
    x_hbm, dc_h, v_h, r_h, s_h, w_h,
    x_ref, e_ref, edge_ref, tab, flags,
    dcv, vel, rate, spec, wv, acc, sems, xsems,
):
    k = lax.axis_index("mode")
    odd_row = lax.axis_index("space") % 2 == 1

    def chunk(c, h):
        rows = pl.ds(pl.multiple_of(c * CHUNK, CHUNK), CHUNK)
        return pltpu.make_async_copy(x_hbm.at[rows, pl.ds(h * 128, 128)], x_ref.at[h, rows, :], xsems.at[h, c])

    few = list(zip((dc_h, v_h, r_h, s_h, w_h), (dcv, vel, rate, spec, wv)))
    few = [pltpu.make_async_copy(a, b, sems.at[n]) for n, (a, b) in enumerate(few)]
    for copy in few:
        copy.start()
    for c in range(8):
        for h in range(2):
            chunk(c, h).start()
    for copy in few:
        copy.wait()

    lane = lax.broadcasted_iota(jnp.int32, (1, DIRS), 1)

    def pick(row, at):
        return jnp.sum(jnp.where(lane == at, row, 0.0))

    cx, cy, cz = [pick(dcv[n : n + 1, :], 2 * k) for n in range(3)]
    cz = jnp.abs(cz)
    flags[0] = cx
    flags[1] = cy
    flags[2] = pick(wv[...], 2 * k)
    flags[3] = pick(wv[...], 2 * k + 1)
    flags[4] = jnp.where((cx > 0.0) == odd_row, 1.0, 0.0)
    v, a = column(vel[...]), 1.0 + column(rate[...])
    share, eta = column(spec[...]), column(rate[...]) * column(spec[...])
    inv = 1.0 / (a + v * cz)
    table = {
        ALPHA: (1.0 - v * jnp.abs(cx) - v * jnp.abs(cy)) * inv,
        BETA: v * jnp.abs(cx) * inv,
        GAMMA: v * jnp.abs(cy) * inv,
        KAPPA: v * cz * inv,
        SHARE: share,
        ETA: eta * inv,
    }
    for n, col in table.items():
        tab[n] = jnp.broadcast_to(col, (MODES, 128))
    acc[...] = jnp.zeros_like(acc)
    e_ref[...] = jnp.zeros_like(e_ref)

    row = jnp.where(cx > 0.0, ROWS - 1, 0)

    def one(c, carry):
        w = flags[2 + c // 4]
        base = pl.multiple_of(c * CHUNK, CHUNK)
        m0 = pl.multiple_of(8 * (c % 4), 8)
        for h in range(2):
            chunk(c, h).wait()
            for t in range(PLANE // 8):
                part = x_ref[h, pl.ds(base + t * 8, 8), :]
                for p in range(1, 8):
                    part += x_ref[h, pl.ds(base + p * PLANE + t * 8, 8), :]
                e_ref[h, pl.ds(t * 8, 8), :] += w * part
            kp, bt = [tab[n, pl.ds(m0, 8), :] for n in (KAPPA, BETA)]
            rows = []
            for z in range(Z):
                e = x_ref[h, pl.ds(base + z * ROWS + row, 8, stride=PLANE), :]
                edge_ref[h, pl.ds(pl.multiple_of(z * 64 + 8 * c, 8), 8), :] = e
                rows.append(bt * e)

            @pl.when(c < 4)
            def _():
                t = rows[0]
                acc[h, pl.ds(0, 8), :] += w * t
                for z in range(1, Z):
                    t = kp * t + rows[z]
                    acc[h, pl.ds(8 * z, 8), :] += w * t

            @pl.when(c >= 4)
            def _():
                t = rows[Z - 1]
                acc[h, pl.ds(8 * (Z - 1), 8), :] += w * t
                for z in reversed(range(Z - 1)):
                    t = kp * t + rows[z]
                    acc[h, pl.ds(8 * z, 8), :] += w * t
                edge_ref[h, pl.ds(EDGE + 8 + m0, 8), :] = t

        return carry

    lax.fori_loop(0, 8, one, 0)
    for h in range(2):
        for z in range(Z):
            edge_ref[h, pl.ds(EDGE + z, 1), :] = jnp.sum(acc[h, pl.ds(8 * z, 8), :], axis=0, keepdims=True)


def sweep_kernel(
    flags, tab, x_ref, heat, l0_ref, e0_ref, d0, accd, accu,
):
    up_x, up_y = flags[0] > 0.0, flags[1] > 0.0
    accd[...] = jnp.zeros_like(accd)
    accu[...] = jnp.zeros_like(accu)

    def run(pos_x, pos_y):
        rows = (0, 8) if pos_x else (8, 0)
        cols = (0, 1) if pos_y else (1, 0)
        tiles = [(r, c) for r in rows for c in cols]
        sub = lax.broadcasted_iota(jnp.int32, (8, 128), 0) == (0 if pos_x else 7)
        lane = lax.broadcasted_iota(jnp.int32, (8, 128), 1) == (0 if pos_y else 127)

        def pair(i, carry):
            modes = [2 * i, 2 * i + 1]
            coef = [[jnp.broadcast_to(tab[n, pl.ds(m, 1), :], (8, 128)) for n in range(4)] for m in modes]

            def rhs(d, t, z):
                alpha, beta, gamma, _ = coef[t]
                at = pl.multiple_of((d * MODES + modes[t]) * PLANE, PLANE) + z * ROWS
                f = [[x_ref[c, pl.ds(at + r, 8), :] for c in cols] for r in rows]
                rx = [[pltpu.roll(v, 1 if pos_x else 7, 0) for v in vs] for vs in f]
                ry = [[pltpu.roll(v, 1 if pos_y else 127, 1) for v in vs] for vs in f]
                out = []
                for r in range(2):
                    for c in range(2):
                        x = jnp.where(sub, 0.0 if r == 0 else rx[0][c], rx[r][c])
                        y = jnp.where(lane, 0.0 if c == 0 else ry[r][0], ry[r][c])
                        out.append(alpha * f[r][c] + beta * x + gamma * y)
                return out

            for d, acc, order in ((1, accd, range(Z - 1, -1, -1)), (0, accu, range(Z))):
                if d == 1:
                    state = [
                        [jnp.broadcast_to(tab[4, pl.ds(m, 1), :], (8, 128)) * heat[pl.ds(r, 8), pl.ds(c * 128, 128)] for r, c in tiles]
                        for m in modes
                    ]
                else:
                    state = [None, None]
                for z in order:
                    for t in range(2):
                        f = rhs(d, t, z)
                        state[t] = f if state[t] is None else [a + coef[t][3] * b for a, b in zip(f, state[t])]
                        for v, (r, c) in zip(state[t], tiles):
                            l0_ref[d, modes[t], pl.ds(z * ROWS + r, 8), pl.ds(c * 128, 128)] = v
                    for n, (r, c) in enumerate(tiles):
                        acc[c, pl.ds(z * ROWS + r, 8), :] += state[0][n] + state[1][n]
                if d == 1:
                    for t in range(2):
                        for v, (r, c) in zip(state[t], tiles):
                            d0[c, pl.ds(pl.multiple_of(modes[t] * ROWS, ROWS) + r, 8), :] = v
            return carry

        lax.fori_loop(0, MODES // 2, pair, 0)

    for pos_x in (True, False):
        for pos_y in (True, False):
            pl.when((up_x == pos_x) & (up_y == pos_y))(lambda px=pos_x, py=pos_y: run(px, py))

    e0_ref[...] = flags[3] * accd[...] + flags[2] * accu[...]


def split(x):
    high = x.astype(jnp.bfloat16)
    return high, (x - high.astype(F32)).astype(jnp.bfloat16)


def spread(x, hot):
    high, low = split(x)
    dims = (((1,), (1,)), ((), ()))
    return lax.dot_general(high, hot, dims, preferred_element_type=F32) + lax.dot_general(
        low, hot, dims, preferred_element_type=F32
    )


def slot_kernel(
    cnt, flags, dcv, vel, rate, spec, wv, cells, rmap, tab, d0, e0_in,
    hot_ref, rm_ref, par, jm_ref, k0_ref, mt_ref, cz_ref, ksel, nsel, slot_ref, e0_ref, parts,
):
    k = lax.axis_index("mode")
    live = lax.broadcasted_iota(jnp.int32, (1, SLOTS), 1) < cnt[0]
    q = lax.broadcasted_iota(jnp.int32, (COLS, SLOTS), 0)
    hot_ref[...] = jnp.where(q == jnp.where(live, cells[...] & (COLS - 1), -1), 1.0, 0.0).astype(jnp.bfloat16)
    hot = hot_ref[...]
    cell_row = jnp.where(live, cells[...] >> 8, -1)
    rows = lax.broadcasted_iota(jnp.int32, (ROWS, SLOTS), 0)
    rm = jnp.where(rows == cell_row, 1.0, 0.0)
    rm_ref[...] = rm
    idx = jnp.where(cell_row == k, (rmap[...] + 1).astype(F32), 0.0).astype(jnp.bfloat16)
    jm_ref[...] = lax.dot_general(idx, hot, (((1,), (1,)), ((), ())), preferred_element_type=F32)
    mt_ref[...] = rmap[:, pl.ds(pl.multiple_of(128 * (k % 8), 128), 128)].astype(F32)
    mine = jnp.sum(jnp.where(rows == k, rmap[...], 0), axis=0, keepdims=True)
    czr = jnp.zeros((1, SLOTS), F32)
    for j in range(GROUP):
        czr = jnp.where(mine == j, jnp.abs(dcv[2:3, 2 * j : 2 * j + 1]), czr)
    cz_ref[...] = spread(rm * czr, hot)

    v, a = column(vel[...]), 1.0 + column(rate[...])
    eta = column(rate[...]) * column(spec[...])
    c_all = v * jnp.abs(dcv[2:3, :])
    inv_all = 1.0 / (a + c_all)
    k_all = c_all * inv_all
    for n, block in enumerate((k_all, eta * inv_all, jnp.broadcast_to(wv[...], (MODES, DIRS)))):
        par[n, :, pl.ds(0, DIRS)] = block
    term = eta * inv_all * wv[...]
    odd = lax.broadcasted_iota(jnp.int32, (MODES, DIRS), 1) % 2 == 1
    zr = lax.broadcasted_iota(jnp.int32, (Z, 128), 0)
    zc = lax.broadcasted_iota(jnp.int32, (Z, 128), 1)
    total = jnp.zeros((Z, 128), F32)
    for n in range(Z):
        down = jnp.sum(jnp.sum(jnp.where(odd, term, 0.0), axis=1, keepdims=True), axis=0, keepdims=True)
        up = jnp.sum(jnp.sum(jnp.where(odd, 0.0, term), axis=1, keepdims=True), axis=0, keepdims=True)
        total += jnp.where(zc - zr == n, down, 0.0) + jnp.where(zr - zc == n, up, 0.0)
        term = term * k_all
    k0_ref[...] = total

    vb, ab, nb = [jnp.broadcast_to(t, (MODES, 128)) for t in (v, a, 0.9 * eta)]
    for h in range(2):
        for r in (0, 8):
            cz = cz_ref[pl.ds(r, 8), pl.ds(h * 128, 128)]
            gain = jnp.where(cz < 0.1, 0.9 * flags[2], 0.0)
            acc = [jnp.zeros((8, 128), F32) for _ in range(Z)]
            for m in range(MODES):
                at = pl.ds(m * ROWS + r, 8)
                c = vb[m : m + 1, :] * cz
                inv = 1.0 / (ab[m : m + 1, :] + c)
                ksel[h, at, :] = c * inv
                nsel[h, at, :] = nb[m : m + 1, :] * inv
                f = gain * d0[h, at, :]
                kp = jnp.broadcast_to(tab[KAPPA, pl.ds(m, 1), :], (8, 128))
                for z in range(Z):
                    f = kp * f
                    acc[z] += f
            for z in range(Z):
                at = pl.ds(z * ROWS + r, 8)
                e0_ref[h, at, :] = e0_in[h, at, :] + acc[z]

    for r in range(ROWS):
        for t in range(2):
            x = jnp.concatenate(
                [
                    jnp.concatenate([d0[h, pl.ds((2 * t + u) * PLANE + r, 8, stride=ROWS), :] for h in range(2)], axis=1)
                    for u in range(2)
                ],
                axis=0,
            )
            high, low = split(x)
            parts[0, pl.ds(r * MODES + 16 * t, 16), :] = high
            parts[1, pl.ds(r * MODES + 16 * t, 16), :] = low
    for n in range(SLOTS // 256):
        at = pl.ds(n * 256, 256)
        got = jnp.dot(parts[0], hot_ref[:, at], preferred_element_type=F32)
        got += jnp.dot(parts[1], hot_ref[:, at], preferred_element_type=F32)
        total = rm[0:1, n * 256 : n * 256 + 256] * got[0:MODES]
        for r in range(1, ROWS):
            total += rm[r : r + 1, n * 256 : n * 256 + 256] * got[r * MODES : (r + 1) * MODES]
        slot_ref[:, at] = total


def pack_kernel(flags, tab, e_ref, e0_ref, slot_ref, hot, rm, cz_ref, chip, next_chip, out):
    up_x = flags[0] > 0.0
    delta = [jnp.where(flags[4] > 0.5, chip[h, pl.ds(EDGE, 40), :], next_chip[h, pl.ds(EDGE, 40), :]) for h in range(2)]
    extra = []
    for h in range(2):
        at = slice(h * 128, h * 128 + 128)
        cz = jnp.where(up_x, cz_ref[0:1, at], cz_ref[ROWS - 1 : ROWS, at])
        gain = jnp.broadcast_to(jnp.where(cz < 0.1, 0.9 * flags[2], 0.0), (8, 128))
        acc = [jnp.zeros((8, 128), F32) for _ in range(Z)]
        for t in range(MODES // 8):
            f = gain * delta[h][8 + 8 * t : 16 + 8 * t, :]
            for z in range(Z):
                f = tab[KAPPA, pl.ds(8 * t, 8), :] * f
                acc[z] += f
        extra.append(delta[h][0:8, :] + jnp.concatenate([jnp.sum(t, axis=0, keepdims=True) for t in acc], axis=0))
    high, low = split(jnp.concatenate([d[8:40, :] for d in delta], axis=1))
    more = jnp.dot(jnp.concatenate([high, low], axis=0), hot[...], preferred_element_type=F32)
    mask = jnp.where(up_x, rm[0:1, :], rm[ROWS - 1 : ROWS, :])
    slots = slot_ref[...] + mask * (more[0:MODES, :] + more[MODES : 2 * MODES, :])
    for r in range(ROWS):
        tile, low_mode = (r % 8) * 128, 16 * (r // 8)
        for h in range(2):
            at = pl.ds(h * 128, 128)
            part = e0_ref[h, pl.ds(r, 8, stride=ROWS), :]
            if r == 0:
                part += jnp.where(up_x, extra[h], 0.0)
            if r == ROWS - 1:
                part += jnp.where(up_x, 0.0, extra[h])
            out[pl.ds(r * SEND, 8), at] = e_ref[h, pl.ds(r, 8, stride=ROWS), :]
            out[pl.ds(r * SEND + 8, 8), at] = part
            out[pl.ds(r * SEND + 16, 8), at] = slots[low_mode + 8 * h : low_mode + 8 * h + 8, tile : tile + 128]


def middle_kernel(got, par, jm_ref, k0_ref, mt_ref, out, q_ref):
    energy = got[0, 0:8, :]
    rest = got[0, 8:16, :]
    for s in range(1, GROUP):
        energy += got[s, 0:8, :]
        rest += got[s, 8:16, :]
    energy = energy * (1.0 / PAIRS)
    equil = energy / (1.0 + 0.3 * jnp.abs(energy))
    eq = [jnp.broadcast_to(equil[z : z + 1, :], (8, COLS)) for z in range(Z)]
    k_all, n_all, w_all = par[0], par[1], par[2]
    for j in range(GROUP):
        for t in range(MODES // 8):
            at = slice(8 * t, 8 * t + 8)
            kp = jnp.broadcast_to(k_all[at, 2 * j + 1 : 2 * j + 2], (8, COLS))
            eta = jnp.broadcast_to(n_all[at, 2 * j + 1 : 2 * j + 2], (8, COLS))
            s = eq[Z - 1]
            for z in reversed(range(Z - 1)):
                s = kp * s + eq[z]
            q_ref[j, at, :] = (0.9 * eta) * s
    acc = [jnp.zeros((8, COLS), F32) for _ in range(Z)]
    for k in range(GROUP):
        jm = jnp.broadcast_to(jm_ref[k : k + 1, :], (8, COLS))
        jm = jnp.where(jm < 0.5, float(k + 1), jm)
        near = [jnp.abs(jm - float(j + 1)) < 0.5 for j in range(GROUP)]
        w = jnp.broadcast_to(w_all[0:8, 2 * k : 2 * k + 1], (8, COLS))
        for t in range(MODES // 8):
            at = slice(8 * t, 8 * t + 8)
            pick = q_ref[0, at, :]
            for j in range(1, GROUP):
                pick = jnp.where(near[j], q_ref[j, at, :], pick)
            kp = jnp.broadcast_to(k_all[at, 2 * k : 2 * k + 1], (8, COLS))
            pick = w * pick
            for z in range(Z):
                pick = kp * pick
                acc[z] += pick
    bounce = jnp.concatenate([jnp.sum(t, axis=0, keepdims=True) for t in acc], axis=0)
    first = pl.multiple_of(16 * (lax.axis_index("mode") // 8), 16)
    acc = [jnp.zeros((8, COLS), F32) for _ in range(Z)]
    for k in range(GROUP):
        index = jnp.concatenate([jnp.broadcast_to(mt_ref[k : k + 1, :], (8, 128))] * 2, axis=1)
        pick = got[0, 16:24, :]
        for j in range(1, GROUP):
            pick = jnp.where(index > j - 0.5, got[j, 16:24, :], pick)
        pick = 0.9 * pick
        out[k, 0:8, :] = pick
        kp = jnp.concatenate(
            [jnp.broadcast_to(par[0, pl.ds(first + 8 * u, 8), pl.ds(0, 128)][:, 2 * k : 2 * k + 1], (8, 128)) for u in range(2)],
            axis=1,
        )
        pick = jnp.broadcast_to(w_all[0:8, 2 * k : 2 * k + 1], (8, COLS)) * pick
        for z in range(Z):
            pick = kp * pick
            acc[z] += pick
    sums = [jnp.sum(t, axis=0, keepdims=True) for t in acc]
    at_slots = jnp.concatenate([t[:, 0:128] + t[:, 128:256] for t in sums], axis=0) * (1.0 / PAIRS)
    at_slots = jnp.concatenate([at_slots, jnp.zeros((Z, 128), F32)], axis=1)
    fresh = rest + bounce
    for z in range(Z):
        fresh += jnp.broadcast_to(k0_ref[:, z : z + 1], (8, COLS)) * eq[z]
    fresh = fresh * (1.0 / PAIRS)
    for k in range(GROUP):
        out[k, 8:16, :] = equil
        out[k, 16:24, :] = fresh
        out[k, 24:32, :] = at_slots


def finish_kernel(
    flags, tab, l0_ref, left, right, hot_ref, rm_ref, cz_ref, ksel, nsel, chip, next_chip,
    out_hbm, en_ref, eq, res, cell, grid_en, sems,
):
    up_x = flags[0] > 0.0
    hot = hot_ref[...]
    picked = [
        jnp.concatenate([back[pl.ds((8 * half + t) * BACK, 8), :] for t in range(8)], axis=1)
        for half in range(2) for back in (left, right)
    ]
    heard = jnp.concatenate(
        [left[pl.ds(t * BACK + 24, 8), :] + left[pl.ds((8 + t) * BACK + 24, 8), :] for t in range(8)], axis=1
    )
    for part in range(4):
        lhs = []
        for r in range(4 * part, 4 * part + 4):
            lhs += [rm_ref[r : r + 1, :] * t for t in picked + [heard]]
        got = spread(jnp.concatenate(lhs, axis=0), hot)
        for n, r in enumerate(range(4 * part, 4 * part + 4)):
            for h, back in enumerate((left, right)):
                cell[h, pl.ds(r * MODES, MODES), :] = got[40 * n : 40 * n + 32, h * 128 : h * 128 + 128]
                grid_en[h, pl.ds(r * 8, 8), :] = got[40 * n + 32 : 40 * n + 40, h * 128 : h * 128 + 128] + back[pl.ds(r * BACK + 16, 8), :]
    for z in range(Z):
        for h, back in enumerate((left, right)):
            for b in range(2):
                to = (pl.ds(z * ROWS + 8 * b, 8), pl.ds(h * 128, 128))
                eq[to] = back[pl.ds(8 * b * BACK + 8 + z, 8, stride=BACK), :]
                en_ref[to] = grid_en[h, pl.ds(8 * b * 8 + z, 8, stride=8), :]

    def leave(g, d):
        part = pl.ds(g * STEP, STEP)
        return pltpu.make_async_copy(res.at[d, part], out_hbm.at[d, part], sems.at[d, g])

    def run(pos_x, edge):
        first = 0 if pos_x else 8
        sub = lax.broadcasted_iota(jnp.int32, (8, 128), 0) == (0 if pos_x else 7)

        def one(m, carry):
            eta, beta, kappa = [jnp.broadcast_to(tab[n, pl.ds(m, 1), :], (8, 128)) for n in (ETA, BETA, KAPPA)]
            for r in (0, 8):
                for h in range(2):
                    at = [(pl.ds(z * ROWS + r, 8), pl.ds(h * 128, 128)) for z in range(Z)]
                    here = pl.ds(pl.multiple_of(m * ROWS, ROWS) + r, 8)
                    kp = ksel[h, here, :]
                    far = eq[at[Z - 1]]
                    for z in reversed(range(Z - 1)):
                        far = kp * far + eq[at[z]]
                    far = nsel[h, here, :] * far + cell[h, pl.ds(r * MODES + m, 8, stride=MODES), :]
                    rough = cz_ref[pl.ds(r, 8), pl.ds(h * 128, 128)] > 0.1
                    src = [eta * eq[at[z]] for z in range(Z)]

                    def source(d, z):
                        if r != first:
                            return src[z]
                        e = jnp.broadcast_to(edge[h, pl.ds(z * 64 + d * 32 + m, 1), :], (8, 128))
                        return src[z] + jnp.where(sub, beta * e, 0.0)

                    t = None
                    for z in reversed(range(Z)):
                        t = source(1, z) if t is None else kappa * t + source(1, z)
                        bottom = l0_ref[(1, m) + at[z]] + t
                        res[(1, m) + at[z]] = bottom
                    t = jnp.where(rough, far, 0.9 * bottom)
                    for z in range(Z):
                        t = kappa * t + source(0, z)
                        res[(0, m) + at[z]] = l0_ref[(0, m) + at[z]] + t
            return carry

        def some(g, carry):
            lax.fori_loop(g * STEP, g * STEP + STEP, one, 0)
            for d in range(2):
                leave(g, d).start()
            return carry

        lax.fori_loop(0, MODES // STEP, some, 0)

    on_chip = flags[4] > 0.5
    for pos_x in (True, False):
        for here, edge in ((True, chip), (False, next_chip)):
            pl.when((up_x == pos_x) & (on_chip == here))(lambda p=pos_x, e=edge: run(p, e))
    for g in range(MODES // STEP):
        for d in range(2):
            leave(g, d).wait()


def per_device(
    intensity, dir_cos, velocity, rate, spectrum, weight, heat, rough_cells, rough_count, rough_map
):
    smem = pl.BlockSpec(memory_space=pltpu.SMEM)
    vmem = pl.BlockSpec(memory_space=pltpu.VMEM)

    def hbm(x):
        return pltpu.with_memory_space_constraint(x, pltpu.HBM)

    anywhere = pl.BlockSpec(memory_space=pltpu.HBM)
    field = (2, MODES, PLANE, COLS)
    ones = [t.reshape(1, -1) for t in (velocity, rate, spectrum, weight, rough_cells)]
    x, energy, edge, tab, flags = pl.pallas_call(
        edge_kernel,
        in_specs=[anywhere] * 6,
        out_specs=[vmem] * 4 + [smem],
        out_shape=[
            pltpu.VMEM(s, F32)
            for s in ((2, 64 * PLANE, 128), (2, PLANE, 128), (2, EDGE + 40, 128), (6, MODES, 128))
        ]
        + [pltpu.SMEM((5,), F32)],
        scratch_shapes=[
            pltpu.VMEM((3, DIRS), F32),
            pltpu.VMEM((1, MODES), F32),
            pltpu.VMEM((1, MODES), F32),
            pltpu.VMEM((1, MODES), F32),
            pltpu.VMEM((1, DIRS), F32),
            pltpu.VMEM((2, 64, 128), F32),
            pltpu.SemaphoreType.DMA((5,)),
            pltpu.SemaphoreType.DMA((2, 8)),
        ],
        compiler_params=pltpu.CompilerParams(vmem_limit_bytes=8 << 20),
        cost_estimate=pl.CostEstimate(flops=4 << 20, bytes_accessed=8 << 20, transcendentals=0),
        name="edges",
    )(hbm(intensity.reshape(64 * PLANE, COLS)), hbm(dir_cos), *[hbm(t) for t in ones[:4]])
    count = lax.axis_size("space")
    on_chip = [(i, i ^ 1) for i in range(count)]
    across = [(i, i + 1 if i % 2 else i - 1) for i in range(1, count - 1)]
    edge_chip, edge_next = [lax.ppermute(edge, "space", p) for p in (on_chip, across)]

    base, e0, d0 = pl.pallas_call(
        sweep_kernel,
        in_specs=[smem] + [vmem] * 3,
        out_specs=[vmem] * 3,
        out_shape=[pltpu.VMEM(s, F32) for s in (field, (2, PLANE, 128), (2, MODES * ROWS, 128))],
        scratch_shapes=[pltpu.VMEM((2, PLANE, 128), F32), pltpu.VMEM((2, PLANE, 128), F32)],
        compiler_params=pltpu.CompilerParams(vmem_limit_bytes=8 << 20),
        cost_estimate=pl.CostEstimate(flops=30 << 20, bytes_accessed=16 << 20, transcendentals=0),
        name="sweep",
    )(flags, tab, x, heat)

    tables = [
        ((COLS, SLOTS), jnp.bfloat16), ((ROWS, SLOTS), F32), ((3, MODES, 128), F32), ((GROUP, COLS), F32),
        ((Z, 128), F32), ((GROUP, 128), F32), ((ROWS, COLS), F32), ((2, MODES * ROWS, 128), F32),
        ((2, MODES * ROWS, 128), F32), ((MODES, SLOTS), F32), ((2, PLANE, 128), F32),
    ]
    hot, rm, par, jm, k0, mt, cz, ksel, nsel, at_slots, e0 = pl.pallas_call(
        slot_kernel,
        in_specs=[smem] * 2 + [vmem] * 10,
        out_specs=[vmem] * len(tables),
        out_shape=[pltpu.VMEM(*t) for t in tables],
        scratch_shapes=[pltpu.VMEM((2, MODES * ROWS, COLS), jnp.bfloat16)],
        compiler_params=pltpu.CompilerParams(vmem_limit_bytes=12 << 20),
        cost_estimate=pl.CostEstimate(flops=30 << 20, bytes_accessed=8 << 20, transcendentals=0),
        name="slots",
    )(rough_count, flags, dir_cos, *ones, rough_map.T, tab, d0, e0)

    pack = pl.pallas_call(
        pack_kernel,
        in_specs=[smem] + [vmem] * 9,
        out_specs=vmem,
        out_shape=pltpu.VMEM((ROWS * SEND, COLS), F32),
        compiler_params=pltpu.CompilerParams(vmem_limit_bytes=8 << 20),
        name="pack",
    )(flags, tab, energy, e0, at_slots, hot, rm, cz, edge_chip, edge_next)
    got = lax.all_to_all(pack.reshape(GROUP, SEND, COLS), "mode", 0, 0, tiled=True)

    reply = pl.pallas_call(
        middle_kernel,
        in_specs=[vmem] * 5,
        out_specs=vmem,
        out_shape=pltpu.VMEM((GROUP, BACK, COLS), F32),
        scratch_shapes=[pltpu.VMEM((GROUP, MODES, COLS), F32)],
        compiler_params=pltpu.CompilerParams(vmem_limit_bytes=8 << 20),
        name="middle",
    )(got, par, jm, k0, mt)
    back = lax.all_to_all(reply, "mode", 0, 0, tiled=True).reshape(GROUP * BACK, COLS)

    fresh, energy_new = pl.pallas_call(
        finish_kernel,
        grid=(1,),
        in_specs=[smem, vmem, vmem]
        + [pl.BlockSpec((GROUP * BACK, 128), lambda i, h=h: (0, h)) for h in range(2)]
        + [vmem] * 7,
        out_specs=[anywhere, vmem],
        out_shape=[pltpu.HBM(field, F32), jax.ShapeDtypeStruct((PLANE, COLS), F32)],
        scratch_shapes=[
            pltpu.VMEM((PLANE, COLS), F32),
            pltpu.VMEM(field, F32),
            pltpu.VMEM((2, MODES * ROWS, 128), F32),
            pltpu.VMEM((2, PLANE, 128), F32),
            pltpu.SemaphoreType.DMA((2, MODES // STEP)),
        ],
        compiler_params=pltpu.CompilerParams(vmem_limit_bytes=24 << 20),
        name="finish",
    )(flags, tab, base, back, back, hot, rm, cz, ksel, nsel, edge_chip, edge_next)
    return fresh.reshape(intensity.shape), energy_new.reshape(Z, ROWS, COLS)


def solution(mesh):
    in_specs = (
        P("mode", None, "space", None),
        P(),
        P(),
        P(),
        P(),
        P(),
        P("space", None),
        P("space"),
        P("space"),
        P("space", None),
    )
    out_specs = (P("mode", None, "space", None), P(None, "space", None))
    return jax.shard_map(
        per_device, mesh=mesh, in_specs=in_specs, out_specs=out_specs, check_vma=False
    )
```

```python
import jax
import jax.numpy as jnp
from jax import lax
from jax.experimental import pallas as pl
from jax.experimental.pallas import tpu as pltpu
from jax.sharding import PartitionSpec as P

PAIRS = 1024
DIRS = 32
MODES = 32
Z = 8
ROWS = 16
COLS = 256
GROUP = 16
PLANE = Z * ROWS
SEND = 24
BACK = 32
SLOTS = 1024
STEP = 4
F32 = jnp.float32


def column(row):
    r = lax.broadcasted_iota(jnp.int32, (MODES, MODES), 0)
    c = lax.broadcasted_iota(jnp.int32, (MODES, MODES), 1)
    return jnp.sum(jnp.where(r == c, jnp.broadcast_to(row, (MODES, MODES)), 0.0), axis=1, keepdims=True)


ALPHA, BETA, GAMMA, KAPPA, SHARE, ETA = range(6)
CHUNK = 8 * Z
EDGE = 512


def half_tiles(x_hbm, dst, sems, half, c, h):
    src = x_hbm.at[pl.ds(c * CHUNK, CHUNK), half, :, pl.ds(h * 128, 128)]
    return pltpu.make_async_copy(src, dst.at[h, pl.ds(c * CHUNK, CHUNK)], sems.at[h, c])


def edge_kernel(
    x_hbm, dc_h, v_h, r_h, s_h, w_h,
    x_ref, edge_ref, tab, flags,
    dcv, vel, rate, spec, wv, acc, sems, xsems,
):
    k = lax.axis_index("mode")
    odd_row = lax.axis_index("space") % 2 == 1
    few = list(zip((dc_h, v_h, r_h, s_h, w_h), (dcv, vel, rate, spec, wv)))
    few = [pltpu.make_async_copy(a, b, sems.at[n]) for n, (a, b) in enumerate(few)]
    for copy in few:
        copy.start()
    few[0].wait()
    lane = lax.broadcasted_iota(jnp.int32, (1, DIRS), 1)

    def pick(row, at):
        return jnp.sum(jnp.where(lane == at, row, 0.0))

    cx, cy, cz = [pick(dcv[n : n + 1, :], 2 * k) for n in range(3)]
    half = jnp.where(cx > 0.0, 1, 0)
    for c in range(8):
        for h in range(2):
            half_tiles(x_hbm, x_ref, xsems, half, c, h).start()
    for copy in few[1:]:
        copy.wait()
    cz = jnp.abs(cz)
    flags[0] = cx
    flags[1] = cy
    flags[2] = pick(wv[...], 2 * k)
    flags[3] = pick(wv[...], 2 * k + 1)
    flags[4] = jnp.where((cx > 0.0) == odd_row, 1.0, 0.0)
    v, a = column(vel[...]), 1.0 + column(rate[...])
    share, eta = column(spec[...]), column(rate[...]) * column(spec[...])
    inv = 1.0 / (a + v * cz)
    table = {
        ALPHA: (1.0 - v * jnp.abs(cx) - v * jnp.abs(cy)) * inv,
        BETA: v * jnp.abs(cx) * inv,
        GAMMA: v * jnp.abs(cy) * inv,
        KAPPA: v * cz * inv,
        SHARE: share,
        ETA: eta * inv,
    }
    for n, col in table.items():
        tab[n] = jnp.broadcast_to(col, (MODES, 128))
    acc[...] = jnp.zeros_like(acc)

    row = jnp.where(cx > 0.0, 7, 0)
    flat = x_ref.reshape(2, 512 * 8, 128)

    def one(c, carry):
        w = flags[2 + c // 4]
        base = pl.multiple_of(c * CHUNK * 8, CHUNK * 8)
        m0 = pl.multiple_of(8 * (c % 4), 8)
        for h in range(2):
            half_tiles(x_hbm, x_ref, xsems, half, c, h).wait()
            kp, bt = [tab[n, pl.ds(m0, 8), :] for n in (KAPPA, BETA)]
            rows = []
            for z in range(Z):
                e = flat[h, pl.ds(base + z * 8 + row, 8, stride=8 * Z), :]
                edge_ref[h, pl.ds(pl.multiple_of(z * 64 + 8 * c, 8), 8), :] = e
                rows.append(bt * e)

            @pl.when(c < 4)
            def _():
                t = rows[0]
                acc[h, pl.ds(0, 8), :] += w * t
                for z in range(1, Z):
                    t = kp * t + rows[z]
                    acc[h, pl.ds(8 * z, 8), :] += w * t

            @pl.when(c >= 4)
            def _():
                t = rows[Z - 1]
                acc[h, pl.ds(8 * (Z - 1), 8), :] += w * t
                for z in reversed(range(Z - 1)):
                    t = kp * t + rows[z]
                    acc[h, pl.ds(8 * z, 8), :] += w * t
                edge_ref[h, pl.ds(EDGE + 8 + m0, 8), :] = t

        return carry

    lax.fori_loop(0, 8, one, 0)
    for h in range(2):
        for z in range(Z):
            edge_ref[h, pl.ds(EDGE + z, 1), :] = jnp.sum(acc[h, pl.ds(8 * z, 8), :], axis=0, keepdims=True)


def sweep_kernel(
    flags, tab, x_hbm, far_ref, heat, l0_ref, e_ref, e0_ref, d0, near_ref, accd, accu, xsems,
):
    up_x, up_y = flags[0] > 0.0, flags[1] > 0.0
    half = jnp.where(up_x, 0, 1)
    for g in range(4):
        for c in (4 + g, g):
            for h in range(2):
                half_tiles(x_hbm, near_ref, xsems, half, c, h).start()
    accd[...] = jnp.zeros_like(accd)
    accu[...] = jnp.zeros_like(accu)
    e_ref[...] = jnp.zeros_like(e_ref)

    def run(pos_x, pos_y):
        rows = (0, 8) if pos_x else (8, 0)
        cols = (0, 1) if pos_y else (1, 0)
        tiles = [(r, c) for r in rows for c in cols]
        sub = lax.broadcasted_iota(jnp.int32, (8, 128), 0) == (0 if pos_x else 7)
        lane = lax.broadcasted_iota(jnp.int32, (8, 128), 1) == (0 if pos_y else 127)

        def pair(i, carry):
            modes = [2 * i, 2 * i + 1]
            coef = [[jnp.broadcast_to(tab[n, pl.ds(m, 1), :], (8, 128)) for n in range(4)] for m in modes]

            def rhs(d, t, z):
                alpha, beta, gamma, _ = coef[t]
                at = (d * MODES + modes[t]) * Z + z
                f = [[ref[c, at] for c in cols] for ref in (near_ref, far_ref)]
                rx = [[pltpu.roll(v, 1 if pos_x else 7, 0) for v in vs] for vs in f]
                ry = [[pltpu.roll(v, 1 if pos_y else 127, 1) for v in vs] for vs in f]
                out = []
                for r in range(2):
                    for c in range(2):
                        x = jnp.where(sub, 0.0 if r == 0 else rx[0][c], rx[r][c])
                        y = jnp.where(lane, 0.0 if c == 0 else ry[r][0], ry[r][c])
                        out.append(alpha * f[r][c] + beta * x + gamma * y)
                return out, f[0] + f[1]

            for d, acc, order in ((1, accd, range(Z - 1, -1, -1)), (0, accu, range(Z))):
                if d == 1:
                    state = [
                        [jnp.broadcast_to(tab[4, pl.ds(m, 1), :], (8, 128)) * heat[pl.ds(r, 8), pl.ds(c * 128, 128)] for r, c in tiles]
                        for m in modes
                    ]
                else:
                    state = [None, None]
                weight = flags[2 + d]
                for z in order:
                    sums = []
                    for t in range(2):
                        f, raw = rhs(d, t, z)
                        sums.append(raw)
                        state[t] = f if state[t] is None else [a + coef[t][3] * b for a, b in zip(f, state[t])]
                        for v, (r, c) in zip(state[t], tiles):
                            l0_ref[d, modes[t], pl.ds(z * ROWS + r, 8), pl.ds(c * 128, 128)] = v
                    for n, (r, c) in enumerate(tiles):
                        acc[c, pl.ds(z * ROWS + r, 8), :] += state[0][n] + state[1][n]
                        e_ref[c, pl.ds(z * ROWS + r, 8), :] += weight * (sums[0][n] + sums[1][n])
                if d == 1:
                    for t in range(2):
                        for v, (r, c) in zip(state[t], tiles):
                            d0[c, pl.ds(pl.multiple_of(modes[t] * ROWS, ROWS) + r, 8), :] = v
            return carry

        def eight(g, carry):
            for c in (4 + g, g):
                for h in range(2):
                    half_tiles(x_hbm, near_ref, xsems, half, c, h).wait()
            return lax.fori_loop(4 * g, 4 * g + 4, pair, carry)

        lax.fori_loop(0, 4, eight, 0)

    for pos_x in (True, False):
        for pos_y in (True, False):
            pl.when((up_x == pos_x) & (up_y == pos_y))(lambda px=pos_x, py=pos_y: run(px, py))

    e0_ref[...] = flags[3] * accd[...] + flags[2] * accu[...]


def split(x):
    high = x.astype(jnp.bfloat16)
    return high, (x - high.astype(F32)).astype(jnp.bfloat16)


def spread(x, hot):
    high, low = split(x)
    dims = (((1,), (1,)), ((), ()))
    return lax.dot_general(high, hot, dims, preferred_element_type=F32) + lax.dot_general(
        low, hot, dims, preferred_element_type=F32
    )


def slot_kernel(
    cnt, flags, dcv, vel, rate, spec, wv, cells, rmap, tab, d0, e0_in,
    hot_ref, rm_ref, par, jm_ref, k0_ref, mt_ref, cz_ref, ksel, nsel, slot_ref, e0_ref, parts,
):
    k = lax.axis_index("mode")
    live = lax.broadcasted_iota(jnp.int32, (1, SLOTS), 1) < cnt[0]
    q = lax.broadcasted_iota(jnp.int32, (COLS, SLOTS), 0)
    hot_ref[...] = jnp.where(q == jnp.where(live, cells[...] & (COLS - 1), -1), 1.0, 0.0).astype(jnp.bfloat16)
    hot = hot_ref[...]
    cell_row = jnp.where(live, cells[...] >> 8, -1)
    rows = lax.broadcasted_iota(jnp.int32, (ROWS, SLOTS), 0)
    rm = jnp.where(rows == cell_row, 1.0, 0.0)
    rm_ref[...] = rm
    idx = jnp.where(cell_row == k, (rmap[...] + 1).astype(F32), 0.0).astype(jnp.bfloat16)
    jm_ref[...] = lax.dot_general(idx, hot, (((1,), (1,)), ((), ())), preferred_element_type=F32)
    mt_ref[...] = rmap[:, pl.ds(pl.multiple_of(128 * (k % 8), 128), 128)].astype(F32)
    mine = jnp.sum(jnp.where(rows == k, rmap[...], 0), axis=0, keepdims=True)
    czr = jnp.zeros((1, SLOTS), F32)
    for j in range(GROUP):
        czr = jnp.where(mine == j, jnp.abs(dcv[2:3, 2 * j : 2 * j + 1]), czr)
    cz_ref[...] = spread(rm * czr, hot)

    v, a = column(vel[...]), 1.0 + column(rate[...])
    eta = column(rate[...]) * column(spec[...])
    c_all = v * jnp.abs(dcv[2:3, :])
    inv_all = 1.0 / (a + c_all)
    k_all = c_all * inv_all
    for n, block in enumerate((k_all, eta * inv_all, jnp.broadcast_to(wv[...], (MODES, DIRS)))):
        par[n, :, pl.ds(0, DIRS)] = block
    term = eta * inv_all * wv[...]
    odd = lax.broadcasted_iota(jnp.int32, (MODES, DIRS), 1) % 2 == 1
    zr = lax.broadcasted_iota(jnp.int32, (Z, 128), 0)
    zc = lax.broadcasted_iota(jnp.int32, (Z, 128), 1)
    total = jnp.zeros((Z, 128), F32)
    for n in range(Z):
        down = jnp.sum(jnp.sum(jnp.where(odd, term, 0.0), axis=1, keepdims=True), axis=0, keepdims=True)
        up = jnp.sum(jnp.sum(jnp.where(odd, 0.0, term), axis=1, keepdims=True), axis=0, keepdims=True)
        total += jnp.where(zc - zr == n, down, 0.0) + jnp.where(zr - zc == n, up, 0.0)
        term = term * k_all
    k0_ref[...] = total

    vb, ab, nb = [jnp.broadcast_to(t, (MODES, 128)) for t in (v, a, 0.9 * eta)]
    for h in range(2):
        for r in (0, 8):
            cz = cz_ref[pl.ds(r, 8), pl.ds(h * 128, 128)]
            gain = jnp.where(cz < 0.1, 0.9 * flags[2], 0.0)
            acc = [jnp.zeros((8, 128), F32) for _ in range(Z)]
            for m in range(MODES):
                at = pl.ds(m * ROWS + r, 8)
                c = vb[m : m + 1, :] * cz
                inv = 1.0 / (ab[m : m + 1, :] + c)
                ksel[h, at, :] = c * inv
                nsel[h, at, :] = nb[m : m + 1, :] * inv
                f = gain * d0[h, at, :]
                kp = jnp.broadcast_to(tab[KAPPA, pl.ds(m, 1), :], (8, 128))
                for z in range(Z):
                    f = kp * f
                    acc[z] += f
            for z in range(Z):
                at = pl.ds(z * ROWS + r, 8)
                e0_ref[h, at, :] = e0_in[h, at, :] + acc[z]

    for r in range(ROWS):
        for t in range(2):
            x = jnp.concatenate(
                [
                    jnp.concatenate([d0[h, pl.ds((2 * t + u) * PLANE + r, 8, stride=ROWS), :] for h in range(2)], axis=1)
                    for u in range(2)
                ],
                axis=0,
            )
            high, low = split(x)
            parts[0, pl.ds(r * MODES + 16 * t, 16), :] = high
            parts[1, pl.ds(r * MODES + 16 * t, 16), :] = low
    for n in range(SLOTS // 256):
        at = pl.ds(n * 256, 256)
        got = jnp.dot(parts[0], hot_ref[:, at], preferred_element_type=F32)
        got += jnp.dot(parts[1], hot_ref[:, at], preferred_element_type=F32)
        total = rm[0:1, n * 256 : n * 256 + 256] * got[0:MODES]
        for r in range(1, ROWS):
            total += rm[r : r + 1, n * 256 : n * 256 + 256] * got[r * MODES : (r + 1) * MODES]
        slot_ref[:, at] = total


def pack_kernel(flags, tab, e_ref, e0_ref, slot_ref, hot, rm, cz_ref, chip, next_chip, out):
    up_x = flags[0] > 0.0
    delta = [jnp.where(flags[4] > 0.5, chip[h, pl.ds(EDGE, 40), :], next_chip[h, pl.ds(EDGE, 40), :]) for h in range(2)]
    extra = []
    for h in range(2):
        at = slice(h * 128, h * 128 + 128)
        cz = jnp.where(up_x, cz_ref[0:1, at], cz_ref[ROWS - 1 : ROWS, at])
        gain = jnp.broadcast_to(jnp.where(cz < 0.1, 0.9 * flags[2], 0.0), (8, 128))
        acc = [jnp.zeros((8, 128), F32) for _ in range(Z)]
        for t in range(MODES // 8):
            f = gain * delta[h][8 + 8 * t : 16 + 8 * t, :]
            for z in range(Z):
                f = tab[KAPPA, pl.ds(8 * t, 8), :] * f
                acc[z] += f
        extra.append(delta[h][0:8, :] + jnp.concatenate([jnp.sum(t, axis=0, keepdims=True) for t in acc], axis=0))
    high, low = split(jnp.concatenate([d[8:40, :] for d in delta], axis=1))
    more = jnp.dot(jnp.concatenate([high, low], axis=0), hot[...], preferred_element_type=F32)
    mask = jnp.where(up_x, rm[0:1, :], rm[ROWS - 1 : ROWS, :])
    slots = slot_ref[...] + mask * (more[0:MODES, :] + more[MODES : 2 * MODES, :])
    for r in range(ROWS):
        tile, low_mode = (r % 8) * 128, 16 * (r // 8)
        for h in range(2):
            at = pl.ds(h * 128, 128)
            part = e0_ref[h, pl.ds(r, 8, stride=ROWS), :]
            if r == 0:
                part += jnp.where(up_x, extra[h], 0.0)
            if r == ROWS - 1:
                part += jnp.where(up_x, 0.0, extra[h])
            out[pl.ds(r * SEND, 8), at] = e_ref[h, pl.ds(r, 8, stride=ROWS), :]
            out[pl.ds(r * SEND + 8, 8), at] = part
            out[pl.ds(r * SEND + 16, 8), at] = slots[low_mode + 8 * h : low_mode + 8 * h + 8, tile : tile + 128]


def middle_kernel(got, par, jm_ref, k0_ref, mt_ref, out, q_ref):
    energy = got[0, 0:8, :]
    rest = got[0, 8:16, :]
    for s in range(1, GROUP):
        energy += got[s, 0:8, :]
        rest += got[s, 8:16, :]
    energy = energy * (1.0 / PAIRS)
    equil = energy / (1.0 + 0.3 * jnp.abs(energy))
    eq = [jnp.broadcast_to(equil[z : z + 1, :], (8, COLS)) for z in range(Z)]
    k_all, n_all, w_all = par[0], par[1], par[2]
    for j in range(GROUP):
        for t in range(MODES // 8):
            at = slice(8 * t, 8 * t + 8)
            kp = jnp.broadcast_to(k_all[at, 2 * j + 1 : 2 * j + 2], (8, COLS))
            eta = jnp.broadcast_to(n_all[at, 2 * j + 1 : 2 * j + 2], (8, COLS))
            s = eq[Z - 1]
            for z in reversed(range(Z - 1)):
                s = kp * s + eq[z]
            q_ref[j, at, :] = (0.9 * eta) * s
    acc = [jnp.zeros((8, COLS), F32) for _ in range(Z)]
    for k in range(GROUP):
        jm = jnp.broadcast_to(jm_ref[k : k + 1, :], (8, COLS))
        jm = jnp.where(jm < 0.5, float(k + 1), jm)
        w = jnp.broadcast_to(w_all[0:8, 2 * k : 2 * k + 1], (8, COLS))
        for t in range(MODES // 8):
            at = slice(8 * t, 8 * t + 8)
            pick = q_ref[0, at, :]
            for j in range(1, GROUP):
                pick = jnp.where(jm > j + 0.5, q_ref[j, at, :], pick)
            kp = jnp.broadcast_to(k_all[at, 2 * k : 2 * k + 1], (8, COLS))
            pick = w * pick
            for z in range(Z):
                pick = kp * pick
                acc[z] += pick
    bounce = jnp.concatenate([jnp.sum(t, axis=0, keepdims=True) for t in acc], axis=0)
    first = pl.multiple_of(16 * (lax.axis_index("mode") // 8), 16)
    acc = [jnp.zeros((8, COLS), F32) for _ in range(Z)]
    for k in range(GROUP):
        index = jnp.concatenate([jnp.broadcast_to(mt_ref[k : k + 1, :], (8, 128))] * 2, axis=1)
        pick = got[0, 16:24, :]
        for j in range(1, GROUP):
            pick = jnp.where(index > j - 0.5, got[j, 16:24, :], pick)
        pick = 0.9 * pick
        out[k, 0:8, :] = pick
        kp = jnp.concatenate(
            [jnp.broadcast_to(par[0, pl.ds(first + 8 * u, 8), pl.ds(0, 128)][:, 2 * k : 2 * k + 1], (8, 128)) for u in range(2)],
            axis=1,
        )
        pick = jnp.broadcast_to(w_all[0:8, 2 * k : 2 * k + 1], (8, COLS)) * pick
        for z in range(Z):
            pick = kp * pick
            acc[z] += pick
    sums = [jnp.sum(t, axis=0, keepdims=True) for t in acc]
    at_slots = jnp.concatenate([t[:, 0:128] + t[:, 128:256] for t in sums], axis=0) * (1.0 / PAIRS)
    at_slots = jnp.concatenate([at_slots, jnp.zeros((Z, 128), F32)], axis=1)
    fresh = rest + bounce
    for z in range(Z):
        fresh += jnp.broadcast_to(k0_ref[:, z : z + 1], (8, COLS)) * eq[z]
    fresh = fresh * (1.0 / PAIRS)
    for k in range(GROUP):
        out[k, 8:16, :] = equil
        out[k, 16:24, :] = fresh
        out[k, 24:32, :] = at_slots


def finish_kernel(
    flags, tab, l0_ref, left, right, hot_ref, rm_ref, cz_ref, ksel, nsel, chip, next_chip,
    out_hbm, en_ref, eq, res, cell, grid_en, sems,
):
    up_x, on_chip = flags[0] > 0.0, flags[4] > 0.5
    for z in range(Z):
        for h, back in enumerate((left, right)):
            for b in range(2):
                eq[pl.ds(z * ROWS + 8 * b, 8), pl.ds(h * 128, 128)] = back[pl.ds(8 * b * BACK + 8 + z, 8, stride=BACK), :]

    def leave(g, d):
        part = pl.ds(g * STEP, STEP)
        return pltpu.make_async_copy(res.at[d, part], out_hbm.at[d, part], sems.at[d, g])

    def run(d, pos_x, edge):
        first = 0 if pos_x else 8
        sub = lax.broadcasted_iota(jnp.int32, (8, 128), 0) == (0 if pos_x else 7)

        def pair(i, carry):
            modes = [2 * i, 2 * i + 1]
            eta, beta, kappa = [
                [jnp.broadcast_to(tab[n, pl.ds(m, 1), :], (8, 128)) for m in modes] for n in (ETA, BETA, KAPPA)
            ]
            for r in (0, 8):
                for h in range(2):
                    at = [(pl.ds(z * ROWS + r, 8), pl.ds(h * 128, 128)) for z in range(Z)]
                    e = [eq[to] for to in at]

                    def source(n, z):
                        s = eta[n] * e[z]
                        if r == first:
                            row = edge[h, pl.ds(z * 64 + d * 32 + modes[n], 1), :]
                            s += jnp.where(sub, beta[n] * jnp.broadcast_to(row, (8, 128)), 0.0)
                        return s

                    t = [None, None]
                    if d == 0:
                        rough = cz_ref[pl.ds(r, 8), pl.ds(h * 128, 128)] > 0.1
                        here = [pl.ds(pl.multiple_of(m * ROWS, ROWS) + r, 8) for m in modes]
                        kp = [ksel[h, to, :] for to in here]
                        far = [e[Z - 1]] * 2
                        for z in reversed(range(Z - 1)):
                            far = [a * b + e[z] for a, b in zip(kp, far)]
                        for n, m in enumerate(modes):
                            far[n] = nsel[h, here[n], :] * far[n] + cell[h, pl.ds(r * MODES + m, 8, stride=MODES), :]
                            t[n] = jnp.where(rough, far[n], 0.9 * res[(1, m) + at[0]])
                    for z in range(Z) if d == 0 else range(Z - 1, -1, -1):
                        for n, m in enumerate(modes):
                            t[n] = source(n, z) if t[n] is None else kappa[n] * t[n] + source(n, z)
                            res[(d, m) + at[z]] = l0_ref[(d, m) + at[z]] + t[n]
            return carry

        def some(g, carry):
            lax.fori_loop(g * STEP // 2, g * STEP // 2 + STEP // 2, pair, 0)
            leave(g, d).start()
            return carry

        lax.fori_loop(0, MODES // STEP, some, 0)

    def all_modes(d):
        for pos_x in (True, False):
            for here, edge in ((True, chip), (False, next_chip)):
                pl.when((up_x == pos_x) & (on_chip == here))(lambda p=pos_x, e=edge: run(d, p, e))

    all_modes(1)
    hot = hot_ref[...]
    picked = [
        jnp.concatenate([back[pl.ds((8 * half + t) * BACK, 8), :] for t in range(8)], axis=1)
        for half in range(2) for back in (left, right)
    ]
    heard = jnp.concatenate(
        [left[pl.ds(t * BACK + 24, 8), :] + left[pl.ds((8 + t) * BACK + 24, 8), :] for t in range(8)], axis=1
    )
    for part in range(4):
        lhs = []
        for r in range(4 * part, 4 * part + 4):
            lhs += [rm_ref[r : r + 1, :] * t for t in picked + [heard]]
        got = spread(jnp.concatenate(lhs, axis=0), hot)
        for n, r in enumerate(range(4 * part, 4 * part + 4)):
            for h, back in enumerate((left, right)):
                cell[h, pl.ds(r * MODES, MODES), :] = got[40 * n : 40 * n + 32, h * 128 : h * 128 + 128]
                grid_en[h, pl.ds(r * 8, 8), :] = got[40 * n + 32 : 40 * n + 40, h * 128 : h * 128 + 128] + back[pl.ds(r * BACK + 16, 8), :]
    all_modes(0)
    for z in range(Z):
        for h in range(2):
            for b in range(2):
                en_ref[pl.ds(z * ROWS + 8 * b, 8), pl.ds(h * 128, 128)] = grid_en[h, pl.ds(8 * b * 8 + z, 8, stride=8), :]
    for g in range(MODES // STEP):
        for d in range(2):
            leave(g, d).wait()


def per_device(
    intensity, dir_cos, velocity, rate, spectrum, weight, heat, rough_cells, rough_count, rough_map
):
    smem = pl.BlockSpec(memory_space=pltpu.SMEM)
    vmem = pl.BlockSpec(memory_space=pltpu.VMEM)

    def hbm(x):
        return pltpu.with_memory_space_constraint(x, pltpu.HBM)

    anywhere = pl.BlockSpec(memory_space=pltpu.HBM)
    field = (2, MODES, PLANE, COLS)
    ones = [t.reshape(1, -1) for t in (velocity, rate, spectrum, weight, rough_cells)]
    tiles = hbm(intensity.reshape(512, 2, 8, COLS))
    x, edge, tab, flags = pl.pallas_call(
        edge_kernel,
        in_specs=[anywhere] * 6,
        out_specs=[vmem] * 3 + [smem],
        out_shape=[
            pltpu.VMEM(s, F32)
            for s in ((2, 512, 8, 128), (2, EDGE + 40, 128), (6, MODES, 128))
        ]
        + [pltpu.SMEM((5,), F32)],
        scratch_shapes=[
            pltpu.VMEM((3, DIRS), F32),
            pltpu.VMEM((1, MODES), F32),
            pltpu.VMEM((1, MODES), F32),
            pltpu.VMEM((1, MODES), F32),
            pltpu.VMEM((1, DIRS), F32),
            pltpu.VMEM((2, 64, 128), F32),
            pltpu.SemaphoreType.DMA((5,)),
            pltpu.SemaphoreType.DMA((2, 8)),
        ],
        compiler_params=pltpu.CompilerParams(vmem_limit_bytes=8 << 20),
        cost_estimate=pl.CostEstimate(flops=4 << 20, bytes_accessed=8 << 20, transcendentals=0),
        name="edges",
    )(tiles, hbm(dir_cos), *[hbm(t) for t in ones[:4]])
    count = lax.axis_size("space")
    on_chip = [(i, i ^ 1) for i in range(count)]
    across = [(i, i + 1 if i % 2 else i - 1) for i in range(1, count - 1)]
    edge_chip, edge_next = [lax.ppermute(edge, "space", p) for p in (on_chip, across)]

    base, energy, e0, d0 = pl.pallas_call(
        sweep_kernel,
        in_specs=[smem, vmem, anywhere, vmem, vmem],
        out_specs=[vmem] * 4,
        out_shape=[pltpu.VMEM(s, F32) for s in (field, (2, PLANE, 128), (2, PLANE, 128), (2, MODES * ROWS, 128))],
        scratch_shapes=[
            pltpu.VMEM((2, 512, 8, 128), F32),
            pltpu.VMEM((2, PLANE, 128), F32),
            pltpu.VMEM((2, PLANE, 128), F32),
            pltpu.SemaphoreType.DMA((2, 8)),
        ],
        compiler_params=pltpu.CompilerParams(vmem_limit_bytes=12 << 20),
        cost_estimate=pl.CostEstimate(flops=30 << 20, bytes_accessed=16 << 20, transcendentals=0),
        name="sweep",
    )(flags, tab, tiles, x, heat)

    tables = [
        ((COLS, SLOTS), jnp.bfloat16), ((ROWS, SLOTS), F32), ((3, MODES, 128), F32), ((GROUP, COLS), F32),
        ((Z, 128), F32), ((GROUP, 128), F32), ((ROWS, COLS), F32), ((2, MODES * ROWS, 128), F32),
        ((2, MODES * ROWS, 128), F32), ((MODES, SLOTS), F32), ((2, PLANE, 128), F32),
    ]
    hot, rm, par, jm, k0, mt, cz, ksel, nsel, at_slots, e0 = pl.pallas_call(
        slot_kernel,
        in_specs=[smem] * 2 + [vmem] * 10,
        out_specs=[vmem] * len(tables),
        out_shape=[pltpu.VMEM(*t) for t in tables],
        scratch_shapes=[pltpu.VMEM((2, MODES * ROWS, COLS), jnp.bfloat16)],
        compiler_params=pltpu.CompilerParams(vmem_limit_bytes=12 << 20),
        cost_estimate=pl.CostEstimate(flops=30 << 20, bytes_accessed=8 << 20, transcendentals=0),
        name="slots",
    )(rough_count, flags, dir_cos, *ones, rough_map.T, tab, d0, e0)

    pack = pl.pallas_call(
        pack_kernel,
        in_specs=[smem] + [vmem] * 9,
        out_specs=vmem,
        out_shape=pltpu.VMEM((ROWS * SEND, COLS), F32),
        compiler_params=pltpu.CompilerParams(vmem_limit_bytes=8 << 20),
        name="pack",
    )(flags, tab, energy, e0, at_slots, hot, rm, cz, edge_chip, edge_next)
    got = lax.all_to_all(pack.reshape(GROUP, SEND, COLS), "mode", 0, 0, tiled=True)

    reply = pl.pallas_call(
        middle_kernel,
        in_specs=[vmem] * 5,
        out_specs=vmem,
        out_shape=pltpu.VMEM((GROUP, BACK, COLS), F32),
        scratch_shapes=[pltpu.VMEM((GROUP, MODES, COLS), F32)],
        compiler_params=pltpu.CompilerParams(vmem_limit_bytes=8 << 20),
        name="middle",
    )(got, par, jm, k0, mt)
    back = lax.all_to_all(reply, "mode", 0, 0, tiled=True).reshape(GROUP * BACK, COLS)

    fresh, energy_new = pl.pallas_call(
        finish_kernel,
        grid=(1,),
        in_specs=[smem, vmem, vmem]
        + [pl.BlockSpec((GROUP * BACK, 128), lambda i, h=h: (0, h)) for h in range(2)]
        + [vmem] * 7,
        out_specs=[anywhere, vmem],
        out_shape=[pltpu.HBM(field, F32), jax.ShapeDtypeStruct((PLANE, COLS), F32)],
        scratch_shapes=[
            pltpu.VMEM((PLANE, COLS), F32),
            pltpu.VMEM(field, F32),
            pltpu.VMEM((2, MODES * ROWS, 128), F32),
            pltpu.VMEM((2, PLANE, 128), F32),
            pltpu.SemaphoreType.DMA((2, MODES // STEP)),
        ],
        compiler_params=pltpu.CompilerParams(vmem_limit_bytes=24 << 20),
        name="finish",
    )(flags, tab, base, back, back, hot, rm, cz, ksel, nsel, edge_chip, edge_next)
    return fresh.reshape(intensity.shape), energy_new.reshape(Z, ROWS, COLS)


def solution(mesh):
    in_specs = (
        P("mode", None, "space", None),
        P(),
        P(),
        P(),
        P(),
        P(),
        P("space", None),
        P("space"),
        P("space"),
        P("space", None),
    )
    out_specs = (P("mode", None, "space", None), P(None, "space", None))
    return jax.shard_map(
        per_device, mesh=mesh, in_specs=in_specs, out_specs=out_specs, check_vma=False
    )
```

```python
import jax
import jax.numpy as jnp
from jax import lax
from jax.experimental import pallas as pl
from jax.experimental.pallas import tpu as pltpu
from jax.sharding import PartitionSpec as P

PAIRS = 1024
DIRS = 32
MODES = 32
Z = 8
ROWS = 16
COLS = 256
GROUP = 16
PLANE = Z * ROWS
SEND = 24
BACK = 32
SLOTS = 1024
STEP = 4
F32 = jnp.float32


def column(row):
    r = lax.broadcasted_iota(jnp.int32, (MODES, MODES), 0)
    c = lax.broadcasted_iota(jnp.int32, (MODES, MODES), 1)
    return jnp.sum(jnp.where(r == c, jnp.broadcast_to(row, (MODES, MODES)), 0.0), axis=1, keepdims=True)


ALPHA, BETA, GAMMA, KAPPA, SHARE, ETA = range(6)
CHUNK = 8 * Z
EDGE = 512


def half_tiles(x_hbm, dst, sems, half, c, h):
    src = x_hbm.at[pl.ds(c * CHUNK, CHUNK), half, :, pl.ds(h * 128, 128)]
    return pltpu.make_async_copy(src, dst.at[h, pl.ds(c * CHUNK, CHUNK)], sems.at[h, c])


def edge_kernel(
    x_hbm, dc_h, v_h, r_h, s_h, w_h,
    x_ref, edge_ref, tab, flags,
    dcv, vel, rate, spec, wv, acc, sems, xsems,
):
    k = lax.axis_index("mode")
    odd_row = lax.axis_index("space") % 2 == 1
    few = list(zip((dc_h, v_h, r_h, s_h, w_h), (dcv, vel, rate, spec, wv)))
    few = [pltpu.make_async_copy(a, b, sems.at[n]) for n, (a, b) in enumerate(few)]
    for copy in few:
        copy.start()
    few[0].wait()
    lane = lax.broadcasted_iota(jnp.int32, (1, DIRS), 1)

    def pick(row, at):
        return jnp.sum(jnp.where(lane == at, row, 0.0))

    cx, cy, cz = [pick(dcv[n : n + 1, :], 2 * k) for n in range(3)]
    half = jnp.where(cx > 0.0, 1, 0)
    for c in range(8):
        for h in range(2):
            half_tiles(x_hbm, x_ref, xsems, half, c, h).start()
    for copy in few[1:]:
        copy.wait()
    cz = jnp.abs(cz)
    flags[0] = cx
    flags[1] = cy
    flags[2] = pick(wv[...], 2 * k)
    flags[3] = pick(wv[...], 2 * k + 1)
    flags[4] = jnp.where((cx > 0.0) == odd_row, 1.0, 0.0)
    v, a = column(vel[...]), 1.0 + column(rate[...])
    share, eta = column(spec[...]), column(rate[...]) * column(spec[...])
    inv = 1.0 / (a + v * cz)
    table = {
        ALPHA: (1.0 - v * jnp.abs(cx) - v * jnp.abs(cy)) * inv,
        BETA: v * jnp.abs(cx) * inv,
        GAMMA: v * jnp.abs(cy) * inv,
        KAPPA: v * cz * inv,
        SHARE: share,
        ETA: eta * inv,
    }
    for n, col in table.items():
        tab[n] = jnp.broadcast_to(col, (MODES, 128))
    acc[...] = jnp.zeros_like(acc)

    row = jnp.where(cx > 0.0, 7, 0)
    flat = x_ref.reshape(2, 512 * 8, 128)

    def one(c, carry):
        w = flags[2 + c // 4]
        base = pl.multiple_of(c * CHUNK * 8, CHUNK * 8)
        m0 = pl.multiple_of(8 * (c % 4), 8)
        for h in range(2):
            half_tiles(x_hbm, x_ref, xsems, half, c, h).wait()
            kp, bt = [tab[n, pl.ds(m0, 8), :] for n in (KAPPA, BETA)]
            rows = []
            for z in range(Z):
                e = flat[h, pl.ds(base + z * 8 + row, 8, stride=8 * Z), :]
                edge_ref[h, pl.ds(pl.multiple_of(z * 64 + 8 * c, 8), 8), :] = e
                rows.append(bt * e)

            @pl.when(c < 4)
            def _():
                t = rows[0]
                acc[h, pl.ds(0, 8), :] += w * t
                for z in range(1, Z):
                    t = kp * t + rows[z]
                    acc[h, pl.ds(8 * z, 8), :] += w * t

            @pl.when(c >= 4)
            def _():
                t = rows[Z - 1]
                acc[h, pl.ds(8 * (Z - 1), 8), :] += w * t
                for z in reversed(range(Z - 1)):
                    t = kp * t + rows[z]
                    acc[h, pl.ds(8 * z, 8), :] += w * t
                edge_ref[h, pl.ds(EDGE + 8 + m0, 8), :] = t

        return carry

    lax.fori_loop(0, 8, one, 0)
    for h in range(2):
        for z in range(Z):
            edge_ref[h, pl.ds(EDGE + z, 1), :] = jnp.sum(acc[h, pl.ds(8 * z, 8), :], axis=0, keepdims=True)


def sweep_kernel(
    flags, tab, x_hbm, far_ref, heat, l0_ref, e_ref, e0_ref, d0, near_ref, accd, accu, xsems,
):
    up_x, up_y = flags[0] > 0.0, flags[1] > 0.0
    half = jnp.where(up_x, 0, 1)
    for g in range(4):
        for c in (4 + g, g):
            for h in range(2):
                half_tiles(x_hbm, near_ref, xsems, half, c, h).start()
    accd[...] = jnp.zeros_like(accd)
    accu[...] = jnp.zeros_like(accu)
    e_ref[...] = jnp.zeros_like(e_ref)

    def run(pos_x, pos_y):
        rows = (0, 8) if pos_x else (8, 0)
        cols = (0, 1) if pos_y else (1, 0)
        tiles = [(r, c) for r in rows for c in cols]
        sub = lax.broadcasted_iota(jnp.int32, (8, 128), 0) == (0 if pos_x else 7)
        lane = lax.broadcasted_iota(jnp.int32, (8, 128), 1) == (0 if pos_y else 127)

        def pair(i, carry):
            modes = [2 * i, 2 * i + 1]
            coef = [[jnp.broadcast_to(tab[n, pl.ds(m, 1), :], (8, 128)) for n in range(4)] for m in modes]

            def rhs(d, t, z):
                alpha, beta, gamma, _ = coef[t]
                at = (d * MODES + modes[t]) * Z + z
                f = [[ref[c, at] for c in cols] for ref in (near_ref, far_ref)]
                rx = [[pltpu.roll(v, 1 if pos_x else 7, 0) for v in vs] for vs in f]
                ry = [[pltpu.roll(v, 1 if pos_y else 127, 1) for v in vs] for vs in f]
                out = []
                for r in range(2):
                    for c in range(2):
                        x = jnp.where(sub, 0.0 if r == 0 else rx[0][c], rx[r][c])
                        y = jnp.where(lane, 0.0 if c == 0 else ry[r][0], ry[r][c])
                        out.append(alpha * f[r][c] + beta * x + gamma * y)
                return out, f[0] + f[1]

            for d, acc, order in ((1, accd, range(Z - 1, -1, -1)), (0, accu, range(Z))):
                if d == 1:
                    state = [
                        [jnp.broadcast_to(tab[4, pl.ds(m, 1), :], (8, 128)) * heat[pl.ds(r, 8), pl.ds(c * 128, 128)] for r, c in tiles]
                        for m in modes
                    ]
                else:
                    state = [None, None]
                weight = flags[2 + d]
                for z in order:
                    sums = []
                    for t in range(2):
                        f, raw = rhs(d, t, z)
                        sums.append(raw)
                        state[t] = f if state[t] is None else [a + coef[t][3] * b for a, b in zip(f, state[t])]
                        for v, (r, c) in zip(state[t], tiles):
                            l0_ref[d, modes[t], pl.ds(z * ROWS + r, 8), pl.ds(c * 128, 128)] = v
                    for n, (r, c) in enumerate(tiles):
                        acc[c, pl.ds(z * ROWS + r, 8), :] += state[0][n] + state[1][n]
                        e_ref[c, pl.ds(z * ROWS + r, 8), :] += weight * (sums[0][n] + sums[1][n])
                if d == 1:
                    for t in range(2):
                        for v, (r, c) in zip(state[t], tiles):
                            d0[c, pl.ds(pl.multiple_of(modes[t] * ROWS, ROWS) + r, 8), :] = v
            return carry

        def eight(g, carry):
            for c in (4 + g, g):
                for h in range(2):
                    half_tiles(x_hbm, near_ref, xsems, half, c, h).wait()
            return lax.fori_loop(4 * g, 4 * g + 4, pair, carry)

        lax.fori_loop(0, 4, eight, 0)

    for pos_x in (True, False):
        for pos_y in (True, False):
            pl.when((up_x == pos_x) & (up_y == pos_y))(lambda px=pos_x, py=pos_y: run(px, py))

    e0_ref[...] = flags[3] * accd[...] + flags[2] * accu[...]


def split(x):
    high = x.astype(jnp.bfloat16)
    return high, (x - high.astype(F32)).astype(jnp.bfloat16)


def spread(x, hot):
    high, low = split(x)
    dims = (((1,), (1,)), ((), ()))
    return lax.dot_general(high, hot, dims, preferred_element_type=F32) + lax.dot_general(
        low, hot, dims, preferred_element_type=F32
    )


def slot_kernel(
    cnt, flags, dcv, vel, rate, spec, wv, cells, rmap, tab, d0, e0_in,
    hot_ref, rm_ref, par, jm_ref, k0_ref, mt_ref, cz_ref, ksel, nsel, slot_ref, e0_ref, parts,
):
    k = lax.axis_index("mode")
    live = lax.broadcasted_iota(jnp.int32, (1, SLOTS), 1) < cnt[0]
    q = lax.broadcasted_iota(jnp.int32, (COLS, SLOTS), 0)
    hot_ref[...] = jnp.where(q == jnp.where(live, cells[...] & (COLS - 1), -1), 1.0, 0.0).astype(jnp.bfloat16)
    hot = hot_ref[...]
    cell_row = jnp.where(live, cells[...] >> 8, -1)
    rows = lax.broadcasted_iota(jnp.int32, (ROWS, SLOTS), 0)
    rm = jnp.where(rows == cell_row, 1.0, 0.0)
    rm_ref[...] = rm
    idx = jnp.where(cell_row == k, (rmap[...] + 1).astype(F32), 0.0).astype(jnp.bfloat16)
    jm_ref[...] = lax.dot_general(idx, hot, (((1,), (1,)), ((), ())), preferred_element_type=F32)
    mt_ref[...] = rmap[:, pl.ds(pl.multiple_of(128 * (k % 8), 128), 128)].astype(F32)
    mine = jnp.sum(jnp.where(rows == k, rmap[...], 0), axis=0, keepdims=True)
    czr = jnp.zeros((1, SLOTS), F32)
    for j in range(GROUP):
        czr = jnp.where(mine == j, jnp.abs(dcv[2:3, 2 * j : 2 * j + 1]), czr)
    cz_ref[...] = spread(rm * czr, hot)

    v, a = column(vel[...]), 1.0 + column(rate[...])
    eta = column(rate[...]) * column(spec[...])
    c_all = v * jnp.abs(dcv[2:3, :])
    inv_all = 1.0 / (a + c_all)
    k_all = c_all * inv_all
    for n, block in enumerate((k_all, eta * inv_all, jnp.broadcast_to(wv[...], (MODES, DIRS)))):
        par[n, :, pl.ds(0, DIRS)] = block
    term = eta * inv_all * wv[...]
    odd = lax.broadcasted_iota(jnp.int32, (MODES, DIRS), 1) % 2 == 1
    zr = lax.broadcasted_iota(jnp.int32, (Z, 128), 0)
    zc = lax.broadcasted_iota(jnp.int32, (Z, 128), 1)
    total = jnp.zeros((Z, 128), F32)
    for n in range(Z):
        down = jnp.sum(jnp.sum(jnp.where(odd, term, 0.0), axis=1, keepdims=True), axis=0, keepdims=True)
        up = jnp.sum(jnp.sum(jnp.where(odd, 0.0, term), axis=1, keepdims=True), axis=0, keepdims=True)
        total += jnp.where(zc - zr == n, down, 0.0) + jnp.where(zr - zc == n, up, 0.0)
        term = term * k_all
    k0_ref[...] = total

    vb, ab, nb = [jnp.broadcast_to(t, (MODES, 128)) for t in (v, a, 0.9 * eta)]
    for h in range(2):
        for r in (0, 8):
            cz = cz_ref[pl.ds(r, 8), pl.ds(h * 128, 128)]
            gain = jnp.where(cz < 0.1, 0.9 * flags[2], 0.0)
            acc = [jnp.zeros((8, 128), F32) for _ in range(Z)]
            for m in range(MODES):
                at = pl.ds(m * ROWS + r, 8)
                c = vb[m : m + 1, :] * cz
                inv = 1.0 / (ab[m : m + 1, :] + c)
                ksel[h, at, :] = c * inv
                nsel[h, at, :] = nb[m : m + 1, :] * inv
                f = gain * d0[h, at, :]
                kp = jnp.broadcast_to(tab[KAPPA, pl.ds(m, 1), :], (8, 128))
                for z in range(Z):
                    f = kp * f
                    acc[z] += f
            for z in range(Z):
                at = pl.ds(z * ROWS + r, 8)
                e0_ref[h, at, :] = e0_in[h, at, :] + acc[z]

    for r in range(ROWS):
        for t in range(2):
            x = jnp.concatenate(
                [
                    jnp.concatenate([d0[h, pl.ds((2 * t + u) * PLANE + r, 8, stride=ROWS), :] for h in range(2)], axis=1)
                    for u in range(2)
                ],
                axis=0,
            )
            high, low = split(x)
            parts[0, pl.ds(r * MODES + 16 * t, 16), :] = high
            parts[1, pl.ds(r * MODES + 16 * t, 16), :] = low
    for n in range(SLOTS // 256):
        at = pl.ds(n * 256, 256)
        got = jnp.dot(parts[0], hot_ref[:, at], preferred_element_type=F32)
        got += jnp.dot(parts[1], hot_ref[:, at], preferred_element_type=F32)
        total = rm[0:1, n * 256 : n * 256 + 256] * got[0:MODES]
        for r in range(1, ROWS):
            total += rm[r : r + 1, n * 256 : n * 256 + 256] * got[r * MODES : (r + 1) * MODES]
        slot_ref[:, at] = total


def pack_kernel(flags, tab, e_ref, e0_ref, slot_ref, hot, rm, cz_ref, chip, next_chip, out):
    up_x = flags[0] > 0.0
    delta = [jnp.where(flags[4] > 0.5, chip[h, pl.ds(EDGE, 40), :], next_chip[h, pl.ds(EDGE, 40), :]) for h in range(2)]
    extra = []
    for h in range(2):
        at = slice(h * 128, h * 128 + 128)
        cz = jnp.where(up_x, cz_ref[0:1, at], cz_ref[ROWS - 1 : ROWS, at])
        gain = jnp.broadcast_to(jnp.where(cz < 0.1, 0.9 * flags[2], 0.0), (8, 128))
        acc = [jnp.zeros((8, 128), F32) for _ in range(Z)]
        for t in range(MODES // 8):
            f = gain * delta[h][8 + 8 * t : 16 + 8 * t, :]
            for z in range(Z):
                f = tab[KAPPA, pl.ds(8 * t, 8), :] * f
                acc[z] += f
        extra.append(delta[h][0:8, :] + jnp.concatenate([jnp.sum(t, axis=0, keepdims=True) for t in acc], axis=0))
    high, low = split(jnp.concatenate([d[8:40, :] for d in delta], axis=1))
    more = jnp.dot(jnp.concatenate([high, low], axis=0), hot[...], preferred_element_type=F32)
    mask = jnp.where(up_x, rm[0:1, :], rm[ROWS - 1 : ROWS, :])
    slots = slot_ref[...] + mask * (more[0:MODES, :] + more[MODES : 2 * MODES, :])
    for r in range(ROWS):
        tile, low_mode = (r % 8) * 128, 16 * (r // 8)
        for h in range(2):
            part = e0_ref[h, pl.ds(r, 8, stride=ROWS), :]
            if r == 0:
                part += jnp.where(up_x, extra[h], 0.0)
            if r == ROWS - 1:
                part += jnp.where(up_x, 0.0, extra[h])
            out[r, h, 0:8, :] = e_ref[h, pl.ds(r, 8, stride=ROWS), :]
            out[r, h, 8:16, :] = part
            out[r, h, 16:24, :] = slots[low_mode + 8 * h : low_mode + 8 * h + 8, tile : tile + 128]


def middle_kernel(got, par, jm_ref, k0_ref, mt_ref, out, q_ref):
    def take(s, at):
        return jnp.concatenate([got[s, h, at : at + 8, :] for h in range(2)], axis=1)

    energy = take(0, 0)
    rest = take(0, 8)
    for s in range(1, GROUP):
        energy += take(s, 0)
        rest += take(s, 8)
    energy = energy * (1.0 / PAIRS)
    equil = energy / (1.0 + 0.3 * jnp.abs(energy))
    eq = [jnp.broadcast_to(equil[z : z + 1, :], (8, COLS)) for z in range(Z)]
    k_all, n_all, w_all = par[0], par[1], par[2]
    for j in range(GROUP):
        for t in range(MODES // 8):
            at = slice(8 * t, 8 * t + 8)
            kp = jnp.broadcast_to(k_all[at, 2 * j + 1 : 2 * j + 2], (8, COLS))
            eta = jnp.broadcast_to(n_all[at, 2 * j + 1 : 2 * j + 2], (8, COLS))
            s = eq[Z - 1]
            for z in reversed(range(Z - 1)):
                s = kp * s + eq[z]
            q_ref[j, at, :] = (0.9 * eta) * s
    acc = [jnp.zeros((8, COLS), F32) for _ in range(Z)]
    for k in range(GROUP):
        jm = jnp.broadcast_to(jm_ref[k : k + 1, :], (8, COLS))
        jm = jnp.where(jm < 0.5, float(k + 1), jm)
        w = jnp.broadcast_to(w_all[0:8, 2 * k : 2 * k + 1], (8, COLS))
        for t in range(MODES // 8):
            at = slice(8 * t, 8 * t + 8)
            pick = q_ref[0, at, :]
            for j in range(1, GROUP):
                pick = jnp.where(jm > j + 0.5, q_ref[j, at, :], pick)
            kp = jnp.broadcast_to(k_all[at, 2 * k : 2 * k + 1], (8, COLS))
            pick = w * pick
            for z in range(Z):
                pick = kp * pick
                acc[z] += pick
    bounce = jnp.concatenate([jnp.sum(t, axis=0, keepdims=True) for t in acc], axis=0)
    first = pl.multiple_of(16 * (lax.axis_index("mode") // 8), 16)
    acc = [jnp.zeros((8, COLS), F32) for _ in range(Z)]
    for k in range(GROUP):
        index = jnp.concatenate([jnp.broadcast_to(mt_ref[k : k + 1, :], (8, 128))] * 2, axis=1)
        pick = take(0, 16)
        for j in range(1, GROUP):
            pick = jnp.where(index > j - 0.5, take(j, 16), pick)
        pick = 0.9 * pick
        for h in range(2):
            out[k, h, 0:8, :] = pick[:, h * 128 : h * 128 + 128]
        kp = jnp.concatenate(
            [jnp.broadcast_to(par[0, pl.ds(first + 8 * u, 8), pl.ds(0, 128)][:, 2 * k : 2 * k + 1], (8, 128)) for u in range(2)],
            axis=1,
        )
        pick = jnp.broadcast_to(w_all[0:8, 2 * k : 2 * k + 1], (8, COLS)) * pick
        for z in range(Z):
            pick = kp * pick
            acc[z] += pick
    sums = [jnp.sum(t, axis=0, keepdims=True) for t in acc]
    at_slots = jnp.concatenate([t[:, 0:128] + t[:, 128:256] for t in sums], axis=0) * (1.0 / PAIRS)
    empty = jnp.zeros((Z, 128), F32)
    fresh = rest + bounce
    for z in range(Z):
        fresh += jnp.broadcast_to(k0_ref[:, z : z + 1], (8, COLS)) * eq[z]
    fresh = fresh * (1.0 / PAIRS)
    for k in range(GROUP):
        for h in range(2):
            out[k, h, 8:16, :] = equil[:, h * 128 : h * 128 + 128]
            out[k, h, 16:24, :] = fresh[:, h * 128 : h * 128 + 128]
            out[k, h, 24:32, :] = empty if h else at_slots


def finish_kernel(
    flags, tab, l0_ref, back, hot_ref, rm_ref, cz_ref, ksel, nsel, chip, next_chip,
    out_hbm, en_hbm, eq, res, cell, grid_en, en_ref, sems, en_sem,
):
    up_x, on_chip = flags[0] > 0.0, flags[4] > 0.5
    for z in range(Z):
        for h in range(2):
            for b in range(2):
                got = back[pl.ds((16 * b + h) * BACK + 8 + z, 8, stride=2 * BACK), :]
                eq[pl.ds(z * ROWS + 8 * b, 8), pl.ds(h * 128, 128)] = got

    def leave(g, d):
        part = pl.ds(g * STEP, STEP)
        return pltpu.make_async_copy(res.at[d, part], out_hbm.at[d, part], sems.at[d, g])

    def run(d, pos_x, edge):
        first = 0 if pos_x else 8
        sub = lax.broadcasted_iota(jnp.int32, (8, 128), 0) == (0 if pos_x else 7)

        def some(g, carry):
            modes = [STEP * g + n for n in range(STEP)]
            eta, beta, kappa = [
                [jnp.broadcast_to(tab[n, pl.ds(m, 1), :], (8, 128)) for m in modes] for n in (ETA, BETA, KAPPA)
            ]
            for r in (0, 8):
                for h in range(2):
                    at = [(pl.ds(z * ROWS + r, 8), pl.ds(h * 128, 128)) for z in range(Z)]
                    e = [eq[to] for to in at]

                    def source(n, z):
                        s = eta[n] * e[z]
                        if r == first:
                            row = edge[h, pl.ds(z * 64 + d * 32 + modes[n], 1), :]
                            s += jnp.where(sub, beta[n] * jnp.broadcast_to(row, (8, 128)), 0.0)
                        return s

                    t = [None] * STEP
                    if d == 0:
                        rough = cz_ref[pl.ds(r, 8), pl.ds(h * 128, 128)] > 0.1
                        here = [pl.ds(pl.multiple_of(m * ROWS, ROWS) + r, 8) for m in modes]
                        kp = [ksel[h, to, :] for to in here]
                        far = [e[Z - 1]] * STEP
                        for z in reversed(range(Z - 1)):
                            far = [a * b + e[z] for a, b in zip(kp, far)]
                        for n, m in enumerate(modes):
                            far[n] = nsel[h, here[n], :] * far[n] + cell[h, pl.ds(r * MODES + m, 8, stride=MODES), :]
                            t[n] = jnp.where(rough, far[n], 0.9 * res[(1, m) + at[0]])
                    for z in range(Z) if d == 0 else range(Z - 1, -1, -1):
                        for n, m in enumerate(modes):
                            t[n] = source(n, z) if t[n] is None else kappa[n] * t[n] + source(n, z)
                            res[(d, m) + at[z]] = l0_ref[(d, m) + at[z]] + t[n]
            leave(g, d).start()
            return carry

        lax.fori_loop(0, MODES // STEP, some, 0)

    def all_modes(d):
        for pos_x in (True, False):
            for here, edge in ((True, chip), (False, next_chip)):
                pl.when((up_x == pos_x) & (on_chip == here))(lambda p=pos_x, e=edge: run(d, p, e))

    all_modes(1)
    hot = hot_ref[...]
    def tiles_of(half, h, at):
        return [back[pl.ds(((8 * half + t) * 2 + h) * BACK + at, 8), :] for t in range(8)]

    picked = [jnp.concatenate(tiles_of(half, h, 0), axis=1) for half in range(2) for h in range(2)]
    heard = jnp.concatenate(tiles_of(0, 0, 24), axis=1) + jnp.concatenate(tiles_of(1, 0, 24), axis=1)
    high, low = split(jnp.concatenate(picked + [heard, jnp.zeros((8, SLOTS), F32)], axis=0))
    mask = rm_ref[...].astype(jnp.bfloat16)
    dims = (((1,), (1,)), ((), ()))
    for part in range(4):
        got = 0.0
        for value in (high, low):
            lhs = jnp.concatenate([mask[r : r + 1, :] * value for r in range(4 * part, 4 * part + 4)], axis=0)
            got += lax.dot_general(lhs, hot, dims, preferred_element_type=F32)
        for n, r in enumerate(range(4 * part, 4 * part + 4)):
            for h in range(2):
                cell[h, pl.ds(r * MODES, MODES), :] = got[48 * n : 48 * n + 32, h * 128 : h * 128 + 128]
                grid_en[h, pl.ds(r * 8, 8), :] = got[48 * n + 32 : 48 * n + 40, h * 128 : h * 128 + 128] + back[pl.ds((2 * r + h) * BACK + 16, 8), :]
    for z in range(Z):
        for h in range(2):
            for b in range(2):
                en_ref[pl.ds(z * ROWS + 8 * b, 8), pl.ds(h * 128, 128)] = grid_en[h, pl.ds(8 * b * 8 + z, 8, stride=8), :]
    energy_copy = pltpu.make_async_copy(en_ref, en_hbm, en_sem)
    energy_copy.start()
    all_modes(0)
    energy_copy.wait()
    for g in range(MODES // STEP):
        for d in range(2):
            leave(g, d).wait()


def per_device(
    intensity, dir_cos, velocity, rate, spectrum, weight, heat, rough_cells, rough_count, rough_map
):
    smem = pl.BlockSpec(memory_space=pltpu.SMEM)
    vmem = pl.BlockSpec(memory_space=pltpu.VMEM)

    def hbm(x):
        return pltpu.with_memory_space_constraint(x, pltpu.HBM)

    anywhere = pl.BlockSpec(memory_space=pltpu.HBM)
    field = (2, MODES, PLANE, COLS)
    ones = [t.reshape(1, -1) for t in (velocity, rate, spectrum, weight, rough_cells)]
    tiles = hbm(intensity.reshape(512, 2, 8, COLS))
    x, edge, tab, flags = pl.pallas_call(
        edge_kernel,
        in_specs=[anywhere] * 6,
        out_specs=[vmem] * 3 + [smem],
        out_shape=[
            pltpu.VMEM(s, F32)
            for s in ((2, 512, 8, 128), (2, EDGE + 40, 128), (6, MODES, 128))
        ]
        + [pltpu.SMEM((5,), F32)],
        scratch_shapes=[
            pltpu.VMEM((3, DIRS), F32),
            pltpu.VMEM((1, MODES), F32),
            pltpu.VMEM((1, MODES), F32),
            pltpu.VMEM((1, MODES), F32),
            pltpu.VMEM((1, DIRS), F32),
            pltpu.VMEM((2, 64, 128), F32),
            pltpu.SemaphoreType.DMA((5,)),
            pltpu.SemaphoreType.DMA((2, 8)),
        ],
        compiler_params=pltpu.CompilerParams(vmem_limit_bytes=8 << 20),
        cost_estimate=pl.CostEstimate(flops=4 << 20, bytes_accessed=8 << 20, transcendentals=0),
        name="edges",
    )(tiles, hbm(dir_cos), *[hbm(t) for t in ones[:4]])
    count = lax.axis_size("space")
    on_chip = [(i, i ^ 1) for i in range(count)]
    across = [(i, i + 1 if i % 2 else i - 1) for i in range(1, count - 1)]
    edge_chip, edge_next = [lax.ppermute(edge, "space", p) for p in (on_chip, across)]

    base, energy, e0, d0 = pl.pallas_call(
        sweep_kernel,
        in_specs=[smem, vmem, anywhere, vmem, vmem],
        out_specs=[vmem] * 4,
        out_shape=[pltpu.VMEM(s, F32) for s in (field, (2, PLANE, 128), (2, PLANE, 128), (2, MODES * ROWS, 128))],
        scratch_shapes=[
            pltpu.VMEM((2, 512, 8, 128), F32),
            pltpu.VMEM((2, PLANE, 128), F32),
            pltpu.VMEM((2, PLANE, 128), F32),
            pltpu.SemaphoreType.DMA((2, 8)),
        ],
        compiler_params=pltpu.CompilerParams(vmem_limit_bytes=12 << 20),
        cost_estimate=pl.CostEstimate(flops=30 << 20, bytes_accessed=16 << 20, transcendentals=0),
        name="sweep",
    )(flags, tab, tiles, x, heat)

    tables = [
        ((COLS, SLOTS), jnp.bfloat16), ((ROWS, SLOTS), F32), ((3, MODES, 128), F32), ((GROUP, COLS), F32),
        ((Z, 128), F32), ((GROUP, 128), F32), ((ROWS, COLS), F32), ((2, MODES * ROWS, 128), F32),
        ((2, MODES * ROWS, 128), F32), ((MODES, SLOTS), F32), ((2, PLANE, 128), F32),
    ]
    hot, rm, par, jm, k0, mt, cz, ksel, nsel, at_slots, e0 = pl.pallas_call(
        slot_kernel,
        in_specs=[smem] * 2 + [vmem] * 10,
        out_specs=[vmem] * len(tables),
        out_shape=[pltpu.VMEM(*t) for t in tables],
        scratch_shapes=[pltpu.VMEM((2, MODES * ROWS, COLS), jnp.bfloat16)],
        compiler_params=pltpu.CompilerParams(vmem_limit_bytes=12 << 20),
        cost_estimate=pl.CostEstimate(flops=30 << 20, bytes_accessed=8 << 20, transcendentals=0),
        name="slots",
    )(rough_count, flags, dir_cos, *ones, rough_map.T, tab, d0, e0)

    pack = pl.pallas_call(
        pack_kernel,
        in_specs=[smem] + [vmem] * 9,
        out_specs=vmem,
        out_shape=pltpu.VMEM((GROUP, 2, SEND, 128), F32),
        compiler_params=pltpu.CompilerParams(vmem_limit_bytes=8 << 20),
        name="pack",
    )(flags, tab, energy, e0, at_slots, hot, rm, cz, edge_chip, edge_next)
    got = lax.all_to_all(pack, "mode", 0, 0, tiled=True)

    reply = pl.pallas_call(
        middle_kernel,
        in_specs=[vmem] * 5,
        out_specs=vmem,
        out_shape=pltpu.VMEM((GROUP, 2, BACK, 128), F32),
        scratch_shapes=[pltpu.VMEM((GROUP, MODES, COLS), F32)],
        compiler_params=pltpu.CompilerParams(vmem_limit_bytes=8 << 20),
        name="middle",
    )(got, par, jm, k0, mt)
    back = lax.all_to_all(reply, "mode", 0, 0, tiled=True).reshape(GROUP * 2 * BACK, 128)

    fresh, energy_new = pl.pallas_call(
        finish_kernel,
        in_specs=[smem] + [vmem] * 10,
        out_specs=[anywhere, anywhere],
        out_shape=[pltpu.HBM(field, F32), pltpu.HBM((PLANE, COLS), F32)],
        scratch_shapes=[
            pltpu.VMEM((PLANE, COLS), F32),
            pltpu.VMEM(field, F32),
            pltpu.VMEM((2, MODES * ROWS, 128), F32),
            pltpu.VMEM((2, PLANE, 128), F32),
            pltpu.VMEM((PLANE, COLS), F32),
            pltpu.SemaphoreType.DMA((2, MODES // STEP)),
            pltpu.SemaphoreType.DMA,
        ],
        compiler_params=pltpu.CompilerParams(vmem_limit_bytes=24 << 20),
        name="finish",
    )(flags, tab, base, back, hot, rm, cz, ksel, nsel, edge_chip, edge_next)
    return fresh.reshape(intensity.shape), energy_new.reshape(Z, ROWS, COLS)


def solution(mesh):
    in_specs = (
        P("mode", None, "space", None),
        P(),
        P(),
        P(),
        P(),
        P(),
        P("space", None),
        P("space"),
        P("space"),
        P("space", None),
    )
    out_specs = (P("mode", None, "space", None), P(None, "space", None))
    return jax.shard_map(
        per_device, mesh=mesh, in_specs=in_specs, out_specs=out_specs, check_vma=False
    )
```

```python
import jax
import jax.numpy as jnp
from jax import lax
from jax.experimental import pallas as pl
from jax.experimental.pallas import tpu as pltpu
from jax.sharding import PartitionSpec as P

PAIRS = 1024
DIRS = 32
MODES = 32
Z = 8
ROWS = 16
COLS = 256
GROUP = 16
PLANE = Z * ROWS
SEND = 24
BACK = 32
SLOTS = 1024
STEP = 4
F32 = jnp.float32


def column(row):
    r = lax.broadcasted_iota(jnp.int32, (MODES, MODES), 0)
    c = lax.broadcasted_iota(jnp.int32, (MODES, MODES), 1)
    return jnp.sum(jnp.where(r == c, jnp.broadcast_to(row, (MODES, MODES)), 0.0), axis=1, keepdims=True)


ALPHA, BETA, GAMMA, KAPPA, SHARE, ETA = range(6)
CHUNK = 8 * Z
EDGE = 512


def half_tiles(x_hbm, dst, sems, half, c, h):
    src = x_hbm.at[pl.ds(c * CHUNK, CHUNK), half, :, pl.ds(h * 128, 128)]
    return pltpu.make_async_copy(src, dst.at[h, pl.ds(c * CHUNK, CHUNK)], sems.at[h, c])


def edge_kernel(
    x_hbm, dc_h, v_h, r_h, s_h, w_h,
    x_ref, edge_ref, tab, flags,
    dcv, vel, rate, spec, wv, acc, sems, xsems,
):
    k = lax.axis_index("mode")
    odd_row = lax.axis_index("space") % 2 == 1
    few = list(zip((dc_h, v_h, r_h, s_h, w_h), (dcv, vel, rate, spec, wv)))
    few = [pltpu.make_async_copy(a, b, sems.at[n]) for n, (a, b) in enumerate(few)]
    for copy in few:
        copy.start()
    few[0].wait()
    lane = lax.broadcasted_iota(jnp.int32, (1, DIRS), 1)

    def pick(row, at):
        return jnp.sum(jnp.where(lane == at, row, 0.0))

    cx, cy, cz = [pick(dcv[n : n + 1, :], 2 * k) for n in range(3)]
    half = jnp.where(cx > 0.0, 1, 0)
    for c in range(8):
        for h in range(2):
            half_tiles(x_hbm, x_ref, xsems, half, c, h).start()
    for copy in few[1:]:
        copy.wait()
    cz = jnp.abs(cz)
    flags[0] = cx
    flags[1] = cy
    flags[2] = pick(wv[...], 2 * k)
    flags[3] = pick(wv[...], 2 * k + 1)
    flags[4] = jnp.where((cx > 0.0) == odd_row, 1.0, 0.0)
    v, a = column(vel[...]), 1.0 + column(rate[...])
    share, eta = column(spec[...]), column(rate[...]) * column(spec[...])
    inv = 1.0 / (a + v * cz)
    table = {
        ALPHA: (1.0 - v * jnp.abs(cx) - v * jnp.abs(cy)) * inv,
        BETA: v * jnp.abs(cx) * inv,
        GAMMA: v * jnp.abs(cy) * inv,
        KAPPA: v * cz * inv,
        SHARE: share,
        ETA: eta * inv,
    }
    for n, col in table.items():
        tab[n] = jnp.broadcast_to(col, (MODES, 128))
    acc[...] = jnp.zeros_like(acc)

    row = jnp.where(cx > 0.0, 7, 0)
    flat = x_ref.reshape(2, 512 * 8, 128)

    def one(c, carry):
        w = flags[2 + c // 4]
        base = pl.multiple_of(c * CHUNK * 8, CHUNK * 8)
        m0 = pl.multiple_of(8 * (c % 4), 8)
        for h in range(2):
            half_tiles(x_hbm, x_ref, xsems, half, c, h).wait()
            kp, bt = [tab[n, pl.ds(m0, 8), :] for n in (KAPPA, BETA)]
            rows = []
            for z in range(Z):
                e = flat[h, pl.ds(base + z * 8 + row, 8, stride=8 * Z), :]
                edge_ref[h, pl.ds(pl.multiple_of(z * 64 + 8 * c, 8), 8), :] = e
                rows.append(bt * e)

            @pl.when(c < 4)
            def _():
                t = rows[0]
                acc[h, pl.ds(0, 8), :] += w * t
                for z in range(1, Z):
                    t = kp * t + rows[z]
                    acc[h, pl.ds(8 * z, 8), :] += w * t

            @pl.when(c >= 4)
            def _():
                t = rows[Z - 1]
                acc[h, pl.ds(8 * (Z - 1), 8), :] += w * t
                for z in reversed(range(Z - 1)):
                    t = kp * t + rows[z]
                    acc[h, pl.ds(8 * z, 8), :] += w * t
                edge_ref[h, pl.ds(EDGE + 8 + m0, 8), :] = t

        return carry

    lax.fori_loop(0, 8, one, 0)
    for h in range(2):
        for z in range(Z):
            edge_ref[h, pl.ds(EDGE + z, 1), :] = jnp.sum(acc[h, pl.ds(8 * z, 8), :], axis=0, keepdims=True)


def total(values):
    while len(values) > 1:
        values = [a + b for a, b in zip(values[::2], values[1::2])]
    return values[0]


def sweep_kernel(
    flags, tab, x_hbm, far_ref, heat, l0_ref, e_ref, e0_ref, d0, near_ref, accd, accu, rawd, rawu, xsems,
):
    up_x, up_y = flags[0] > 0.0, flags[1] > 0.0
    half = jnp.where(up_x, 0, 1)
    for g in range(4):
        for c in (4 + g, g):
            for h in range(2):
                half_tiles(x_hbm, near_ref, xsems, half, c, h).start()
    accd[...] = jnp.zeros_like(accd)
    accu[...] = jnp.zeros_like(accu)
    rawd[...] = jnp.zeros_like(rawd)
    rawu[...] = jnp.zeros_like(rawu)

    def run(pos_x, pos_y):
        rows = (0, 8) if pos_x else (8, 0)
        cols = (0, 1) if pos_y else (1, 0)
        tiles = [(r, c) for r in rows for c in cols]
        sub = lax.broadcasted_iota(jnp.int32, (8, 128), 0) == (0 if pos_x else 7)
        lane = lax.broadcasted_iota(jnp.int32, (8, 128), 1) == (0 if pos_y else 127)

        def some(i, carry):
            modes = [STEP * i + n for n in range(STEP)]
            coef = [[jnp.broadcast_to(tab[n, pl.ds(m, 1), :], (8, 128)) for n in range(4)] for m in modes]

            def rhs(d, t, z):
                alpha, beta, gamma, _ = coef[t]
                at = (d * MODES + modes[t]) * Z + z
                f = [[ref[c, at] for c in cols] for ref in (near_ref, far_ref)]
                rx = [[pltpu.roll(v, 1 if pos_x else 7, 0) for v in vs] for vs in f]
                ry = [[pltpu.roll(v, 1 if pos_y else 127, 1) for v in vs] for vs in f]
                out = []
                for r in range(2):
                    for c in range(2):
                        x = jnp.where(sub, 0.0 if r == 0 else rx[0][c], rx[r][c])
                        y = jnp.where(lane, 0.0 if c == 0 else ry[r][0], ry[r][c])
                        out.append(alpha * f[r][c] + beta * x + gamma * y)
                return out, f[0] + f[1]

            for d, acc, raw, order in ((1, accd, rawd, range(Z - 1, -1, -1)), (0, accu, rawu, range(Z))):
                if d == 1:
                    state = [
                        [jnp.broadcast_to(tab[4, pl.ds(m, 1), :], (8, 128)) * heat[pl.ds(r, 8), pl.ds(c * 128, 128)] for r, c in tiles]
                        for m in modes
                    ]
                else:
                    state = [None] * STEP
                for z in order:
                    sums = []
                    for t in range(STEP):
                        f, taken = rhs(d, t, z)
                        sums.append(taken)
                        state[t] = f if state[t] is None else [a + coef[t][3] * b for a, b in zip(f, state[t])]
                        for v, (r, c) in zip(state[t], tiles):
                            l0_ref[d, modes[t], pl.ds(z * ROWS + r, 8), pl.ds(c * 128, 128)] = v
                    for n, (r, c) in enumerate(tiles):
                        acc[c, pl.ds(z * ROWS + r, 8), :] += total([t[n] for t in state])
                        raw[c, pl.ds(z * ROWS + r, 8), :] += total([t[n] for t in sums])
                if d == 1:
                    for t in range(STEP):
                        for v, (r, c) in zip(state[t], tiles):
                            d0[c, pl.ds(pl.multiple_of(modes[t] * ROWS, ROWS) + r, 8), :] = v
            return carry

        def eight(g, carry):
            for c in (4 + g, g):
                for h in range(2):
                    half_tiles(x_hbm, near_ref, xsems, half, c, h).wait()
            return lax.fori_loop(2 * g, 2 * g + 2, some, carry)

        lax.fori_loop(0, 4, eight, 0)

    for pos_x in (True, False):
        for pos_y in (True, False):
            pl.when((up_x == pos_x) & (up_y == pos_y))(lambda px=pos_x, py=pos_y: run(px, py))

    e0_ref[...] = flags[3] * accd[...] + flags[2] * accu[...]
    e_ref[...] = flags[3] * rawd[...] + flags[2] * rawu[...]


def split(x):
    high = x.astype(jnp.bfloat16)
    return high, (x - high.astype(F32)).astype(jnp.bfloat16)


def spread(x, hot):
    high, low = split(x)
    dims = (((1,), (1,)), ((), ()))
    return lax.dot_general(high, hot, dims, preferred_element_type=F32) + lax.dot_general(
        low, hot, dims, preferred_element_type=F32
    )


def slot_kernel(
    cnt, flags, dcv, vel, rate, spec, wv, cells, rmap, tab, d0, e0_in,
    hot_ref, rm_ref, par, jm_ref, k0_ref, mt_ref, cz_ref, ksel, nsel, slot_ref, e0_ref, parts,
):
    k = lax.axis_index("mode")
    live = lax.broadcasted_iota(jnp.int32, (1, SLOTS), 1) < cnt[0]
    q = lax.broadcasted_iota(jnp.int32, (COLS, SLOTS), 0)
    hot_ref[...] = jnp.where(q == jnp.where(live, cells[...] & (COLS - 1), -1), 1.0, 0.0).astype(jnp.bfloat16)
    hot = hot_ref[...]
    cell_row = jnp.where(live, cells[...] >> 8, -1)
    rows = lax.broadcasted_iota(jnp.int32, (ROWS, SLOTS), 0)
    rm = jnp.where(rows == cell_row, 1.0, 0.0)
    rm_ref[...] = rm
    idx = jnp.where(cell_row == k, (rmap[...] + 1).astype(F32), 0.0).astype(jnp.bfloat16)
    jm_ref[...] = lax.dot_general(idx, hot, (((1,), (1,)), ((), ())), preferred_element_type=F32)
    mt_ref[...] = rmap[:, pl.ds(pl.multiple_of(128 * (k % 8), 128), 128)].astype(F32)
    mine = jnp.sum(jnp.where(rows == k, rmap[...], 0), axis=0, keepdims=True)
    czr = jnp.zeros((1, SLOTS), F32)
    for j in range(GROUP):
        czr = jnp.where(mine == j, jnp.abs(dcv[2:3, 2 * j : 2 * j + 1]), czr)
    cz_ref[...] = spread(rm * czr, hot)

    v, a = column(vel[...]), 1.0 + column(rate[...])
    eta = column(rate[...]) * column(spec[...])
    c_all = v * jnp.abs(dcv[2:3, :])
    inv_all = 1.0 / (a + c_all)
    k_all = c_all * inv_all
    for n, block in enumerate((k_all, eta * inv_all, jnp.broadcast_to(wv[...], (MODES, DIRS)))):
        par[n, :, pl.ds(0, DIRS)] = block
    term = eta * inv_all * wv[...]
    odd = lax.broadcasted_iota(jnp.int32, (MODES, DIRS), 1) % 2 == 1
    zr = lax.broadcasted_iota(jnp.int32, (Z, 128), 0)
    zc = lax.broadcasted_iota(jnp.int32, (Z, 128), 1)
    total = jnp.zeros((Z, 128), F32)
    for n in range(Z):
        down = jnp.sum(jnp.sum(jnp.where(odd, term, 0.0), axis=1, keepdims=True), axis=0, keepdims=True)
        up = jnp.sum(jnp.sum(jnp.where(odd, 0.0, term), axis=1, keepdims=True), axis=0, keepdims=True)
        total += jnp.where(zc - zr == n, down, 0.0) + jnp.where(zr - zc == n, up, 0.0)
        term = term * k_all
    k0_ref[...] = total

    vb, ab, nb = [jnp.broadcast_to(t, (MODES, 128)) for t in (v, a, 0.9 * eta)]
    for h in range(2):
        for r in (0, 8):
            cz = cz_ref[pl.ds(r, 8), pl.ds(h * 128, 128)]
            gain = jnp.where(cz < 0.1, 0.9 * flags[2], 0.0)
            acc = [jnp.zeros((8, 128), F32) for _ in range(Z)]
            for m in range(MODES):
                at = pl.ds(m * ROWS + r, 8)
                c = vb[m : m + 1, :] * cz
                inv = 1.0 / (ab[m : m + 1, :] + c)
                ksel[h, at, :] = c * inv
                nsel[h, at, :] = nb[m : m + 1, :] * inv
                f = gain * d0[h, at, :]
                kp = jnp.broadcast_to(tab[KAPPA, pl.ds(m, 1), :], (8, 128))
                for z in range(Z):
                    f = kp * f
                    acc[z] += f
            for z in range(Z):
                at = pl.ds(z * ROWS + r, 8)
                e0_ref[h, at, :] = e0_in[h, at, :] + acc[z]

    for r in range(ROWS):
        for t in range(2):
            x = jnp.concatenate(
                [
                    jnp.concatenate([d0[h, pl.ds((2 * t + u) * PLANE + r, 8, stride=ROWS), :] for h in range(2)], axis=1)
                    for u in range(2)
                ],
                axis=0,
            )
            parts[pl.ds(r * MODES + 16 * t, 16), :] = x.astype(jnp.bfloat16)
    for n in range(SLOTS // 256):
        at = pl.ds(n * 256, 256)
        got = jnp.dot(parts[...], hot_ref[:, at], preferred_element_type=F32)
        mine = rm[0:1, n * 256 : n * 256 + 256] * got[0:MODES]
        for r in range(1, ROWS):
            mine += rm[r : r + 1, n * 256 : n * 256 + 256] * got[r * MODES : (r + 1) * MODES]
        slot_ref[:, at] = mine


def pack_kernel(flags, tab, e_ref, e0_ref, slot_ref, hot, rm, cz_ref, chip, next_chip, out):
    up_x = flags[0] > 0.0
    delta = [jnp.where(flags[4] > 0.5, chip[h, pl.ds(EDGE, 40), :], next_chip[h, pl.ds(EDGE, 40), :]) for h in range(2)]
    extra = []
    for h in range(2):
        at = slice(h * 128, h * 128 + 128)
        cz = jnp.where(up_x, cz_ref[0:1, at], cz_ref[ROWS - 1 : ROWS, at])
        gain = jnp.broadcast_to(jnp.where(cz < 0.1, 0.9 * flags[2], 0.0), (8, 128))
        acc = [jnp.zeros((8, 128), F32) for _ in range(Z)]
        for t in range(MODES // 8):
            f = gain * delta[h][8 + 8 * t : 16 + 8 * t, :]
            for z in range(Z):
                f = tab[KAPPA, pl.ds(8 * t, 8), :] * f
                acc[z] += f
        extra.append(delta[h][0:8, :] + jnp.concatenate([jnp.sum(t, axis=0, keepdims=True) for t in acc], axis=0))
    high, low = split(jnp.concatenate([d[8:40, :] for d in delta], axis=1))
    more = jnp.dot(jnp.concatenate([high, low], axis=0), hot[...], preferred_element_type=F32)
    mask = jnp.where(up_x, rm[0:1, :], rm[ROWS - 1 : ROWS, :])
    slots = slot_ref[...] + mask * (more[0:MODES, :] + more[MODES : 2 * MODES, :])
    for r in range(ROWS):
        tile, low_mode = (r % 8) * 128, 16 * (r // 8)
        for h in range(2):
            part = e0_ref[h, pl.ds(r, 8, stride=ROWS), :]
            if r == 0:
                part += jnp.where(up_x, extra[h], 0.0)
            if r == ROWS - 1:
                part += jnp.where(up_x, 0.0, extra[h])
            out[r, h, 0:8, :] = e_ref[h, pl.ds(r, 8, stride=ROWS), :]
            out[r, h, 8:16, :] = part
            out[r, h, 16:24, :] = slots[low_mode + 8 * h : low_mode + 8 * h + 8, tile : tile + 128]


def middle_kernel(got, par, jm_ref, k0_ref, mt_ref, out, q_ref):
    def take(s, at):
        return jnp.concatenate([got[s, h, at : at + 8, :] for h in range(2)], axis=1)

    energy = take(0, 0)
    rest = take(0, 8)
    for s in range(1, GROUP):
        energy += take(s, 0)
        rest += take(s, 8)
    energy = energy * (1.0 / PAIRS)
    equil = energy / (1.0 + 0.3 * jnp.abs(energy))
    eq = [jnp.broadcast_to(equil[z : z + 1, :], (8, COLS)) for z in range(Z)]
    k_all, n_all, w_all = par[0], par[1], par[2]
    for j in range(GROUP):
        for t in range(MODES // 8):
            at = slice(8 * t, 8 * t + 8)
            kp = jnp.broadcast_to(k_all[at, 2 * j + 1 : 2 * j + 2], (8, COLS))
            eta = jnp.broadcast_to(n_all[at, 2 * j + 1 : 2 * j + 2], (8, COLS))
            s = eq[Z - 1]
            for z in reversed(range(Z - 1)):
                s = kp * s + eq[z]
            q_ref[j, at, :] = (0.9 * eta) * s
    acc = [jnp.zeros((8, COLS), F32) for _ in range(Z)]
    for k in range(GROUP):
        jm = jnp.broadcast_to(jm_ref[k : k + 1, :], (8, COLS))
        jm = jnp.where(jm < 0.5, float(k + 1), jm)
        w = jnp.broadcast_to(w_all[0:8, 2 * k : 2 * k + 1], (8, COLS))
        for t in range(MODES // 8):
            at = slice(8 * t, 8 * t + 8)
            pick = q_ref[0, at, :]
            for j in range(1, GROUP):
                pick = jnp.where(jm > j + 0.5, q_ref[j, at, :], pick)
            kp = jnp.broadcast_to(k_all[at, 2 * k : 2 * k + 1], (8, COLS))
            pick = w * pick
            for z in range(Z):
                pick = kp * pick
                acc[z] += pick
    bounce = jnp.concatenate([jnp.sum(t, axis=0, keepdims=True) for t in acc], axis=0)
    first = pl.multiple_of(16 * (lax.axis_index("mode") // 8), 16)
    acc = [jnp.zeros((8, COLS), F32) for _ in range(Z)]
    for k in range(GROUP):
        index = jnp.concatenate([jnp.broadcast_to(mt_ref[k : k + 1, :], (8, 128))] * 2, axis=1)
        pick = take(0, 16)
        for j in range(1, GROUP):
            pick = jnp.where(index > j - 0.5, take(j, 16), pick)
        pick = 0.9 * pick
        for h in range(2):
            out[k, h, 0:8, :] = pick[:, h * 128 : h * 128 + 128]
        kp = jnp.concatenate(
            [jnp.broadcast_to(par[0, pl.ds(first + 8 * u, 8), pl.ds(0, 128)][:, 2 * k : 2 * k + 1], (8, 128)) for u in range(2)],
            axis=1,
        )
        pick = jnp.broadcast_to(w_all[0:8, 2 * k : 2 * k + 1], (8, COLS)) * pick
        for z in range(Z):
            pick = kp * pick
            acc[z] += pick
    sums = [jnp.sum(t, axis=0, keepdims=True) for t in acc]
    at_slots = jnp.concatenate([t[:, 0:128] + t[:, 128:256] for t in sums], axis=0) * (1.0 / PAIRS)
    empty = jnp.zeros((Z, 128), F32)
    fresh = rest + bounce
    for z in range(Z):
        fresh += jnp.broadcast_to(k0_ref[:, z : z + 1], (8, COLS)) * eq[z]
    fresh = fresh * (1.0 / PAIRS)
    for k in range(GROUP):
        for h in range(2):
            out[k, h, 8:16, :] = equil[:, h * 128 : h * 128 + 128]
            out[k, h, 16:24, :] = fresh[:, h * 128 : h * 128 + 128]
            out[k, h, 24:32, :] = empty if h else at_slots


def finish_kernel(
    flags, tab, l0_ref, back, hot_ref, rm_ref, cz_ref, ksel, nsel, chip, next_chip,
    out_hbm, en_hbm, eq, res, cell, grid_en, en_ref, sems, en_sem,
):
    up_x, on_chip = flags[0] > 0.0, flags[4] > 0.5
    for z in range(Z):
        for h in range(2):
            for b in range(2):
                got = back[pl.ds((16 * b + h) * BACK + 8 + z, 8, stride=2 * BACK), :]
                eq[pl.ds(z * ROWS + 8 * b, 8), pl.ds(h * 128, 128)] = got

    def leave(g, d):
        part = pl.ds(g * STEP, STEP)
        return pltpu.make_async_copy(res.at[d, part], out_hbm.at[d, part], sems.at[d, g])

    def run(d, pos_x, edge):
        first = 0 if pos_x else 8
        sub = lax.broadcasted_iota(jnp.int32, (8, 128), 0) == (0 if pos_x else 7)

        def some(g, carry):
            modes = [STEP * g + n for n in range(STEP)]
            eta, beta, kappa = [
                [jnp.broadcast_to(tab[n, pl.ds(m, 1), :], (8, 128)) for m in modes] for n in (ETA, BETA, KAPPA)
            ]
            for r in (0, 8):
                for h in range(2):
                    at = [(pl.ds(z * ROWS + r, 8), pl.ds(h * 128, 128)) for z in range(Z)]
                    e = [eq[to] for to in at]

                    def source(n, z):
                        s = eta[n] * e[z]
                        if r == first:
                            row = edge[h, pl.ds(z * 64 + d * 32 + modes[n], 1), :]
                            s += jnp.where(sub, beta[n] * jnp.broadcast_to(row, (8, 128)), 0.0)
                        return s

                    t = [None] * STEP
                    if d == 0:
                        rough = cz_ref[pl.ds(r, 8), pl.ds(h * 128, 128)] > 0.1
                        here = [pl.ds(pl.multiple_of(m * ROWS, ROWS) + r, 8) for m in modes]
                        kp = [ksel[h, to, :] for to in here]
                        far = [e[Z - 1]] * STEP
                        for z in reversed(range(Z - 1)):
                            far = [a * b + e[z] for a, b in zip(kp, far)]
                        for n, m in enumerate(modes):
                            far[n] = nsel[h, here[n], :] * far[n] + cell[h, pl.ds(r * MODES + m, 8, stride=MODES), :]
                            t[n] = jnp.where(rough, far[n], 0.9 * res[(1, m) + at[0]])
                    for z in range(Z) if d == 0 else range(Z - 1, -1, -1):
                        for n, m in enumerate(modes):
                            t[n] = source(n, z) if t[n] is None else kappa[n] * t[n] + source(n, z)
                            res[(d, m) + at[z]] = l0_ref[(d, m) + at[z]] + t[n]
            leave(g, d).start()
            return carry

        lax.fori_loop(0, MODES // STEP, some, 0)

    def all_modes(d):
        for pos_x in (True, False):
            for here, edge in ((True, chip), (False, next_chip)):
                pl.when((up_x == pos_x) & (on_chip == here))(lambda p=pos_x, e=edge: run(d, p, e))

    all_modes(1)
    hot = hot_ref[...]
    def tiles_of(half, h, at):
        return [back[pl.ds(((8 * half + t) * 2 + h) * BACK + at, 8), :] for t in range(8)]

    picked = [jnp.concatenate(tiles_of(half, h, 0), axis=1) for half in range(2) for h in range(2)]
    heard = jnp.concatenate(tiles_of(0, 0, 24), axis=1) + jnp.concatenate(tiles_of(1, 0, 24), axis=1)
    heard_high = heard.astype(jnp.bfloat16).astype(F32)
    value = jnp.concatenate(picked + [heard_high, heard - heard_high], axis=0).astype(jnp.bfloat16)
    mask = rm_ref[...].astype(jnp.bfloat16)
    dims = (((1,), (1,)), ((), ()))
    for part in range(4):
        lhs = jnp.concatenate([mask[r : r + 1, :] * value for r in range(4 * part, 4 * part + 4)], axis=0)
        got = lax.dot_general(lhs, hot, dims, preferred_element_type=F32)
        for n, r in enumerate(range(4 * part, 4 * part + 4)):
            for h in range(2):
                cell[h, pl.ds(r * MODES, MODES), :] = got[48 * n : 48 * n + 32, h * 128 : h * 128 + 128]
                both = got[48 * n + 32 : 48 * n + 40, h * 128 : h * 128 + 128] + got[48 * n + 40 : 48 * n + 48, h * 128 : h * 128 + 128]
                grid_en[h, pl.ds(r * 8, 8), :] = both + back[pl.ds((2 * r + h) * BACK + 16, 8), :]
    for z in range(Z):
        for h in range(2):
            for b in range(2):
                en_ref[pl.ds(z * ROWS + 8 * b, 8), pl.ds(h * 128, 128)] = grid_en[h, pl.ds(8 * b * 8 + z, 8, stride=8), :]
    energy_copy = pltpu.make_async_copy(en_ref, en_hbm, en_sem)
    energy_copy.start()
    all_modes(0)
    energy_copy.wait()
    for g in range(MODES // STEP):
        for d in range(2):
            leave(g, d).wait()


def per_device(
    intensity, dir_cos, velocity, rate, spectrum, weight, heat, rough_cells, rough_count, rough_map
):
    smem = pl.BlockSpec(memory_space=pltpu.SMEM)
    vmem = pl.BlockSpec(memory_space=pltpu.VMEM)

    def hbm(x):
        return pltpu.with_memory_space_constraint(x, pltpu.HBM)

    anywhere = pl.BlockSpec(memory_space=pltpu.HBM)
    field = (2, MODES, PLANE, COLS)
    ones = [t.reshape(1, -1) for t in (velocity, rate, spectrum, weight, rough_cells)]
    tiles = hbm(intensity.reshape(512, 2, 8, COLS))
    x, edge, tab, flags = pl.pallas_call(
        edge_kernel,
        in_specs=[anywhere] * 6,
        out_specs=[vmem] * 3 + [smem],
        out_shape=[
            pltpu.VMEM(s, F32)
            for s in ((2, 512, 8, 128), (2, EDGE + 40, 128), (6, MODES, 128))
        ]
        + [pltpu.SMEM((5,), F32)],
        scratch_shapes=[
            pltpu.VMEM((3, DIRS), F32),
            pltpu.VMEM((1, MODES), F32),
            pltpu.VMEM((1, MODES), F32),
            pltpu.VMEM((1, MODES), F32),
            pltpu.VMEM((1, DIRS), F32),
            pltpu.VMEM((2, 64, 128), F32),
            pltpu.SemaphoreType.DMA((5,)),
            pltpu.SemaphoreType.DMA((2, 8)),
        ],
        compiler_params=pltpu.CompilerParams(vmem_limit_bytes=8 << 20),
        cost_estimate=pl.CostEstimate(flops=4 << 20, bytes_accessed=8 << 20, transcendentals=0),
        name="edges",
    )(tiles, hbm(dir_cos), *[hbm(t) for t in ones[:4]])
    count = lax.axis_size("space")
    on_chip = [(i, i ^ 1) for i in range(count)]
    across = [(i, i + 1 if i % 2 else i - 1) for i in range(1, count - 1)]
    edge_chip, edge_next = [lax.ppermute(edge, "space", p) for p in (on_chip, across)]

    base, energy, e0, d0 = pl.pallas_call(
        sweep_kernel,
        in_specs=[smem, vmem, anywhere, vmem, vmem],
        out_specs=[vmem] * 4,
        out_shape=[pltpu.VMEM(s, F32) for s in (field, (2, PLANE, 128), (2, PLANE, 128), (2, MODES * ROWS, 128))],
        scratch_shapes=[
            pltpu.VMEM((2, 512, 8, 128), F32),
            pltpu.VMEM((2, PLANE, 128), F32),
            pltpu.VMEM((2, PLANE, 128), F32),
            pltpu.VMEM((2, PLANE, 128), F32),
            pltpu.VMEM((2, PLANE, 128), F32),
            pltpu.SemaphoreType.DMA((2, 8)),
        ],
        compiler_params=pltpu.CompilerParams(vmem_limit_bytes=12 << 20),
        cost_estimate=pl.CostEstimate(flops=30 << 20, bytes_accessed=16 << 20, transcendentals=0),
        name="sweep",
    )(flags, tab, tiles, x, heat)

    tables = [
        ((COLS, SLOTS), jnp.bfloat16), ((ROWS, SLOTS), F32), ((3, MODES, 128), F32), ((GROUP, COLS), F32),
        ((Z, 128), F32), ((GROUP, 128), F32), ((ROWS, COLS), F32), ((2, MODES * ROWS, 128), F32),
        ((2, MODES * ROWS, 128), F32), ((MODES, SLOTS), F32), ((2, PLANE, 128), F32),
    ]
    hot, rm, par, jm, k0, mt, cz, ksel, nsel, at_slots, e0 = pl.pallas_call(
        slot_kernel,
        in_specs=[smem] * 2 + [vmem] * 10,
        out_specs=[vmem] * len(tables),
        out_shape=[pltpu.VMEM(*t) for t in tables],
        scratch_shapes=[pltpu.VMEM((MODES * ROWS, COLS), jnp.bfloat16)],
        compiler_params=pltpu.CompilerParams(vmem_limit_bytes=12 << 20),
        cost_estimate=pl.CostEstimate(flops=30 << 20, bytes_accessed=8 << 20, transcendentals=0),
        name="slots",
    )(rough_count, flags, dir_cos, *ones, rough_map.T, tab, d0, e0)

    pack = pl.pallas_call(
        pack_kernel,
        in_specs=[smem] + [vmem] * 9,
        out_specs=vmem,
        out_shape=pltpu.VMEM((GROUP, 2, SEND, 128), F32),
        compiler_params=pltpu.CompilerParams(vmem_limit_bytes=8 << 20),
        name="pack",
    )(flags, tab, energy, e0, at_slots, hot, rm, cz, edge_chip, edge_next)
    got = lax.all_to_all(pack, "mode", 0, 0, tiled=True)

    reply = pl.pallas_call(
        middle_kernel,
        in_specs=[vmem] * 5,
        out_specs=vmem,
        out_shape=pltpu.VMEM((GROUP, 2, BACK, 128), F32),
        scratch_shapes=[pltpu.VMEM((GROUP, MODES, COLS), F32)],
        compiler_params=pltpu.CompilerParams(vmem_limit_bytes=8 << 20),
        name="middle",
    )(got, par, jm, k0, mt)
    back = lax.all_to_all(reply, "mode", 0, 0, tiled=True).reshape(GROUP * 2 * BACK, 128)

    fresh, energy_new = pl.pallas_call(
        finish_kernel,
        in_specs=[smem] + [vmem] * 10,
        out_specs=[anywhere, anywhere],
        out_shape=[pltpu.HBM(field, F32), pltpu.HBM((PLANE, COLS), F32)],
        scratch_shapes=[
            pltpu.VMEM((PLANE, COLS), F32),
            pltpu.VMEM(field, F32),
            pltpu.VMEM((2, MODES * ROWS, 128), F32),
            pltpu.VMEM((2, PLANE, 128), F32),
            pltpu.VMEM((PLANE, COLS), F32),
            pltpu.SemaphoreType.DMA((2, MODES // STEP)),
            pltpu.SemaphoreType.DMA,
        ],
        compiler_params=pltpu.CompilerParams(vmem_limit_bytes=24 << 20),
        name="finish",
    )(flags, tab, base, back, hot, rm, cz, ksel, nsel, edge_chip, edge_next)
    return fresh.reshape(intensity.shape), energy_new.reshape(Z, ROWS, COLS)


def solution(mesh):
    in_specs = (
        P("mode", None, "space", None),
        P(),
        P(),
        P(),
        P(),
        P(),
        P("space", None),
        P("space"),
        P("space"),
        P("space", None),
    )
    out_specs = (P("mode", None, "space", None), P(None, "space", None))
    return jax.shard_map(
        per_device, mesh=mesh, in_specs=in_specs, out_specs=out_specs, check_vma=False
    )
```

```python
import jax
import jax.numpy as jnp
from jax import lax
from jax.experimental import pallas as pl
from jax.experimental.pallas import tpu as pltpu
from jax.sharding import PartitionSpec as P

PAIRS = 1024
DIRS = 32
MODES = 32
Z = 8
ROWS = 16
COLS = 256
GROUP = 16
PLANE = Z * ROWS
SEND = 24
BACK = 7
SLOTS = 1024
STEP = 4
F32 = jnp.float32


def column(row):
    r = lax.broadcasted_iota(jnp.int32, (MODES, MODES), 0)
    c = lax.broadcasted_iota(jnp.int32, (MODES, MODES), 1)
    return jnp.sum(jnp.where(r == c, jnp.broadcast_to(row, (MODES, MODES)), 0.0), axis=1, keepdims=True)


ALPHA, BETA, GAMMA, KAPPA, SHARE, ETA = range(6)
CHUNK = 8 * Z
EDGE = 512


def half_tiles(x_hbm, dst, sems, half, c, h):
    src = x_hbm.at[pl.ds(c * CHUNK, CHUNK), half, :, pl.ds(h * 128, 128)]
    return pltpu.make_async_copy(src, dst.at[h, pl.ds(c * CHUNK, CHUNK)], sems.at[h, c])


def edge_kernel(
    x_hbm, dc_h, v_h, r_h, s_h, w_h,
    x_ref, edge_ref, tab, flags,
    dcv, vel, rate, spec, wv, acc, sems, xsems,
):
    k = lax.axis_index("mode")
    odd_row = lax.axis_index("space") % 2 == 1
    few = list(zip((dc_h, v_h, r_h, s_h, w_h), (dcv, vel, rate, spec, wv)))
    few = [pltpu.make_async_copy(a, b, sems.at[n]) for n, (a, b) in enumerate(few)]
    for copy in few:
        copy.start()
    few[0].wait()
    lane = lax.broadcasted_iota(jnp.int32, (1, DIRS), 1)

    def pick(row, at):
        return jnp.sum(jnp.where(lane == at, row, 0.0))

    cx, cy, cz = [pick(dcv[n : n + 1, :], 2 * k) for n in range(3)]
    half = jnp.where(cx > 0.0, 1, 0)
    for c in range(8):
        for h in range(2):
            half_tiles(x_hbm, x_ref, xsems, half, c, h).start()
    for copy in few[1:]:
        copy.wait()
    cz = jnp.abs(cz)
    flags[0] = cx
    flags[1] = cy
    flags[2] = pick(wv[...], 2 * k)
    flags[3] = pick(wv[...], 2 * k + 1)
    flags[4] = jnp.where((cx > 0.0) == odd_row, 1.0, 0.0)
    v, a = column(vel[...]), 1.0 + column(rate[...])
    share, eta = column(spec[...]), column(rate[...]) * column(spec[...])
    inv = 1.0 / (a + v * cz)
    table = {
        ALPHA: (1.0 - v * jnp.abs(cx) - v * jnp.abs(cy)) * inv,
        BETA: v * jnp.abs(cx) * inv,
        GAMMA: v * jnp.abs(cy) * inv,
        KAPPA: v * cz * inv,
        SHARE: share,
        ETA: eta * inv,
    }
    for n, col in table.items():
        tab[n] = jnp.broadcast_to(col, (MODES, 128))
    acc[...] = jnp.zeros_like(acc)

    row = jnp.where(cx > 0.0, 7, 0)
    flat = x_ref.reshape(2, 512 * 8, 128)

    def one(c, carry):
        w = flags[2 + c // 4]
        base = pl.multiple_of(c * CHUNK * 8, CHUNK * 8)
        m0 = pl.multiple_of(8 * (c % 4), 8)
        for h in range(2):
            half_tiles(x_hbm, x_ref, xsems, half, c, h).wait()
            kp, bt = [tab[n, pl.ds(m0, 8), :] for n in (KAPPA, BETA)]
            rows = []
            for z in range(Z):
                e = flat[h, pl.ds(base + z * 8 + row, 8, stride=8 * Z), :]
                edge_ref[h, pl.ds(pl.multiple_of(z * 64 + 8 * c, 8), 8), :] = e
                rows.append(bt * e)

            @pl.when(c < 4)
            def _():
                t = rows[0]
                acc[h, pl.ds(0, 8), :] += w * t
                for z in range(1, Z):
                    t = kp * t + rows[z]
                    acc[h, pl.ds(8 * z, 8), :] += w * t

            @pl.when(c >= 4)
            def _():
                t = rows[Z - 1]
                acc[h, pl.ds(8 * (Z - 1), 8), :] += w * t
                for z in reversed(range(Z - 1)):
                    t = kp * t + rows[z]
                    acc[h, pl.ds(8 * z, 8), :] += w * t
                edge_ref[h, pl.ds(EDGE + 8 + m0, 8), :] = t

        return carry

    lax.fori_loop(0, 8, one, 0)
    for h in range(2):
        for z in range(Z):
            edge_ref[h, pl.ds(EDGE + z, 1), :] = jnp.sum(acc[h, pl.ds(8 * z, 8), :], axis=0, keepdims=True)


def total(values):
    while len(values) > 1:
        values = [a + b for a, b in zip(values[::2], values[1::2])]
    return values[0]


def sweep_kernel(
    flags, tab, x_hbm, far_ref, heat, l0_ref, e_ref, e0_ref, d0, near_ref, accd, accu, rawd, rawu, xsems,
):
    up_x, up_y = flags[0] > 0.0, flags[1] > 0.0
    half = jnp.where(up_x, 0, 1)
    for g in range(4):
        for c in (4 + g, g):
            for h in range(2):
                half_tiles(x_hbm, near_ref, xsems, half, c, h).start()
    accd[...] = jnp.zeros_like(accd)
    accu[...] = jnp.zeros_like(accu)
    rawd[...] = jnp.zeros_like(rawd)
    rawu[...] = jnp.zeros_like(rawu)

    def run(pos_x, pos_y):
        rows = (0, 8) if pos_x else (8, 0)
        cols = (0, 1) if pos_y else (1, 0)
        tiles = [(r, c) for r in rows for c in cols]
        sub = lax.broadcasted_iota(jnp.int32, (8, 128), 0) == (0 if pos_x else 7)
        lane = lax.broadcasted_iota(jnp.int32, (8, 128), 1) == (0 if pos_y else 127)

        def some(i, carry):
            modes = [STEP * i + n for n in range(STEP)]
            coef = [[jnp.broadcast_to(tab[n, pl.ds(m, 1), :], (8, 128)) for n in range(4)] for m in modes]

            def rhs(d, t, z):
                alpha, beta, gamma, _ = coef[t]
                at = (d * MODES + modes[t]) * Z + z
                f = [[ref[c, at] for c in cols] for ref in (near_ref, far_ref)]
                rx = [[pltpu.roll(v, 1 if pos_x else 7, 0) for v in vs] for vs in f]
                ry = [[pltpu.roll(v, 1 if pos_y else 127, 1) for v in vs] for vs in f]
                out = []
                for r in range(2):
                    for c in range(2):
                        x = jnp.where(sub, 0.0 if r == 0 else rx[0][c], rx[r][c])
                        y = jnp.where(lane, 0.0 if c == 0 else ry[r][0], ry[r][c])
                        out.append(alpha * f[r][c] + beta * x + gamma * y)
                return out, f[0] + f[1]

            for d, acc, raw, order in ((1, accd, rawd, range(Z - 1, -1, -1)), (0, accu, rawu, range(Z))):
                if d == 1:
                    state = [
                        [jnp.broadcast_to(tab[4, pl.ds(m, 1), :], (8, 128)) * heat[pl.ds(r, 8), pl.ds(c * 128, 128)] for r, c in tiles]
                        for m in modes
                    ]
                else:
                    state = [None] * STEP
                for z in order:
                    sums = []
                    for t in range(STEP):
                        f, taken = rhs(d, t, z)
                        sums.append(taken)
                        state[t] = f if state[t] is None else [a + coef[t][3] * b for a, b in zip(f, state[t])]
                        for v, (r, c) in zip(state[t], tiles):
                            l0_ref[d, modes[t], pl.ds(z * ROWS + r, 8), pl.ds(c * 128, 128)] = v
                    for n, (r, c) in enumerate(tiles):
                        acc[c, pl.ds(z * ROWS + r, 8), :] += total([t[n] for t in state])
                        raw[c, pl.ds(z * ROWS + r, 8), :] += total([t[n] for t in sums])
                if d == 1:
                    for t in range(STEP):
                        for v, (r, c) in zip(state[t], tiles):
                            d0[c, pl.ds(pl.multiple_of(modes[t] * ROWS, ROWS) + r, 8), :] = v
            return carry

        def eight(g, carry):
            for c in (4 + g, g):
                for h in range(2):
                    half_tiles(x_hbm, near_ref, xsems, half, c, h).wait()
            return lax.fori_loop(2 * g, 2 * g + 2, some, carry)

        lax.fori_loop(0, 4, eight, 0)

    for pos_x in (True, False):
        for pos_y in (True, False):
            pl.when((up_x == pos_x) & (up_y == pos_y))(lambda px=pos_x, py=pos_y: run(px, py))

    e0_ref[...] = flags[3] * accd[...] + flags[2] * accu[...]
    e_ref[...] = flags[3] * rawd[...] + flags[2] * rawu[...]


def split(x):
    high = x.astype(jnp.bfloat16)
    return high, (x - high.astype(F32)).astype(jnp.bfloat16)


def spread(x, hot):
    high, low = split(x)
    dims = (((1,), (1,)), ((), ()))
    return lax.dot_general(high, hot, dims, preferred_element_type=F32) + lax.dot_general(
        low, hot, dims, preferred_element_type=F32
    )


def slot_kernel(
    cnt, flags, dcv, vel, rate, spec, wv, cells, rmap, tab, d0, e0_in,
    hot_ref, rm_ref, par, jm_ref, k0_ref, mt_ref, cz_ref, ksel, nsel, slot_ref, e0_ref, parts,
):
    k = lax.axis_index("mode")
    live = lax.broadcasted_iota(jnp.int32, (1, SLOTS), 1) < cnt[0]
    q = lax.broadcasted_iota(jnp.int32, (COLS, SLOTS), 0)
    hot_ref[...] = jnp.where(q == jnp.where(live, cells[...] & (COLS - 1), -1), 1.0, 0.0).astype(jnp.bfloat16)
    hot = hot_ref[...]
    cell_row = jnp.where(live, cells[...] >> 8, -1)
    rows = lax.broadcasted_iota(jnp.int32, (ROWS, SLOTS), 0)
    rm = jnp.where(rows == cell_row, 1.0, 0.0)
    rm_ref[...] = rm
    idx = jnp.where(cell_row == k, (rmap[...] + 1).astype(F32), 0.0).astype(jnp.bfloat16)
    jm_ref[...] = lax.dot_general(idx, hot, (((1,), (1,)), ((), ())), preferred_element_type=F32)
    mt_ref[...] = rmap[:, pl.ds(pl.multiple_of(128 * (k % 8), 128), 128)].astype(F32)
    mine = jnp.sum(jnp.where(rows == k, rmap[...], 0), axis=0, keepdims=True)
    czr = jnp.zeros((1, SLOTS), F32)
    for j in range(GROUP):
        czr = jnp.where(mine == j, jnp.abs(dcv[2:3, 2 * j : 2 * j + 1]), czr)
    cz_ref[...] = spread(rm * czr, hot)

    v, a = column(vel[...]), 1.0 + column(rate[...])
    eta = column(rate[...]) * column(spec[...])
    c_all = v * jnp.abs(dcv[2:3, :])
    inv_all = 1.0 / (a + c_all)
    k_all = c_all * inv_all
    for n, block in enumerate((k_all, eta * inv_all, jnp.broadcast_to(wv[...], (MODES, DIRS)))):
        par[n, :, pl.ds(0, DIRS)] = block
    term = eta * inv_all * wv[...]
    odd = lax.broadcasted_iota(jnp.int32, (MODES, DIRS), 1) % 2 == 1
    zr = lax.broadcasted_iota(jnp.int32, (Z, 128), 0)
    zc = lax.broadcasted_iota(jnp.int32, (Z, 128), 1)
    total = jnp.zeros((Z, 128), F32)
    for n in range(Z):
        down = jnp.sum(jnp.sum(jnp.where(odd, term, 0.0), axis=1, keepdims=True), axis=0, keepdims=True)
        up = jnp.sum(jnp.sum(jnp.where(odd, 0.0, term), axis=1, keepdims=True), axis=0, keepdims=True)
        total += jnp.where(zc - zr == n, down, 0.0) + jnp.where(zr - zc == n, up, 0.0)
        term = term * k_all
    k0_ref[...] = total

    vb, ab, nb = [jnp.broadcast_to(t, (MODES, 128)) for t in (v, a, 0.9 * eta)]
    for h in range(2):
        for r in (0, 8):
            cz = cz_ref[pl.ds(r, 8), pl.ds(h * 128, 128)]
            gain = jnp.where(cz < 0.1, 0.9 * flags[2], 0.0)
            acc = [jnp.zeros((8, 128), F32) for _ in range(Z)]
            for m in range(MODES):
                at = pl.ds(m * ROWS + r, 8)
                c = vb[m : m + 1, :] * cz
                inv = 1.0 / (ab[m : m + 1, :] + c)
                ksel[h, at, :] = c * inv
                nsel[h, at, :] = nb[m : m + 1, :] * inv
                f = gain * d0[h, at, :]
                kp = jnp.broadcast_to(tab[KAPPA, pl.ds(m, 1), :], (8, 128))
                for z in range(Z):
                    f = kp * f
                    acc[z] += f
            for z in range(Z):
                at = pl.ds(z * ROWS + r, 8)
                e0_ref[h, at, :] = e0_in[h, at, :] + acc[z]

    for r in range(ROWS):
        for t in range(2):
            x = jnp.concatenate(
                [
                    jnp.concatenate([d0[h, pl.ds((2 * t + u) * PLANE + r, 8, stride=ROWS), :] for h in range(2)], axis=1)
                    for u in range(2)
                ],
                axis=0,
            )
            parts[pl.ds(r * MODES + 16 * t, 16), :] = x.astype(jnp.bfloat16)
    for n in range(SLOTS // 256):
        at = pl.ds(n * 256, 256)
        got = jnp.dot(parts[...], hot_ref[:, at], preferred_element_type=F32)
        mine = rm[0:1, n * 256 : n * 256 + 256] * got[0:MODES]
        for r in range(1, ROWS):
            mine += rm[r : r + 1, n * 256 : n * 256 + 256] * got[r * MODES : (r + 1) * MODES]
        slot_ref[:, at] = mine


def pack_kernel(flags, tab, e_ref, e0_ref, slot_ref, hot, rm, cz_ref, chip, next_chip, out):
    up_x = flags[0] > 0.0
    delta = [jnp.where(flags[4] > 0.5, chip[h, pl.ds(EDGE, 40), :], next_chip[h, pl.ds(EDGE, 40), :]) for h in range(2)]
    extra = []
    for h in range(2):
        at = slice(h * 128, h * 128 + 128)
        cz = jnp.where(up_x, cz_ref[0:1, at], cz_ref[ROWS - 1 : ROWS, at])
        gain = jnp.broadcast_to(jnp.where(cz < 0.1, 0.9 * flags[2], 0.0), (8, 128))
        acc = [jnp.zeros((8, 128), F32) for _ in range(Z)]
        for t in range(MODES // 8):
            f = gain * delta[h][8 + 8 * t : 16 + 8 * t, :]
            for z in range(Z):
                f = tab[KAPPA, pl.ds(8 * t, 8), :] * f
                acc[z] += f
        extra.append(delta[h][0:8, :] + jnp.concatenate([jnp.sum(t, axis=0, keepdims=True) for t in acc], axis=0))
    high, low = split(jnp.concatenate([d[8:40, :] for d in delta], axis=1))
    more = jnp.dot(jnp.concatenate([high, low], axis=0), hot[...], preferred_element_type=F32)
    mask = jnp.where(up_x, rm[0:1, :], rm[ROWS - 1 : ROWS, :])
    slots = slot_ref[...] + mask * (more[0:MODES, :] + more[MODES : 2 * MODES, :])
    for r in range(ROWS):
        tile, low_mode = (r % 8) * 128, 16 * (r // 8)
        for h in range(2):
            part = e0_ref[h, pl.ds(r, 8, stride=ROWS), :]
            if r == 0:
                part += jnp.where(up_x, extra[h], 0.0)
            if r == ROWS - 1:
                part += jnp.where(up_x, 0.0, extra[h])
            out[r, h, 0:8, :] = e_ref[h, pl.ds(r, 8, stride=ROWS), :]
            out[r, h, 8:16, :] = part
            out[r, h, 16:24, :] = slots[low_mode + 8 * h : low_mode + 8 * h + 8, tile : tile + 128]


def middle_kernel(got, par, jm_ref, k0_ref, mt_ref, out, q_ref):
    def take(s, at):
        return jnp.concatenate([got[s, h, at : at + 8, :] for h in range(2)], axis=1)

    energy = take(0, 0)
    rest = take(0, 8)
    for s in range(1, GROUP):
        energy += take(s, 0)
        rest += take(s, 8)
    energy = energy * (1.0 / PAIRS)
    equil = energy / (1.0 + 0.3 * jnp.abs(energy))
    eq = [jnp.broadcast_to(equil[z : z + 1, :], (8, COLS)) for z in range(Z)]
    k_all, n_all, w_all = par[0], par[1], par[2]
    for j in range(GROUP):
        for t in range(MODES // 8):
            at = slice(8 * t, 8 * t + 8)
            kp = jnp.broadcast_to(k_all[at, 2 * j + 1 : 2 * j + 2], (8, COLS))
            eta = jnp.broadcast_to(n_all[at, 2 * j + 1 : 2 * j + 2], (8, COLS))
            s = eq[Z - 1]
            for z in reversed(range(Z - 1)):
                s = kp * s + eq[z]
            q_ref[j, at, :] = (0.9 * eta) * s
    acc = [jnp.zeros((8, COLS), F32) for _ in range(Z)]
    for k in range(GROUP):
        jm = jnp.broadcast_to(jm_ref[k : k + 1, :], (8, COLS))
        jm = jnp.where(jm < 0.5, float(k + 1), jm)
        w = jnp.broadcast_to(w_all[0:8, 2 * k : 2 * k + 1], (8, COLS))
        for t in range(MODES // 8):
            at = slice(8 * t, 8 * t + 8)
            pick = q_ref[0, at, :]
            for j in range(1, GROUP):
                pick = jnp.where(jm > j + 0.5, q_ref[j, at, :], pick)
            kp = jnp.broadcast_to(k_all[at, 2 * k : 2 * k + 1], (8, COLS))
            pick = w * pick
            for z in range(Z):
                pick = kp * pick
                acc[z] += pick
    bounce = jnp.concatenate([jnp.sum(t, axis=0, keepdims=True) for t in acc], axis=0)
    first = pl.multiple_of(16 * (lax.axis_index("mode") // 8), 16)
    acc = [jnp.zeros((8, COLS), F32) for _ in range(Z)]
    for k in range(GROUP):
        index = jnp.concatenate([jnp.broadcast_to(mt_ref[k : k + 1, :], (8, 128))] * 2, axis=1)
        pick = take(0, 16)
        for j in range(1, GROUP):
            pick = jnp.where(index > j - 0.5, take(j, 16), pick)
        pick = 0.9 * pick
        for h in range(2):
            out[k, h] = pick[:, h * 128 : h * 128 + 128]
        kp = jnp.concatenate(
            [jnp.broadcast_to(par[0, pl.ds(first + 8 * u, 8), pl.ds(0, 128)][:, 2 * k : 2 * k + 1], (8, 128)) for u in range(2)],
            axis=1,
        )
        pick = jnp.broadcast_to(w_all[0:8, 2 * k : 2 * k + 1], (8, COLS)) * pick
        for z in range(Z):
            pick = kp * pick
            acc[z] += pick
    sums = [jnp.sum(t, axis=0, keepdims=True) for t in acc]
    at_slots = jnp.concatenate([t[:, 0:128] + t[:, 128:256] for t in sums], axis=0) * (1.0 / PAIRS)
    fresh = rest + bounce
    for z in range(Z):
        fresh += jnp.broadcast_to(k0_ref[:, z : z + 1], (8, COLS)) * eq[z]
    fresh = fresh * (1.0 / PAIRS)
    for k in range(GROUP):
        for h in range(2):
            out[k, 2 + h] = equil[:, h * 128 : h * 128 + 128]
            out[k, 4 + h] = fresh[:, h * 128 : h * 128 + 128]
        out[k, 6] = at_slots


def finish_kernel(
    flags, tab, l0_ref, back, hot_ref, rm_ref, cz_ref, ksel, nsel, chip, next_chip,
    out_hbm, en_hbm, eq, res, cell, grid_en, en_ref, sems, en_sem,
):
    up_x, on_chip = flags[0] > 0.0, flags[4] > 0.5
    for z in range(Z):
        for h in range(2):
            for b in range(2):
                got = back[pl.ds((8 * b * BACK + 2 + h) * 8 + z, 8, stride=8 * BACK), :]
                eq[pl.ds(z * ROWS + 8 * b, 8), pl.ds(h * 128, 128)] = got

    def leave(g, d):
        part = pl.ds(g * STEP, STEP)
        return pltpu.make_async_copy(res.at[d, part], out_hbm.at[d, part], sems.at[d, g])

    def run(d, pos_x, edge):
        first = 0 if pos_x else 8
        sub = lax.broadcasted_iota(jnp.int32, (8, 128), 0) == (0 if pos_x else 7)

        def some(g, carry):
            modes = [STEP * g + n for n in range(STEP)]
            eta, beta, kappa = [
                [jnp.broadcast_to(tab[n, pl.ds(m, 1), :], (8, 128)) for m in modes] for n in (ETA, BETA, KAPPA)
            ]
            for r in (0, 8):
                for h in range(2):
                    at = [(pl.ds(z * ROWS + r, 8), pl.ds(h * 128, 128)) for z in range(Z)]
                    e = [eq[to] for to in at]

                    def source(n, z):
                        s = eta[n] * e[z]
                        if r == first:
                            row = edge[h, pl.ds(z * 64 + d * 32 + modes[n], 1), :]
                            s += jnp.where(sub, beta[n] * jnp.broadcast_to(row, (8, 128)), 0.0)
                        return s

                    t = [None] * STEP
                    if d == 0:
                        rough = cz_ref[pl.ds(r, 8), pl.ds(h * 128, 128)] > 0.1
                        here = [pl.ds(pl.multiple_of(m * ROWS, ROWS) + r, 8) for m in modes]
                        kp = [ksel[h, to, :] for to in here]
                        far = [e[Z - 1]] * STEP
                        for z in reversed(range(Z - 1)):
                            far = [a * b + e[z] for a, b in zip(kp, far)]
                        for n, m in enumerate(modes):
                            far[n] = nsel[h, here[n], :] * far[n] + cell[h, pl.ds(r * MODES + m, 8, stride=MODES), :]
                            t[n] = jnp.where(rough, far[n], 0.9 * res[(1, m) + at[0]])
                    for z in range(Z) if d == 0 else range(Z - 1, -1, -1):
                        for n, m in enumerate(modes):
                            t[n] = source(n, z) if t[n] is None else kappa[n] * t[n] + source(n, z)
                            res[(d, m) + at[z]] = l0_ref[(d, m) + at[z]] + t[n]
            leave(g, d).start()
            return carry

        lax.fori_loop(0, MODES // STEP, some, 0)

    def all_modes(d):
        for pos_x in (True, False):
            for here, edge in ((True, chip), (False, next_chip)):
                pl.when((up_x == pos_x) & (on_chip == here))(lambda p=pos_x, e=edge: run(d, p, e))

    all_modes(1)
    hot = hot_ref[...]
    def tiles_of(half, n):
        return [back[pl.ds(((8 * half + t) * BACK + n) * 8, 8), :] for t in range(8)]

    picked = [jnp.concatenate(tiles_of(half, h), axis=1) for half in range(2) for h in range(2)]
    heard = jnp.concatenate(tiles_of(0, 6), axis=1) + jnp.concatenate(tiles_of(1, 6), axis=1)
    heard_high = heard.astype(jnp.bfloat16).astype(F32)
    value = jnp.concatenate(picked + [heard_high, heard - heard_high], axis=0).astype(jnp.bfloat16)
    mask = rm_ref[...].astype(jnp.bfloat16)
    dims = (((1,), (1,)), ((), ()))
    for part in range(4):
        lhs = jnp.concatenate([mask[r : r + 1, :] * value for r in range(4 * part, 4 * part + 4)], axis=0)
        got = lax.dot_general(lhs, hot, dims, preferred_element_type=F32)
        for n, r in enumerate(range(4 * part, 4 * part + 4)):
            for h in range(2):
                cell[h, pl.ds(r * MODES, MODES), :] = got[48 * n : 48 * n + 32, h * 128 : h * 128 + 128]
                both = got[48 * n + 32 : 48 * n + 40, h * 128 : h * 128 + 128] + got[48 * n + 40 : 48 * n + 48, h * 128 : h * 128 + 128]
                grid_en[h, pl.ds(r * 8, 8), :] = both + back[pl.ds((r * BACK + 4 + h) * 8, 8), :]
    for z in range(Z):
        for h in range(2):
            for b in range(2):
                en_ref[pl.ds(z * ROWS + 8 * b, 8), pl.ds(h * 128, 128)] = grid_en[h, pl.ds(8 * b * 8 + z, 8, stride=8), :]
    energy_copy = pltpu.make_async_copy(en_ref, en_hbm, en_sem)
    energy_copy.start()
    all_modes(0)
    energy_copy.wait()
    for g in range(MODES // STEP):
        for d in range(2):
            leave(g, d).wait()


def per_device(
    intensity, dir_cos, velocity, rate, spectrum, weight, heat, rough_cells, rough_count, rough_map
):
    smem = pl.BlockSpec(memory_space=pltpu.SMEM)
    vmem = pl.BlockSpec(memory_space=pltpu.VMEM)

    def hbm(x):
        return pltpu.with_memory_space_constraint(x, pltpu.HBM)

    anywhere = pl.BlockSpec(memory_space=pltpu.HBM)
    field = (2, MODES, PLANE, COLS)
    ones = [t.reshape(1, -1) for t in (velocity, rate, spectrum, weight, rough_cells)]
    tiles = hbm(intensity.reshape(512, 2, 8, COLS))
    x, edge, tab, flags = pl.pallas_call(
        edge_kernel,
        in_specs=[anywhere] * 6,
        out_specs=[vmem] * 3 + [smem],
        out_shape=[
            pltpu.VMEM(s, F32)
            for s in ((2, 512, 8, 128), (2, EDGE + 40, 128), (6, MODES, 128))
        ]
        + [pltpu.SMEM((5,), F32)],
        scratch_shapes=[
            pltpu.VMEM((3, DIRS), F32),
            pltpu.VMEM((1, MODES), F32),
            pltpu.VMEM((1, MODES), F32),
            pltpu.VMEM((1, MODES), F32),
            pltpu.VMEM((1, DIRS), F32),
            pltpu.VMEM((2, 64, 128), F32),
            pltpu.SemaphoreType.DMA((5,)),
            pltpu.SemaphoreType.DMA((2, 8)),
        ],
        compiler_params=pltpu.CompilerParams(vmem_limit_bytes=8 << 20),
        cost_estimate=pl.CostEstimate(flops=4 << 20, bytes_accessed=8 << 20, transcendentals=0),
        name="edges",
    )(tiles, hbm(dir_cos), *[hbm(t) for t in ones[:4]])
    count = lax.axis_size("space")
    on_chip = [(i, i ^ 1) for i in range(count)]
    across = [(i, i + 1 if i % 2 else i - 1) for i in range(1, count - 1)]
    edge_chip, edge_next = [lax.ppermute(edge, "space", p) for p in (on_chip, across)]

    base, energy, e0, d0 = pl.pallas_call(
        sweep_kernel,
        in_specs=[smem, vmem, anywhere, vmem, vmem],
        out_specs=[vmem] * 4,
        out_shape=[pltpu.VMEM(s, F32) for s in (field, (2, PLANE, 128), (2, PLANE, 128), (2, MODES * ROWS, 128))],
        scratch_shapes=[
            pltpu.VMEM((2, 512, 8, 128), F32),
            pltpu.VMEM((2, PLANE, 128), F32),
            pltpu.VMEM((2, PLANE, 128), F32),
            pltpu.VMEM((2, PLANE, 128), F32),
            pltpu.VMEM((2, PLANE, 128), F32),
            pltpu.SemaphoreType.DMA((2, 8)),
        ],
        compiler_params=pltpu.CompilerParams(vmem_limit_bytes=12 << 20),
        cost_estimate=pl.CostEstimate(flops=30 << 20, bytes_accessed=16 << 20, transcendentals=0),
        name="sweep",
    )(flags, tab, tiles, x, heat)

    tables = [
        ((COLS, SLOTS), jnp.bfloat16), ((ROWS, SLOTS), F32), ((3, MODES, 128), F32), ((GROUP, COLS), F32),
        ((Z, 128), F32), ((GROUP, 128), F32), ((ROWS, COLS), F32), ((2, MODES * ROWS, 128), F32),
        ((2, MODES * ROWS, 128), F32), ((MODES, SLOTS), F32), ((2, PLANE, 128), F32),
    ]
    hot, rm, par, jm, k0, mt, cz, ksel, nsel, at_slots, e0 = pl.pallas_call(
        slot_kernel,
        in_specs=[smem] * 2 + [vmem] * 10,
        out_specs=[vmem] * len(tables),
        out_shape=[pltpu.VMEM(*t) for t in tables],
        scratch_shapes=[pltpu.VMEM((MODES * ROWS, COLS), jnp.bfloat16)],
        compiler_params=pltpu.CompilerParams(vmem_limit_bytes=12 << 20),
        cost_estimate=pl.CostEstimate(flops=30 << 20, bytes_accessed=8 << 20, transcendentals=0),
        name="slots",
    )(rough_count, flags, dir_cos, *ones, rough_map.T, tab, d0, e0)

    pack = pl.pallas_call(
        pack_kernel,
        in_specs=[smem] + [vmem] * 9,
        out_specs=vmem,
        out_shape=pltpu.VMEM((GROUP, 2, SEND, 128), F32),
        compiler_params=pltpu.CompilerParams(vmem_limit_bytes=8 << 20),
        name="pack",
    )(flags, tab, energy, e0, at_slots, hot, rm, cz, edge_chip, edge_next)
    got = lax.all_to_all(pack, "mode", 0, 0, tiled=True)

    reply = pl.pallas_call(
        middle_kernel,
        in_specs=[vmem] * 5,
        out_specs=vmem,
        out_shape=pltpu.VMEM((GROUP, BACK, 8, 128), F32),
        scratch_shapes=[pltpu.VMEM((GROUP, MODES, COLS), F32)],
        compiler_params=pltpu.CompilerParams(vmem_limit_bytes=8 << 20),
        name="middle",
    )(got, par, jm, k0, mt)
    back = lax.all_to_all(reply, "mode", 0, 0, tiled=True).reshape(GROUP * BACK * 8, 128)

    fresh, energy_new = pl.pallas_call(
        finish_kernel,
        in_specs=[smem] + [vmem] * 10,
        out_specs=[anywhere, anywhere],
        out_shape=[pltpu.HBM(field, F32), pltpu.HBM((PLANE, COLS), F32)],
        scratch_shapes=[
            pltpu.VMEM((PLANE, COLS), F32),
            pltpu.VMEM(field, F32),
            pltpu.VMEM((2, MODES * ROWS, 128), F32),
            pltpu.VMEM((2, PLANE, 128), F32),
            pltpu.VMEM((PLANE, COLS), F32),
            pltpu.SemaphoreType.DMA((2, MODES // STEP)),
            pltpu.SemaphoreType.DMA,
        ],
        compiler_params=pltpu.CompilerParams(vmem_limit_bytes=24 << 20),
        name="finish",
    )(flags, tab, base, back, hot, rm, cz, ksel, nsel, edge_chip, edge_next)
    return fresh.reshape(intensity.shape), energy_new.reshape(Z, ROWS, COLS)


def solution(mesh):
    in_specs = (
        P("mode", None, "space", None),
        P(),
        P(),
        P(),
        P(),
        P(),
        P("space", None),
        P("space"),
        P("space"),
        P("space", None),
    )
    out_specs = (P("mode", None, "space", None), P(None, "space", None))
    return jax.shard_map(
        per_device, mesh=mesh, in_specs=in_specs, out_specs=out_specs, check_vma=False
    )
```

```python
import jax
import jax.numpy as jnp
from jax import lax
from jax.experimental import pallas as pl
from jax.experimental.pallas import tpu as pltpu
from jax.sharding import PartitionSpec as P

PAIRS = 1024
DIRS = 32
MODES = 32
Z = 8
ROWS = 16
COLS = 256
GROUP = 16
PLANE = Z * ROWS
SEND = 24
BACK = 7
SLOTS = 1024
STEP = 4
F32 = jnp.float32


def column(row):
    r = lax.broadcasted_iota(jnp.int32, (MODES, MODES), 0)
    c = lax.broadcasted_iota(jnp.int32, (MODES, MODES), 1)
    return jnp.sum(jnp.where(r == c, jnp.broadcast_to(row, (MODES, MODES)), 0.0), axis=1, keepdims=True)


ALPHA, BETA, GAMMA, KAPPA, SHARE, ETA = range(6)
CHUNK = 8 * Z
EDGE = 512


def half_tiles(x_hbm, dst, sems, half, c, h):
    src = x_hbm.at[pl.ds(c * CHUNK, CHUNK), half, :, pl.ds(h * 128, 128)]
    return pltpu.make_async_copy(src, dst.at[h, pl.ds(c * CHUNK, CHUNK)], sems.at[h, c])


def edge_kernel(
    x_hbm, dc_h, v_h, r_h, s_h, w_h,
    x_ref, edge_ref, tab, flags,
    dcv, vel, rate, spec, wv, acc, sems, xsems,
):
    k = lax.axis_index("mode")
    odd_row = lax.axis_index("space") % 2 == 1
    few = list(zip((dc_h, v_h, r_h, s_h, w_h), (dcv, vel, rate, spec, wv)))
    few = [pltpu.make_async_copy(a, b, sems.at[n]) for n, (a, b) in enumerate(few)]
    for copy in few:
        copy.start()
    few[0].wait()
    lane = lax.broadcasted_iota(jnp.int32, (1, DIRS), 1)

    def pick(row, at):
        return jnp.sum(jnp.where(lane == at, row, 0.0))

    cx, cy, cz = [pick(dcv[n : n + 1, :], 2 * k) for n in range(3)]
    half = jnp.where(cx > 0.0, 1, 0)
    for c in range(8):
        for h in range(2):
            half_tiles(x_hbm, x_ref, xsems, half, c, h).start()
    for copy in few[1:]:
        copy.wait()
    cz = jnp.abs(cz)
    flags[0] = cx
    flags[1] = cy
    flags[2] = pick(wv[...], 2 * k)
    flags[3] = pick(wv[...], 2 * k + 1)
    flags[4] = jnp.where((cx > 0.0) == odd_row, 1.0, 0.0)
    v, a = column(vel[...]), 1.0 + column(rate[...])
    share, eta = column(spec[...]), column(rate[...]) * column(spec[...])
    inv = 1.0 / (a + v * cz)
    table = {
        ALPHA: (1.0 - v * jnp.abs(cx) - v * jnp.abs(cy)) * inv,
        BETA: v * jnp.abs(cx) * inv,
        GAMMA: v * jnp.abs(cy) * inv,
        KAPPA: v * cz * inv,
        SHARE: share,
        ETA: eta * inv,
    }
    for n, col in table.items():
        tab[n] = jnp.broadcast_to(col, (MODES, 128))
    acc[...] = jnp.zeros_like(acc)

    row = jnp.where(cx > 0.0, 7, 0)
    flat = x_ref.reshape(2, 512 * 8, 128)

    def one(c, carry):
        w = flags[2 + c // 4]
        base = pl.multiple_of(c * CHUNK * 8, CHUNK * 8)
        m0 = pl.multiple_of(8 * (c % 4), 8)
        for h in range(2):
            half_tiles(x_hbm, x_ref, xsems, half, c, h).wait()
            kp, bt = [tab[n, pl.ds(m0, 8), :] for n in (KAPPA, BETA)]
            rows = []
            for z in range(Z):
                e = flat[h, pl.ds(base + z * 8 + row, 8, stride=8 * Z), :]
                edge_ref[h, pl.ds(pl.multiple_of(z * 64 + 8 * c, 8), 8), :] = e
                rows.append(bt * e)

            @pl.when(c < 4)
            def _():
                t = rows[0]
                acc[h, pl.ds(0, 8), :] += w * t
                for z in range(1, Z):
                    t = kp * t + rows[z]
                    acc[h, pl.ds(8 * z, 8), :] += w * t

            @pl.when(c >= 4)
            def _():
                t = rows[Z - 1]
                acc[h, pl.ds(8 * (Z - 1), 8), :] += w * t
                for z in reversed(range(Z - 1)):
                    t = kp * t + rows[z]
                    acc[h, pl.ds(8 * z, 8), :] += w * t
                edge_ref[h, pl.ds(EDGE + 8 + m0, 8), :] = t

        return carry

    lax.fori_loop(0, 8, one, 0)
    for h in range(2):
        for z in range(Z):
            edge_ref[h, pl.ds(EDGE + z, 1), :] = jnp.sum(acc[h, pl.ds(8 * z, 8), :], axis=0, keepdims=True)


def total(values):
    while len(values) > 1:
        values = [a + b for a, b in zip(values[::2], values[1::2])]
    return values[0]


def sweep_kernel(
    flags, tab, x_hbm, far_ref, heat, l0_ref, e_ref, e0_ref, d0, near_ref, accd, accu, rawd, rawu, xsems,
):
    up_x, up_y = flags[0] > 0.0, flags[1] > 0.0
    half = jnp.where(up_x, 0, 1)
    for g in range(4):
        for c in (4 + g, g):
            for h in range(2):
                half_tiles(x_hbm, near_ref, xsems, half, c, h).start()
    accd[...] = jnp.zeros_like(accd)
    accu[...] = jnp.zeros_like(accu)
    rawd[...] = jnp.zeros_like(rawd)
    rawu[...] = jnp.zeros_like(rawu)

    def run(pos_x, pos_y):
        rows = (0, 8) if pos_x else (8, 0)
        cols = (0, 1) if pos_y else (1, 0)
        tiles = [(r, c) for r in rows for c in cols]
        sub = lax.broadcasted_iota(jnp.int32, (8, 128), 0) == (0 if pos_x else 7)
        lane = lax.broadcasted_iota(jnp.int32, (8, 128), 1) == (0 if pos_y else 127)

        def some(i, carry):
            modes = [STEP * i + n for n in range(STEP)]
            coef = [[jnp.broadcast_to(tab[n, pl.ds(m, 1), :], (8, 128)) for n in range(4)] for m in modes]

            def rhs(d, t, z):
                alpha, beta, gamma, _ = coef[t]
                at = (d * MODES + modes[t]) * Z + z
                f = [[ref[c, at] for c in cols] for ref in (near_ref, far_ref)]
                rx = [[pltpu.roll(v, 1 if pos_x else 7, 0) for v in vs] for vs in f]
                ry = [[pltpu.roll(v, 1 if pos_y else 127, 1) for v in vs] for vs in f]
                out = []
                for r in range(2):
                    for c in range(2):
                        x = jnp.where(sub, 0.0 if r == 0 else rx[0][c], rx[r][c])
                        y = jnp.where(lane, 0.0 if c == 0 else ry[r][0], ry[r][c])
                        out.append(alpha * f[r][c] + beta * x + gamma * y)
                return out, f[0] + f[1]

            for d, acc, raw, order in ((1, accd, rawd, range(Z - 1, -1, -1)), (0, accu, rawu, range(Z))):

                @pl.when(i % 2 == 0)
                def _(d=d):
                    for h in range(2):
                        half_tiles(x_hbm, near_ref, xsems, half, i // 2 + 4 * d, h).wait()

                if d == 1:
                    state = [
                        [jnp.broadcast_to(tab[4, pl.ds(m, 1), :], (8, 128)) * heat[pl.ds(r, 8), pl.ds(c * 128, 128)] for r, c in tiles]
                        for m in modes
                    ]
                else:
                    state = [None] * STEP
                for z in order:
                    sums = []
                    for t in range(STEP):
                        f, taken = rhs(d, t, z)
                        sums.append(taken)
                        state[t] = f if state[t] is None else [a + coef[t][3] * b for a, b in zip(f, state[t])]
                        for v, (r, c) in zip(state[t], tiles):
                            l0_ref[d, modes[t], pl.ds(z * ROWS + r, 8), pl.ds(c * 128, 128)] = v
                    for n, (r, c) in enumerate(tiles):
                        acc[c, pl.ds(z * ROWS + r, 8), :] += total([t[n] for t in state])
                        raw[c, pl.ds(z * ROWS + r, 8), :] += total([t[n] for t in sums])
                if d == 1:
                    for t in range(STEP):
                        for v, (r, c) in zip(state[t], tiles):
                            d0[c, pl.ds(pl.multiple_of(modes[t] * ROWS, ROWS) + r, 8), :] = v
            return carry

        def eight(g, carry):
            return lax.fori_loop(2 * g, 2 * g + 2, some, carry)

        lax.fori_loop(0, 4, eight, 0)

    for pos_x in (True, False):
        for pos_y in (True, False):
            pl.when((up_x == pos_x) & (up_y == pos_y))(lambda px=pos_x, py=pos_y: run(px, py))

    e0_ref[...] = flags[3] * accd[...] + flags[2] * accu[...]
    e_ref[...] = flags[3] * rawd[...] + flags[2] * rawu[...]


def split(x):
    high = x.astype(jnp.bfloat16)
    return high, (x - high.astype(F32)).astype(jnp.bfloat16)


def spread(x, hot):
    high, low = split(x)
    dims = (((1,), (1,)), ((), ()))
    return lax.dot_general(high, hot, dims, preferred_element_type=F32) + lax.dot_general(
        low, hot, dims, preferred_element_type=F32
    )


def slot_kernel(
    cnt, flags, dcv, vel, rate, spec, wv, cells, rmap, tab, d0, e0_in,
    hot_ref, rm_ref, par, jm_ref, k0_ref, mt_ref, cz_ref, ksel, nsel, slot_ref, e0_ref, parts,
):
    k = lax.axis_index("mode")
    live = lax.broadcasted_iota(jnp.int32, (1, SLOTS), 1) < cnt[0]
    q = lax.broadcasted_iota(jnp.int32, (COLS, SLOTS), 0)
    hot_ref[...] = jnp.where(q == jnp.where(live, cells[...] & (COLS - 1), -1), 1.0, 0.0).astype(jnp.bfloat16)
    hot = hot_ref[...]
    cell_row = jnp.where(live, cells[...] >> 8, -1)
    rows = lax.broadcasted_iota(jnp.int32, (ROWS, SLOTS), 0)
    rm = jnp.where(rows == cell_row, 1.0, 0.0)
    rm_ref[...] = rm
    idx = jnp.where(cell_row == k, (rmap[...] + 1).astype(F32), 0.0).astype(jnp.bfloat16)
    jm_ref[...] = lax.dot_general(idx, hot, (((1,), (1,)), ((), ())), preferred_element_type=F32)
    mt_ref[...] = rmap[:, pl.ds(pl.multiple_of(128 * (k % 8), 128), 128)].astype(F32)
    mine = jnp.sum(jnp.where(rows == k, rmap[...], 0), axis=0, keepdims=True)
    czr = jnp.zeros((1, SLOTS), F32)
    for j in range(GROUP):
        czr = jnp.where(mine == j, jnp.abs(dcv[2:3, 2 * j : 2 * j + 1]), czr)
    cz_ref[...] = spread(rm * czr, hot)

    v, a = column(vel[...]), 1.0 + column(rate[...])
    eta = column(rate[...]) * column(spec[...])
    c_all = v * jnp.abs(dcv[2:3, :])
    inv_all = 1.0 / (a + c_all)
    k_all = c_all * inv_all
    for n, block in enumerate((k_all, eta * inv_all, jnp.broadcast_to(wv[...], (MODES, DIRS)))):
        par[n, :, pl.ds(0, DIRS)] = block
    term = eta * inv_all * wv[...]
    odd = lax.broadcasted_iota(jnp.int32, (MODES, DIRS), 1) % 2 == 1
    zr = lax.broadcasted_iota(jnp.int32, (Z, 128), 0)
    zc = lax.broadcasted_iota(jnp.int32, (Z, 128), 1)
    total = jnp.zeros((Z, 128), F32)
    for n in range(Z):
        down = jnp.sum(jnp.sum(jnp.where(odd, term, 0.0), axis=1, keepdims=True), axis=0, keepdims=True)
        up = jnp.sum(jnp.sum(jnp.where(odd, 0.0, term), axis=1, keepdims=True), axis=0, keepdims=True)
        total += jnp.where(zc - zr == n, down, 0.0) + jnp.where(zr - zc == n, up, 0.0)
        term = term * k_all
    k0_ref[...] = total

    vb, ab, nb = [jnp.broadcast_to(t, (MODES, 128)) for t in (v, a, 0.9 * eta)]
    for h in range(2):
        for r in (0, 8):
            cz = cz_ref[pl.ds(r, 8), pl.ds(h * 128, 128)]
            gain = jnp.where(cz < 0.1, 0.9 * flags[2], 0.0)
            acc = [jnp.zeros((8, 128), F32) for _ in range(Z)]
            for m in range(MODES):
                at = pl.ds(m * ROWS + r, 8)
                c = vb[m : m + 1, :] * cz
                inv = 1.0 / (ab[m : m + 1, :] + c)
                ksel[h, at, :] = c * inv
                nsel[h, at, :] = nb[m : m + 1, :] * inv
                f = gain * d0[h, at, :]
                kp = jnp.broadcast_to(tab[KAPPA, pl.ds(m, 1), :], (8, 128))
                for z in range(Z):
                    f = kp * f
                    acc[z] += f
            for z in range(Z):
                at = pl.ds(z * ROWS + r, 8)
                e0_ref[h, at, :] = e0_in[h, at, :] + acc[z]

    for r in range(ROWS):
        for t in range(2):
            x = jnp.concatenate(
                [
                    jnp.concatenate([d0[h, pl.ds((2 * t + u) * PLANE + r, 8, stride=ROWS), :] for h in range(2)], axis=1)
                    for u in range(2)
                ],
                axis=0,
            )
            parts[pl.ds(r * MODES + 16 * t, 16), :] = x.astype(jnp.bfloat16)
    for n in range(SLOTS // 256):
        at = pl.ds(n * 256, 256)
        got = jnp.dot(parts[...], hot_ref[:, at], preferred_element_type=F32)
        mine = rm[0:1, n * 256 : n * 256 + 256] * got[0:MODES]
        for r in range(1, ROWS):
            mine += rm[r : r + 1, n * 256 : n * 256 + 256] * got[r * MODES : (r + 1) * MODES]
        slot_ref[:, at] = mine


def pack_kernel(flags, tab, e_ref, e0_ref, slot_ref, hot, rm, cz_ref, chip, next_chip, out):
    up_x = flags[0] > 0.0
    delta = [jnp.where(flags[4] > 0.5, chip[h, pl.ds(EDGE, 40), :], next_chip[h, pl.ds(EDGE, 40), :]) for h in range(2)]
    extra = []
    for h in range(2):
        at = slice(h * 128, h * 128 + 128)
        cz = jnp.where(up_x, cz_ref[0:1, at], cz_ref[ROWS - 1 : ROWS, at])
        gain = jnp.broadcast_to(jnp.where(cz < 0.1, 0.9 * flags[2], 0.0), (8, 128))
        acc = [jnp.zeros((8, 128), F32) for _ in range(Z)]
        for t in range(MODES // 8):
            f = gain * delta[h][8 + 8 * t : 16 + 8 * t, :]
            for z in range(Z):
                f = tab[KAPPA, pl.ds(8 * t, 8), :] * f
                acc[z] += f
        extra.append(delta[h][0:8, :] + jnp.concatenate([jnp.sum(t, axis=0, keepdims=True) for t in acc], axis=0))
    high, low = split(jnp.concatenate([d[8:40, :] for d in delta], axis=1))
    more = jnp.dot(jnp.concatenate([high, low], axis=0), hot[...], preferred_element_type=F32)
    mask = jnp.where(up_x, rm[0:1, :], rm[ROWS - 1 : ROWS, :])
    slots = slot_ref[...] + mask * (more[0:MODES, :] + more[MODES : 2 * MODES, :])
    for r in range(ROWS):
        tile, low_mode = (r % 8) * 128, 16 * (r // 8)
        for h in range(2):
            part = e0_ref[h, pl.ds(r, 8, stride=ROWS), :]
            if r == 0:
                part += jnp.where(up_x, extra[h], 0.0)
            if r == ROWS - 1:
                part += jnp.where(up_x, 0.0, extra[h])
            out[r, h, 0:8, :] = e_ref[h, pl.ds(r, 8, stride=ROWS), :]
            out[r, h, 8:16, :] = part
            out[r, h, 16:24, :] = slots[low_mode + 8 * h : low_mode + 8 * h + 8, tile : tile + 128]


def middle_kernel(got, par, jm_ref, k0_ref, mt_ref, out, q_ref):
    def take(s, at):
        return jnp.concatenate([got[s, h, at : at + 8, :] for h in range(2)], axis=1)

    energy = take(0, 0)
    rest = take(0, 8)
    for s in range(1, GROUP):
        energy += take(s, 0)
        rest += take(s, 8)
    energy = energy * (1.0 / PAIRS)
    equil = energy / (1.0 + 0.3 * jnp.abs(energy))
    eq = [jnp.broadcast_to(equil[z : z + 1, :], (8, COLS)) for z in range(Z)]
    k_all, n_all, w_all = par[0], par[1], par[2]
    for j in range(GROUP):
        for t in range(MODES // 8):
            at = slice(8 * t, 8 * t + 8)
            kp = jnp.broadcast_to(k_all[at, 2 * j + 1 : 2 * j + 2], (8, COLS))
            eta = jnp.broadcast_to(n_all[at, 2 * j + 1 : 2 * j + 2], (8, COLS))
            s = eq[Z - 1]
            for z in reversed(range(Z - 1)):
                s = kp * s + eq[z]
            q_ref[j, at, :] = (0.9 * eta) * s
    acc = [jnp.zeros((8, COLS), F32) for _ in range(Z)]
    for k in range(GROUP):
        jm = jnp.broadcast_to(jm_ref[k : k + 1, :], (8, COLS))
        jm = jnp.where(jm < 0.5, float(k + 1), jm)
        w = jnp.broadcast_to(w_all[0:8, 2 * k : 2 * k + 1], (8, COLS))
        for t in range(MODES // 8):
            at = slice(8 * t, 8 * t + 8)
            pick = q_ref[0, at, :]
            for j in range(1, GROUP):
                pick = jnp.where(jm > j + 0.5, q_ref[j, at, :], pick)
            kp = jnp.broadcast_to(k_all[at, 2 * k : 2 * k + 1], (8, COLS))
            pick = w * pick
            for z in range(Z):
                pick = kp * pick
                acc[z] += pick
    bounce = jnp.concatenate([jnp.sum(t, axis=0, keepdims=True) for t in acc], axis=0)
    first = pl.multiple_of(16 * (lax.axis_index("mode") // 8), 16)
    acc = [jnp.zeros((8, COLS), F32) for _ in range(Z)]
    for k in range(GROUP):
        index = jnp.concatenate([jnp.broadcast_to(mt_ref[k : k + 1, :], (8, 128))] * 2, axis=1)
        pick = take(0, 16)
        for j in range(1, GROUP):
            pick = jnp.where(index > j - 0.5, take(j, 16), pick)
        pick = 0.9 * pick
        for h in range(2):
            out[k, h] = pick[:, h * 128 : h * 128 + 128]
        kp = jnp.concatenate(
            [jnp.broadcast_to(par[0, pl.ds(first + 8 * u, 8), pl.ds(0, 128)][:, 2 * k : 2 * k + 1], (8, 128)) for u in range(2)],
            axis=1,
        )
        pick = jnp.broadcast_to(w_all[0:8, 2 * k : 2 * k + 1], (8, COLS)) * pick
        for z in range(Z):
            pick = kp * pick
            acc[z] += pick
    sums = [jnp.sum(t, axis=0, keepdims=True) for t in acc]
    at_slots = jnp.concatenate([t[:, 0:128] + t[:, 128:256] for t in sums], axis=0) * (1.0 / PAIRS)
    fresh = rest + bounce
    for z in range(Z):
        fresh += jnp.broadcast_to(k0_ref[:, z : z + 1], (8, COLS)) * eq[z]
    fresh = fresh * (1.0 / PAIRS)
    for k in range(GROUP):
        for h in range(2):
            out[k, 2 + h] = equil[:, h * 128 : h * 128 + 128]
            out[k, 4 + h] = fresh[:, h * 128 : h * 128 + 128]
        out[k, 6] = at_slots


def finish_kernel(
    flags, tab, l0_ref, back, hot_ref, rm_ref, cz_ref, ksel, nsel, chip, next_chip,
    out_hbm, en_hbm, eq, res, cell, grid_en, en_ref, sems, en_sem,
):
    up_x, on_chip = flags[0] > 0.0, flags[4] > 0.5
    for z in range(Z):
        for h in range(2):
            for b in range(2):
                got = back[pl.ds((8 * b * BACK + 2 + h) * 8 + z, 8, stride=8 * BACK), :]
                eq[pl.ds(z * ROWS + 8 * b, 8), pl.ds(h * 128, 128)] = got

    def leave(g, d):
        part = pl.ds(g * STEP, STEP)
        return pltpu.make_async_copy(res.at[d, part], out_hbm.at[d, part], sems.at[d, g])

    def run(d, pos_x, edge):
        first = 0 if pos_x else 8
        sub = lax.broadcasted_iota(jnp.int32, (8, 128), 0) == (0 if pos_x else 7)

        def some(g, carry):
            modes = [STEP * g + n for n in range(STEP)]
            eta, beta, kappa = [
                [jnp.broadcast_to(tab[n, pl.ds(m, 1), :], (8, 128)) for m in modes] for n in (ETA, BETA, KAPPA)
            ]
            for r in (0, 8):
                for h in range(2):
                    at = [(pl.ds(z * ROWS + r, 8), pl.ds(h * 128, 128)) for z in range(Z)]
                    e = [eq[to] for to in at]

                    def source(n, z):
                        s = eta[n] * e[z]
                        if r == first:
                            row = edge[h, pl.ds(z * 64 + d * 32 + modes[n], 1), :]
                            s += jnp.where(sub, beta[n] * jnp.broadcast_to(row, (8, 128)), 0.0)
                        return s

                    t = [None] * STEP
                    if d == 0:
                        rough = cz_ref[pl.ds(r, 8), pl.ds(h * 128, 128)] > 0.1
                        here = [pl.ds(pl.multiple_of(m * ROWS, ROWS) + r, 8) for m in modes]
                        kp = [ksel[h, to, :] for to in here]
                        far = [e[Z - 1]] * STEP
                        for z in reversed(range(Z - 1)):
                            far = [a * b + e[z] for a, b in zip(kp, far)]
                        for n, m in enumerate(modes):
                            far[n] = nsel[h, here[n], :] * far[n] + cell[h, pl.ds(r * MODES + m, 8, stride=MODES), :]
                            t[n] = jnp.where(rough, far[n], 0.9 * res[(1, m) + at[0]])
                    for z in range(Z) if d == 0 else range(Z - 1, -1, -1):
                        for n, m in enumerate(modes):
                            t[n] = source(n, z) if t[n] is None else kappa[n] * t[n] + source(n, z)
                            res[(d, m) + at[z]] = l0_ref[(d, m) + at[z]] + t[n]
            leave(g, d).start()
            return carry

        lax.fori_loop(0, MODES // STEP, some, 0)

    def all_modes(d):
        for pos_x in (True, False):
            for here, edge in ((True, chip), (False, next_chip)):
                pl.when((up_x == pos_x) & (on_chip == here))(lambda p=pos_x, e=edge: run(d, p, e))

    all_modes(1)
    hot = hot_ref[...]
    def tiles_of(half, n):
        return [back[pl.ds(((8 * half + t) * BACK + n) * 8, 8), :] for t in range(8)]

    picked = [jnp.concatenate(tiles_of(half, h), axis=1) for half in range(2) for h in range(2)]
    heard = jnp.concatenate(tiles_of(0, 6), axis=1) + jnp.concatenate(tiles_of(1, 6), axis=1)
    heard_high = heard.astype(jnp.bfloat16).astype(F32)
    value = jnp.concatenate(picked + [heard_high, heard - heard_high], axis=0).astype(jnp.bfloat16)
    mask = rm_ref[...].astype(jnp.bfloat16)
    dims = (((1,), (1,)), ((), ()))
    for part in range(4):
        lhs = jnp.concatenate([mask[r : r + 1, :] * value for r in range(4 * part, 4 * part + 4)], axis=0)
        got = lax.dot_general(lhs, hot, dims, preferred_element_type=F32)
        for n, r in enumerate(range(4 * part, 4 * part + 4)):
            for h in range(2):
                cell[h, pl.ds(r * MODES, MODES), :] = got[48 * n : 48 * n + 32, h * 128 : h * 128 + 128]
                both = got[48 * n + 32 : 48 * n + 40, h * 128 : h * 128 + 128] + got[48 * n + 40 : 48 * n + 48, h * 128 : h * 128 + 128]
                grid_en[h, pl.ds(r * 8, 8), :] = both + back[pl.ds((r * BACK + 4 + h) * 8, 8), :]
    for z in range(Z):
        for h in range(2):
            for b in range(2):
                en_ref[pl.ds(z * ROWS + 8 * b, 8), pl.ds(h * 128, 128)] = grid_en[h, pl.ds(8 * b * 8 + z, 8, stride=8), :]
    energy_copy = pltpu.make_async_copy(en_ref, en_hbm, en_sem)
    energy_copy.start()
    all_modes(0)
    energy_copy.wait()
    for g in range(MODES // STEP):
        for d in range(2):
            leave(g, d).wait()


def per_device(
    intensity, dir_cos, velocity, rate, spectrum, weight, heat, rough_cells, rough_count, rough_map
):
    smem = pl.BlockSpec(memory_space=pltpu.SMEM)
    vmem = pl.BlockSpec(memory_space=pltpu.VMEM)

    def hbm(x):
        return pltpu.with_memory_space_constraint(x, pltpu.HBM)

    anywhere = pl.BlockSpec(memory_space=pltpu.HBM)
    field = (2, MODES, PLANE, COLS)
    ones = [t.reshape(1, -1) for t in (velocity, rate, spectrum, weight, rough_cells)]
    tiles = hbm(intensity.reshape(512, 2, 8, COLS))
    x, edge, tab, flags = pl.pallas_call(
        edge_kernel,
        in_specs=[anywhere] * 6,
        out_specs=[vmem] * 3 + [smem],
        out_shape=[
            pltpu.VMEM(s, F32)
            for s in ((2, 512, 8, 128), (2, EDGE + 40, 128), (6, MODES, 128))
        ]
        + [pltpu.SMEM((5,), F32)],
        scratch_shapes=[
            pltpu.VMEM((3, DIRS), F32),
            pltpu.VMEM((1, MODES), F32),
            pltpu.VMEM((1, MODES), F32),
            pltpu.VMEM((1, MODES), F32),
            pltpu.VMEM((1, DIRS), F32),
            pltpu.VMEM((2, 64, 128), F32),
            pltpu.SemaphoreType.DMA((5,)),
            pltpu.SemaphoreType.DMA((2, 8)),
        ],
        compiler_params=pltpu.CompilerParams(vmem_limit_bytes=8 << 20),
        cost_estimate=pl.CostEstimate(flops=4 << 20, bytes_accessed=8 << 20, transcendentals=0),
        name="edges",
    )(tiles, hbm(dir_cos), *[hbm(t) for t in ones[:4]])
    count = lax.axis_size("space")
    on_chip = [(i, i ^ 1) for i in range(count)]
    across = [(i, i + 1 if i % 2 else i - 1) for i in range(1, count - 1)]
    edge_chip, edge_next = [lax.ppermute(edge, "space", p) for p in (on_chip, across)]

    base, energy, e0, d0 = pl.pallas_call(
        sweep_kernel,
        in_specs=[smem, vmem, anywhere, vmem, vmem],
        out_specs=[vmem] * 4,
        out_shape=[pltpu.VMEM(s, F32) for s in (field, (2, PLANE, 128), (2, PLANE, 128), (2, MODES * ROWS, 128))],
        scratch_shapes=[
            pltpu.VMEM((2, 512, 8, 128), F32),
            pltpu.VMEM((2, PLANE, 128), F32),
            pltpu.VMEM((2, PLANE, 128), F32),
            pltpu.VMEM((2, PLANE, 128), F32),
            pltpu.VMEM((2, PLANE, 128), F32),
            pltpu.SemaphoreType.DMA((2, 8)),
        ],
        compiler_params=pltpu.CompilerParams(vmem_limit_bytes=12 << 20),
        cost_estimate=pl.CostEstimate(flops=30 << 20, bytes_accessed=16 << 20, transcendentals=0),
        name="sweep",
    )(flags, tab, tiles, x, heat)

    tables = [
        ((COLS, SLOTS), jnp.bfloat16), ((ROWS, SLOTS), F32), ((3, MODES, 128), F32), ((GROUP, COLS), F32),
        ((Z, 128), F32), ((GROUP, 128), F32), ((ROWS, COLS), F32), ((2, MODES * ROWS, 128), F32),
        ((2, MODES * ROWS, 128), F32), ((MODES, SLOTS), F32), ((2, PLANE, 128), F32),
    ]
    hot, rm, par, jm, k0, mt, cz, ksel, nsel, at_slots, e0 = pl.pallas_call(
        slot_kernel,
        in_specs=[smem] * 2 + [vmem] * 10,
        out_specs=[vmem] * len(tables),
        out_shape=[pltpu.VMEM(*t) for t in tables],
        scratch_shapes=[pltpu.VMEM((MODES * ROWS, COLS), jnp.bfloat16)],
        compiler_params=pltpu.CompilerParams(vmem_limit_bytes=12 << 20),
        cost_estimate=pl.CostEstimate(flops=30 << 20, bytes_accessed=8 << 20, transcendentals=0),
        name="slots",
    )(rough_count, flags, dir_cos, *ones, rough_map.T, tab, d0, e0)

    pack = pl.pallas_call(
        pack_kernel,
        in_specs=[smem] + [vmem] * 9,
        out_specs=vmem,
        out_shape=pltpu.VMEM((GROUP, 2, SEND, 128), F32),
        compiler_params=pltpu.CompilerParams(vmem_limit_bytes=8 << 20),
        name="pack",
    )(flags, tab, energy, e0, at_slots, hot, rm, cz, edge_chip, edge_next)
    got = lax.all_to_all(pack, "mode", 0, 0, tiled=True)

    reply = pl.pallas_call(
        middle_kernel,
        in_specs=[vmem] * 5,
        out_specs=vmem,
        out_shape=pltpu.VMEM((GROUP, BACK, 8, 128), F32),
        scratch_shapes=[pltpu.VMEM((GROUP, MODES, COLS), F32)],
        compiler_params=pltpu.CompilerParams(vmem_limit_bytes=8 << 20),
        name="middle",
    )(got, par, jm, k0, mt)
    back = lax.all_to_all(reply, "mode", 0, 0, tiled=True).reshape(GROUP * BACK * 8, 128)

    fresh, energy_new = pl.pallas_call(
        finish_kernel,
        in_specs=[smem] + [vmem] * 10,
        out_specs=[anywhere, anywhere],
        out_shape=[pltpu.HBM(field, F32), pltpu.HBM((PLANE, COLS), F32)],
        scratch_shapes=[
            pltpu.VMEM((PLANE, COLS), F32),
            pltpu.VMEM(field, F32),
            pltpu.VMEM((2, MODES * ROWS, 128), F32),
            pltpu.VMEM((2, PLANE, 128), F32),
            pltpu.VMEM((PLANE, COLS), F32),
            pltpu.SemaphoreType.DMA((2, MODES // STEP)),
            pltpu.SemaphoreType.DMA,
        ],
        compiler_params=pltpu.CompilerParams(vmem_limit_bytes=24 << 20),
        name="finish",
    )(flags, tab, base, back, hot, rm, cz, ksel, nsel, edge_chip, edge_next)
    return fresh.reshape(intensity.shape), energy_new.reshape(Z, ROWS, COLS)


def solution(mesh):
    in_specs = (
        P("mode", None, "space", None),
        P(),
        P(),
        P(),
        P(),
        P(),
        P("space", None),
        P("space"),
        P("space"),
        P("space", None),
    )
    out_specs = (P("mode", None, "space", None), P(None, "space", None))
    return jax.shard_map(
        per_device, mesh=mesh, in_specs=in_specs, out_specs=out_specs, check_vma=False
    )
```
